32 devices in a mesh: dp: 2 (over y), expert: 16 (over z, x, core).
Axes of the slice: x: 2, y: 2, z: 4, core: 2. Of those that a mesh axis runs over, the one named last changes fastest.
Arguments:
- tokens: bfloat16 [16, 768, 1536], P('expert', 'dp'), may hold values from -6 to 6
- cotangent: bfloat16 [16, 768, 1536], P('expert', 'dp'), may hold values from -6 to 6
- segment_ids: int32 [16, 768], P('expert', 'dp'), may hold values from 0 to 192, as said below
- padding: int32 [16, 768], P('expert', 'dp'), may hold values from 0 to 1, as said below
- routes: int32 [16, 768, 4], P('expert', 'dp'), may hold values from 0 to 15, all different within a row
- placement_order: int32 [16, 768, 4], P('expert', 'dp'), may hold values from 0 to 1535, as said below
- norm_attn: bfloat16 [1536], P('dp'), may hold values from 0.5 to 1.5
- w_query: bfloat16 [1536, 1536], P('dp'), may hold values from -0.15625 to 0.15625
- w_key: bfloat16 [1536, 256], P('dp'), may hold values from -0.15625 to 0.15625
- w_value: bfloat16 [1536, 256], P('dp'), may hold values from -0.15625 to 0.15625
- w_out: bfloat16 [1536, 1536], P('dp'), may hold values from -0.875 to 0.875
- norm_ffn: bfloat16 [1536], P('dp'), may hold values from 0.5 to 1.5
- w_router: bfloat16 [1536, 16], P('dp'), may hold values from -0.078125 to 0.078125
- w_gate: bfloat16 [16, 1536, 768], P('expert', 'dp'), may hold values from -0.15625 to 0.15625
- w_up: bfloat16 [16, 1536, 768], P('expert', 'dp'), may hold values from -0.15625 to 0.15625
- w_down: bfloat16 [16, 768, 1536], P('expert', None, 'dp'), may hold values from -0.4375 to 0.4375
Outputs:
- mixed: bfloat16 [16, 768, 1536], P('expert', 'dp')
- grad_tokens: float32 [16, 768, 1536], P('expert', 'dp')
- grad_norm_attn: float32 [1536], P('dp')
- grad_query: float32 [1536, 1536], P('dp')
- grad_key: float32 [1536, 256], P('dp')
- grad_value: float32 [1536, 256], P('dp')
- grad_out: float32 [1536, 1536], P('dp')
- grad_norm_ffn: float32 [1536], P('dp')
- grad_router: float32 [1536, 16], P('dp')
- grad_gate: float32 [16, 1536, 768], P('expert', 'dp')
- grad_up: float32 [16, 1536, 768], P('expert', 'dp')
- grad_down: float32 [16, 768, 1536], P('expert', None, 'dp')
The draws below stay inside these ranges and needn't reach their ends.
Inputs may be any that keep to these rules, and one draw needn't show every extreme that they name: `segment_ids`: along each sequence the ids never fall; padded tokens carry the id 384 // 2 and real tokens smaller ones. `padding`: along each sequence, ones come before zeros. `routes`: each token names 4 different experts. `placement_order`: over the tokens of one device (aligned blocks of 384 tokens of a sequence), the 1536 entries are a permutation.
All inputs are finite; a program needn't handle non-finite values.
Results may differ from the reference program's by a relative error of at most 0.025.
Values may be sent and summed in bfloat16 or wider, within the bound.
No kernel may reach another device: no remote copies, remote signals or barrier semaphores. Data moves between devices by JAX's collectives and lax.ppermute only.
A program may use at most 192 MiB of HBM per device.

```python
import math
import jax
import jax.numpy as jnp
from jax import lax

D = 1536
HEADS = 12
KV_HEADS = 2
HEAD_DIM = 128
EH = 768
TOP = 4
TOK_DEV = 384
EXPERTS = 16
SEQ_LEN = 768
SEQS = 16
CAP = 108


def documents(key):
    start_key, end_key, flag_key = jax.random.split(key, 3)
    half_block = TOK_DEV // 2
    first_place = jax.random.randint(start_key, (SEQS, 1), 1, half_block)
    tail_length = jax.random.randint(end_key, (SEQS, 1), 1, half_block)
    places = jnp.arange(SEQ_LEN, dtype=jnp.int32)[None, :]
    cuts = jax.random.randint(flag_key, (SEQS, SEQ_LEN), 0, 16) == 0
    edges = (places == first_place) | cuts & (places < first_place) & (places > 0)
    segment = jnp.cumsum(edges.astype(jnp.int32), axis=1).astype(jnp.int32)
    in_tail = places >= SEQ_LEN - tail_length
    segment = jnp.where(in_tail, half_block, segment).astype(jnp.int32)
    valid = jnp.where(in_tail, 0, 1).astype(jnp.int32) + jnp.zeros((SEQS, SEQ_LEN), jnp.int32)
    return (segment, valid)


def draw_segment_ids(key, part):
    segment, valid = documents(key)
    return segment


def draw_padding(key, part):
    segment, valid = documents(key)
    return valid


def draw_placement_order(key, part):
    key = jax.random.fold_in(key, 7)
    block_count = SEQS * (SEQ_LEN // TOK_DEV)
    block_keys = jax.random.split(key, block_count)
    orders = jax.vmap(lambda block_key: jax.random.permutation(block_key, TOK_DEV * TOP))(block_keys)
    return orders.reshape(SEQS, SEQ_LEN, TOP).astype(jnp.int32)


def shard_levels(rng, dims, shards, smallest, largest):
    def one(dim, blocks):
        heights = jax.random.uniform(jax.random.fold_in(jax.random.fold_in(rng, 6), dim), (blocks,), jnp.float32, smallest / len(shards), largest / len(shards))
        return jnp.repeat(jnp.exp(heights), dims[dim] // blocks).reshape((-1,) + (1,) * (len(dims) - dim - 1))

    level = one(*shards[0])
    for cut in shards[1:]:
        level = level * one(*cut)
    return level


def different_ones(stream_key, rows, number_of, top, lift):
    order = jax.random.permutation(jax.random.fold_in(stream_key, 1), number_of)
    pull = order
    for power in range(3):
        pull = pull * pull // number_of
    pull = pull * lift // number_of
    lots = jax.random.randint(jax.random.fold_in(stream_key, 2), (rows, number_of), 0, 4096) + pull
    sure = jax.random.permutation(jax.random.fold_in(stream_key, 3), rows)[jnp.arange(number_of) % rows]
    lots = jnp.where(jnp.arange(rows)[:, None] == sure[None, :], 1 << 14, lots)
    score = lots * number_of + jnp.arange(number_of)
    return lax.top_k(score.astype(jnp.int32), top)[1].astype(jnp.int32)


def normal_values(rng, extent, deviation, reach, pieces=(), held_as=jnp.bfloat16):
    values = jax.random.normal(rng, extent, jnp.float32) * deviation
    if len(pieces) > 0:
        values = shard_levels(rng, extent, pieces, -0.22, 0.18) * values
    return jnp.clip(values, min=-reach, max=reach).astype(held_as)


def setup_inputs(seed: int = 0) -> dict:
    arg_keys = jax.random.split(jax.random.key(seed), 17)
    tokens = normal_values(arg_keys[0], (SEQS, SEQ_LEN, D), 1.0, 6.0, ((0, 16), (1, 2)))
    cotangent = normal_values(arg_keys[1], (SEQS, SEQ_LEN, D), 1.0, 6.0, ((0, 16), (1, 2)))
    segment_ids = draw_segment_ids(jax.random.fold_in(arg_keys[16], 71), 0)
    padding = draw_padding(jax.random.fold_in(arg_keys[16], 71), 0)
    routes = different_ones(arg_keys[4], SEQS * SEQ_LEN, EXPERTS, TOP, 2048).reshape((SEQS, SEQ_LEN, TOP))
    placement_order = draw_placement_order(jax.random.fold_in(arg_keys[16], 71), 0)
    norm_attn = jnp.clip(1.0 + 0.1 * jax.random.normal(arg_keys[6], (D,), jnp.float32), 0.5, 1.5).astype(jnp.bfloat16)
    w_query = normal_values(arg_keys[7], (D, HEADS * HEAD_DIM), D ** -0.5, 0.15625, ((0, 2),))
    w_key = normal_values(arg_keys[8], (D, KV_HEADS * HEAD_DIM), D ** -0.5, 0.15625, ((0, 2),))
    w_value = normal_values(arg_keys[9], (D, KV_HEADS * HEAD_DIM), D ** -0.5, 0.15625, ((0, 2),))
    w_out = normal_values(arg_keys[10], (HEADS * HEAD_DIM, D), (HEADS * HEAD_DIM // 32) ** -0.5, 0.875, ((0, 2),))
    norm_ffn = jnp.clip(1.0 + 0.1 * jax.random.normal(arg_keys[11], (D,), jnp.float32), 0.5, 1.5).astype(jnp.bfloat16)
    w_router = normal_values(arg_keys[12], (D, EXPERTS), (4 * D) ** -0.5, 0.078125, ((0, 2),))
    w_gate = normal_values(arg_keys[13], (EXPERTS, D, EH), D ** -0.5, 0.15625, ((0, 16), (1, 2)))
    w_up = normal_values(arg_keys[14], (EXPERTS, D, EH), D ** -0.5, 0.15625, ((0, 16), (1, 2)))
    w_down = normal_values(arg_keys[15], (EXPERTS, EH, D), (EH // 4) ** -0.5, 0.4375, ((0, 16), (2, 2)))
    return {"tokens": tokens, "cotangent": cotangent, "segment_ids": segment_ids, "padding": padding, "routes": routes, "placement_order": placement_order, "norm_attn": norm_attn, "w_query": w_query, "w_key": w_key, "w_value": w_value, "w_out": w_out, "norm_ffn": norm_ffn, "w_router": w_router, "w_gate": w_gate, "w_up": w_up, "w_down": w_down}


FULL_PRECISION = lax.Precision.HIGHEST
EPSILON = 1e-06
ROPE_BASE = 1000000.0
MASKED = -1e+30

@jax.custom_vjp
def reduced_input(v):
    return lax.optimization_barrier(v.astype(jnp.bfloat16)).astype(jnp.float32)

@jax.custom_vjp
def reduced_gradient(v):
    return v

def low_keep(v):
    return (reduced_input(v), None)

def low_pass(kept, grad):
    return (grad,)

def back_keep(v):
    return (v, None)

def back_low(kept, grad):
    return (reduced_input(grad),)
reduced_input.defvjp(low_keep, low_pass)
reduced_gradient.defvjp(back_keep, back_low)

def rope_tables(position, half_width):
    frequency = ROPE_BASE ** (-jnp.arange(half_width, dtype=jnp.float32) / half_width)
    angle = position.astype(jnp.float32)[:, None] * frequency[None, :]
    return (jnp.cos(angle)[:, None, :], jnp.sin(angle)[:, None, :])

def rotate(vectors, cosine, sine):
    half_width = vectors.shape[-1] // 2
    first_half = vectors[..., :half_width]
    second_half = vectors[..., half_width:]
    return jnp.concatenate([first_half * cosine - second_half * sine, second_half * cosine + first_half * sine], axis=-1)

def normalize(values, gain):
    return values * lax.rsqrt(lax.optimization_barrier(jnp.mean(values * values, axis=-1, keepdims=True)) + EPSILON) * gain

def sequence_attention(queries, key_rows, value_tokens, segment, valid):
    length = queries.shape[0]
    row_block = math.gcd(length, 512)
    scale = 1.0 / math.sqrt(queries.shape[-1])
    places = jnp.arange(length, dtype=jnp.int32)
    key_info = jnp.where(valid == 1, segment, -1)

    def one_block(block_index):
        block_start = (block_index * row_block).astype(jnp.int32)
        query_rows = lax.dynamic_slice_in_dim(queries, block_start, row_block, 0)
        row_places = block_start + jnp.arange(row_block, dtype=jnp.int32)
        row_segment = lax.dynamic_slice_in_dim(segment, block_start, row_block, 0)
        scores = reduced_gradient(jnp.einsum('tkgd,skd->kgts', query_rows, key_rows, precision=FULL_PRECISION) * scale)
        allowed = (places[None, :] <= row_places[:, None]) & (key_info[None, :] == row_segment[:, None]) | (places[None, :] == row_places[:, None])
        scores = jnp.where(allowed, scores, MASKED)
        probs = reduced_input(jax.nn.softmax(scores, axis=-1))
        return jnp.einsum('kgts,skd->tkgd', probs, value_tokens, precision=FULL_PRECISION)
    blocks = lax.map(jax.checkpoint(one_block), jnp.arange(length // row_block, dtype=jnp.int32))
    return blocks.reshape((length,) + blocks.shape[2:])

def slot_tables(route_ids, order_ids):
    pair_count = route_ids.shape[0] * route_ids.shape[1]
    flat_route = route_ids.reshape(pair_count)
    flat_order = order_ids.reshape(pair_count)
    by_order = jnp.zeros((pair_count,), jnp.int32).at[flat_order].set(flat_route)
    onehot = (by_order[:, None] == jnp.arange(EXPERTS, dtype=jnp.int32)[None, :]).astype(jnp.int32)
    before = jnp.cumsum(onehot, axis=0) - onehot
    slot_rank = lax.optimization_barrier(jnp.sum(before * onehot, axis=1))[flat_order]
    keep_mask = slot_rank < CAP
    targets = jnp.where(keep_mask, flat_route * CAP + slot_rank, EXPERTS * CAP).astype(jnp.int32)
    tables = jnp.full((EXPERTS * CAP + 1,), pair_count, jnp.int32).at[targets].set(jnp.arange(pair_count, dtype=jnp.int32))
    return (keep_mask, targets, tables[:EXPERTS * CAP])

def expert_apply(operands):
    row_data, gate_matrix, up_matrix, down_matrix = operands
    gate_pre = reduced_gradient(jnp.dot(row_data, gate_matrix, precision=FULL_PRECISION))
    up_pre = reduced_gradient(jnp.dot(row_data, up_matrix, precision=FULL_PRECISION))
    active = reduced_input(jax.nn.silu(gate_pre) * up_pre)
    return reduced_gradient(reduced_input(jnp.dot(active, down_matrix, precision=FULL_PRECISION)))

def reference(tokens, cotangent, segment_ids, padding, routes, placement_order, norm_attn, w_query, w_key, w_value, w_out, norm_ffn, w_router, w_gate, w_up, w_down):
    shard_count = SEQ_LEN // TOK_DEV
    pair_count = TOK_DEV * TOP
    block_routes = routes.reshape(SEQS * shard_count, TOK_DEV, TOP)
    block_order = placement_order.reshape(SEQS * shard_count, TOK_DEV, TOP)
    keep_mask, targets, tables = jax.vmap(slot_tables)(block_routes, block_order)
    keep_float = keep_mask.reshape(SEQS, SEQ_LEN, TOP).astype(jnp.float32)
    targets = targets.reshape(SEQS, shard_count, pair_count)
    token_tables = (tables // TOP).astype(jnp.int32).reshape(SEQS, shard_count, EXPERTS * CAP)
    cosine, sine = rope_tables(jnp.arange(SEQ_LEN, dtype=jnp.int32), HEAD_DIM // 2)
    head_group = HEADS // KV_HEADS
    pick_rows = jax.vmap(jax.vmap(lambda table_rows, picks: table_rows[picks]))

    def forward(input_tokens, gain_attn, query_weight, key_weight, value_weight, output_weight, gain_ffn, router_weight, gate_stack, up_stack, down_stack):
        first_normalized = reduced_input(normalize(input_tokens, gain_attn))
        query_before_rotation = reduced_gradient(jnp.einsum('qka,at->qkt', first_normalized, query_weight, precision=FULL_PRECISION))
        key_before_rotation = reduced_gradient(jnp.einsum('qka,at->qkt', first_normalized, key_weight, precision=FULL_PRECISION))
        value_tokens = reduced_input(reduced_gradient(jnp.einsum('qka,at->qkt', first_normalized, value_weight, precision=FULL_PRECISION)))
        queries = reduced_input(rotate(query_before_rotation.reshape(SEQS, SEQ_LEN, HEADS, HEAD_DIM), cosine, sine))
        key_rows = reduced_input(rotate(key_before_rotation.reshape(SEQS, SEQ_LEN, KV_HEADS, HEAD_DIM), cosine, sine))
        attention_output = lax.map(lambda operands: sequence_attention(operands[0], operands[1], operands[2], operands[3], operands[4]), (queries.reshape(SEQS, SEQ_LEN, KV_HEADS, head_group, HEAD_DIM), key_rows, value_tokens.reshape(SEQS, SEQ_LEN, KV_HEADS, HEAD_DIM), segment_ids, padding))
        attention_output = reduced_gradient(reduced_input(attention_output.reshape(SEQS, SEQ_LEN, HEADS * HEAD_DIM)))
        expert_middle = input_tokens + reduced_gradient(jnp.einsum('wpz,zn->wpn', attention_output, output_weight, precision=FULL_PRECISION))
        second_normalized = reduced_input(normalize(expert_middle, gain_ffn))
        router_scores = reduced_gradient(jnp.einsum('qka,at->qkt', second_normalized, router_weight, precision=FULL_PRECISION))
        gate_probs = jax.nn.softmax(jnp.take_along_axis(router_scores, routes, axis=2), axis=-1)
        blocks_hidden = second_normalized.reshape(SEQS, shard_count, TOK_DEV, D)
        padded_hidden = jnp.concatenate([blocks_hidden, jnp.zeros((SEQS, shard_count, 1, D), blocks_hidden.dtype)], axis=2)
        sent_rows = reduced_gradient(pick_rows(padded_hidden, token_tables))
        by_expert = sent_rows.reshape(SEQS, shard_count, EXPERTS, CAP, D).transpose(2, 1, 0, 3, 4).reshape(EXPERTS, shard_count * SEQS * CAP, D)
        results = lax.map(jax.checkpoint(expert_apply), (by_expert, gate_stack, up_stack, down_stack))
        returned = results.reshape(EXPERTS, shard_count, SEQS, CAP, D).transpose(2, 1, 0, 3, 4).reshape(SEQS, shard_count, EXPERTS * CAP, D)
        returned = jnp.concatenate([returned, jnp.zeros((SEQS, shard_count, 1, D), returned.dtype)], axis=2)
        pair_rows = pick_rows(returned, targets).reshape(SEQS, SEQ_LEN, TOP, D)
        mixture = lax.optimization_barrier(jnp.sum((gate_probs * keep_float)[..., None] * pair_rows, axis=2))
        return expert_middle + mixture
    floats = [operand.astype(jnp.float32) for operand in (tokens, norm_attn, w_query, w_key, w_value, w_out, norm_ffn, w_router, w_gate, w_up, w_down)]
    output, pullback = jax.vjp(forward, *floats)
    grads = pullback(cotangent.astype(jnp.float32))
    return (output.astype(jnp.bfloat16), grads[0], grads[1], grads[2], grads[3], grads[4], grads[5], grads[6], grads[7], grads[8], grads[9], grads[10])
```

```python
import functools
import math

import jax
import jax.numpy as jnp
from jax import lax
from jax.experimental import pallas as pl
from jax.experimental.pallas import tpu as pltpu
from jax.sharding import PartitionSpec as P

HEADS = 12
KV_HEADS = 2
HEAD_DIM = 128
TOP = 4
GROUP = HEADS // KV_HEADS
PLANE = 4
LANES = 128

EPSILON = 1e-06
ROPE_BASE = 1000000.0
MASKED = -1e30
MIB = 1024 * 1024

f32 = jnp.float32
bf16 = jnp.bfloat16


def dot(a, b):
    return jnp.dot(a, b, preferred_element_type=f32)


def dot_nt(a, b):
    return lax.dot_general(a, b, (((1,), (1,)), ((), ())), preferred_element_type=f32)


def dot_tn(a, b):
    return lax.dot_general(a, b, (((0,), (0,)), ((), ())), preferred_element_type=f32)


def whole(shape):
    return pl.BlockSpec(shape, lambda *_: (0,) * len(shape))


def call(kernel, grid, in_specs, out_specs, out_shape, scratch=(), prefetch=0, flops=0, moved=0, vmem=48, aliases=None):
    return pl.pallas_call(
        kernel,
        grid_spec=pltpu.PrefetchScalarGridSpec(
            num_scalar_prefetch=prefetch,
            grid=grid,
            in_specs=in_specs,
            out_specs=out_specs,
            scratch_shapes=list(scratch),
        ),
        out_shape=out_shape,
        input_output_aliases=aliases or {},
        cost_estimate=pl.CostEstimate(flops=flops, bytes_accessed=moved, transcendentals=0),
        compiler_params=pltpu.CompilerParams(
            dimension_semantics=("arbitrary",) * len(grid), vmem_limit_bytes=vmem * MIB
        ),
    )


def qkv_kernel(offsets, x_ref, gain_ref, cos_ref, sin_ref, *refs):
    pieces, (out_ref, h_ref) = refs[:-2], refs[-2:]
    step = pl.program_id(0)

    @pl.when(step == 0)
    def _():
        x = x_ref[...].astype(f32)
        r = lax.rsqrt(jnp.mean(x * x, axis=1, keepdims=True) + EPSILON)
        h_ref[...] = (x * r * gain_ref[...]).astype(bf16)

    acc = None
    for n, w_ref in enumerate(pieces):
        rows = w_ref.shape[0]
        start = pl.multiple_of(offsets[n], LANES)
        part = dot(h_ref[:, pl.ds(start, rows)], w_ref[...])
        acc = part if acc is None else acc + part

    rotary = step * out_ref.shape[1] < (HEADS + KV_HEADS) * HEAD_DIM

    @pl.when(rotary)
    def _():
        for n in range(out_ref.shape[1] // HEAD_DIM):
            a = acc[:, n * HEAD_DIM : (n + 1) * HEAD_DIM]
            turned = a * cos_ref[...] + pltpu.roll(a, HEAD_DIM // 2, 1) * sin_ref[...]
            out_ref[:, n * HEAD_DIM : (n + 1) * HEAD_DIM] = turned.astype(bf16)

    @pl.when(jnp.logical_not(rotary))
    def _():
        out_ref[...] = acc.astype(bf16)


def project_qkv(x, gain, cosine, sine, offsets, pieces):
    tokens, width = x.shape
    columns = pieces[0].shape[1]
    tile = 256
    return call(
        qkv_kernel,
        (columns // tile,),
        [whole(x.shape), whole(gain.shape), whole(cosine.shape), whole(sine.shape)]
        + [pl.BlockSpec((p.shape[0], tile), lambda i, *_: (0, i)) for p in pieces],
        [pl.BlockSpec((tokens, tile), lambda i, *_: (0, i)), whole(x.shape)],
        [jax.ShapeDtypeStruct((tokens, columns), bf16), jax.ShapeDtypeStruct(x.shape, bf16)],
        prefetch=1,
        flops=2 * tokens * width * columns,
        moved=2 * width * columns + 4 * tokens * columns,
    )(offsets, x, gain, cosine, sine, *pieces)


def attend_kernel(q_ref, k_ref, v_ref, segment_ref, place_ref, info_ref, key_place_ref, o_ref, p_ref, bias_ref):
    @pl.when(pl.program_id(0) == 0)
    def _():
        place = place_ref[...]
        key_place = key_place_ref[...]
        allowed = (key_place <= place) & (info_ref[...] == segment_ref[...]) | (key_place == place)
        bias_ref[...] = jnp.where(allowed, 0.0, MASKED)

    scores = dot_nt(q_ref[...], k_ref[...]) * (1.0 / math.sqrt(HEAD_DIM)) + bias_ref[...]
    peak = jnp.max(scores, axis=1, keepdims=True)
    exps = jnp.exp(scores - peak)
    probs = (exps * (1.0 / jnp.sum(exps, axis=1, keepdims=True))).astype(bf16)
    p_ref[0] = probs
    o_ref[...] = dot(probs, v_ref[...]).astype(bf16)


def attend(qkv, keys_values, segment, place, info, key_place):
    tokens = qkv.shape[0]
    keys = keys_values.shape[0]
    return call(
        attend_kernel,
        (HEADS,),
        [
            pl.BlockSpec((tokens, HEAD_DIM), lambda h: (0, h)),
            pl.BlockSpec((keys, HEAD_DIM), lambda h: (0, h // GROUP)),
            pl.BlockSpec((keys, HEAD_DIM), lambda h: (0, KV_HEADS + h // GROUP)),
            whole((tokens, 1)),
            whole((tokens, 1)),
            whole((1, keys)),
            whole((1, keys)),
        ],
        [
            pl.BlockSpec((tokens, HEAD_DIM), lambda h: (0, h)),
            pl.BlockSpec((1, tokens, keys), lambda h: (h, 0, 0)),
        ],
        [
            jax.ShapeDtypeStruct((tokens, HEADS * HEAD_DIM), bf16),
            jax.ShapeDtypeStruct((HEADS, tokens, keys), bf16),
        ],
        scratch=[pltpu.VMEM((tokens, keys), f32)],
        flops=4 * HEADS * tokens * keys * HEAD_DIM,
        moved=2 * HEADS * tokens * keys,
    )(qkv, keys_values, keys_values, segment, place, info, key_place)


def attend_back_kernel(p_ref, do_ref, q_ref, k_ref, v_ref, cos_ref, sin_ref, dq_ref, dk_ref, dv_ref):
    scale = 1.0 / math.sqrt(HEAD_DIM)
    member = lax.rem(pl.program_id(0), GROUP)
    probs = p_ref[0]
    wide = probs.astype(f32)
    do = do_ref[...]
    grad_probs = dot_nt(do, v_ref[...])
    delta = jnp.sum(wide * grad_probs, axis=1, keepdims=True)
    grad_scores = (wide * (grad_probs - delta)).astype(bf16)
    dq = dot(grad_scores, k_ref[...]) * scale
    dq_ref[...] = (dq * cos_ref[...] - pltpu.roll(dq, HEAD_DIM // 2, 1) * sin_ref[...]).astype(bf16)
    dk = dot_tn(grad_scores, q_ref[...]) * scale
    dv = dot_tn(probs, do)

    @pl.when(member == 0)
    def _():
        dk_ref[...] = dk
        dv_ref[...] = dv

    @pl.when(member > 0)
    def _():
        dk_ref[...] += dk
        dv_ref[...] += dv


def attend_back(probs, do, qkv, keys_values, cosine, sine):
    tokens = qkv.shape[0]
    keys = keys_values.shape[0]
    kv_width = KV_HEADS * HEAD_DIM
    return call(
        attend_back_kernel,
        (HEADS,),
        [
            pl.BlockSpec((1, tokens, keys), lambda h: (h, 0, 0)),
            pl.BlockSpec((tokens, HEAD_DIM), lambda h: (0, h)),
            pl.BlockSpec((tokens, HEAD_DIM), lambda h: (0, h)),
            pl.BlockSpec((keys, HEAD_DIM), lambda h: (0, h // GROUP)),
            pl.BlockSpec((keys, HEAD_DIM), lambda h: (0, KV_HEADS + h // GROUP)),
            whole(cosine.shape),
            whole(sine.shape),
        ],
        [
            pl.BlockSpec((tokens, HEAD_DIM), lambda h: (0, h)),
            pl.BlockSpec((keys, HEAD_DIM), lambda h: (0, h // GROUP)),
            pl.BlockSpec((keys, HEAD_DIM), lambda h: (0, h // GROUP)),
        ],
        [
            jax.ShapeDtypeStruct((tokens, HEADS * HEAD_DIM), bf16),
            jax.ShapeDtypeStruct((keys, kv_width), f32),
            jax.ShapeDtypeStruct((keys, kv_width), f32),
        ],
        flops=8 * HEADS * tokens * keys * HEAD_DIM,
        moved=2 * HEADS * tokens * keys,
    )(probs, do, qkv, keys_values, keys_values, cosine, sine)


def middle_kernel(experts, offsets, o_ref, x_ref, gain_ref, router_ref, routes_ref, *refs):
    pieces, (middle_ref, payload_ref, gates_ref) = refs[:-3], refs[-3:]
    step = pl.program_id(0)
    tile = x_ref.shape[1]
    acc = x_ref[...].astype(f32)
    for n, w_ref in enumerate(pieces):
        start = pl.multiple_of(offsets[n], LANES)
        acc = acc + dot(o_ref[:, pl.ds(start, w_ref.shape[0])], w_ref[...])
    middle_ref[:, pl.ds(pl.multiple_of(step * tile, tile), tile)] = acc

    @pl.when(step == pl.num_programs(0) - 1)
    def _():
        middle = middle_ref[...]
        width = middle.shape[1]
        r = lax.rsqrt(jnp.mean(middle * middle, axis=1, keepdims=True) + EPSILON)
        h = (middle * r * gain_ref[...]).astype(bf16)
        payload_ref[:, :width] = h
        logits = dot_nt(h, router_ref[...])
        lane = lax.broadcasted_iota(jnp.int32, logits.shape, 1)
        chosen = lane == routes_ref[:, 0:1]
        for k in range(1, TOP):
            chosen = chosen | (lane == routes_ref[:, k : k + 1])
        logits = jnp.where(chosen, logits, MASKED)
        exps = jnp.where(chosen, jnp.exp(logits - jnp.max(logits, axis=1, keepdims=True)), 0.0)
        gates = exps / jnp.sum(exps, axis=1, keepdims=True)
        gates_ref[...] = gates
        high = gates.astype(bf16).astype(f32)
        payload_ref[:, width:] = (high + pltpu.roll(gates - high, experts, 1)).astype(bf16)


def project_out(o, x, gain, router, routes, offsets, pieces, experts):
    tokens, width = x.shape
    tile = 256
    return call(
        functools.partial(middle_kernel, experts),
        (width // tile,),
        [
            whole(o.shape),
            pl.BlockSpec((tokens, tile), lambda i, *_: (0, i)),
            whole(gain.shape),
            whole(router.shape),
            whole(routes.shape),
        ]
        + [pl.BlockSpec((p.shape[0], tile), lambda i, *_: (0, i)) for p in pieces],
        [whole((tokens, width)), whole((tokens, width + LANES)), whole((tokens, LANES))],
        [
            jax.ShapeDtypeStruct((tokens, width), f32),
            jax.ShapeDtypeStruct((tokens, width + LANES), bf16),
            jax.ShapeDtypeStruct((tokens, LANES), f32),
        ],
        prefetch=1,
        flops=2 * tokens * width * o.shape[1],
        moved=2 * width * o.shape[1] + 10 * tokens * width,
    )(offsets, o, x, gain, router, routes, *pieces)


def one_hot(slots_ref, j, rows):
    tokens = slots_ref.shape[1]
    slot = lax.broadcasted_iota(jnp.int32, (rows, tokens), 0)
    return jnp.where(slot == slots_ref[j : j + 1, :], 1.0, 0.0).astype(bf16)


def select_kernel(slots_ref, block_ref, *outs):
    rows = outs[0].shape[0]
    picks = jnp.concatenate([one_hot(slots_ref, j, rows) for j in range(PLANE)], axis=0)
    chosen = dot(picks, block_ref[...]).astype(bf16)
    for j, out in enumerate(outs):
        out[...] = chosen[j * rows : (j + 1) * rows]


def select(slots, block, rows):
    tokens, width = block.shape
    return call(
        select_kernel,
        (1,),
        [whole(slots.shape), whole(block.shape)],
        [whole((rows, width))] * PLANE,
        [jax.ShapeDtypeStruct((rows, width), bf16)] * PLANE,
        flops=2 * PLANE * rows * tokens * width,
        moved=2 * (PLANE * rows + tokens) * width,
    )(slots, block)


def combine_kernel(slots_ref, *refs):
    parts, rest = refs[:PLANE], refs[PLANE:]
    out = rest[-1]
    rows = parts[0].shape[0]
    picks = jnp.concatenate([one_hot(slots_ref, j, rows) for j in range(PLANE)], axis=0)
    total = dot_tn(picks, jnp.concatenate([p[...] for p in parts], axis=0))
    if len(rest) > 1:
        total = total + rest[0][...].astype(f32)
    out[...] = total.astype(out.dtype)


def combine(slots, parts, before, dtype):
    tokens = slots.shape[1]
    rows, width = parts[0].shape
    extra = [] if before is None else [before]
    return call(
        combine_kernel,
        (1,),
        [whole(slots.shape)] + [whole((rows, width))] * PLANE + [whole((tokens, width))] * len(extra),
        whole((tokens, width)),
        jax.ShapeDtypeStruct((tokens, width), dtype),
        flops=2 * PLANE * rows * tokens * width,
        moved=2 * (PLANE * rows + 3 * tokens) * width,
    )(slots, *parts, *extra)


def expert_kernel(experts, at, *refs):
    xs, cs = refs[:PLANE], refs[PLANE : 2 * PLANE]
    wg_ref, wu_ref, wd_ref = refs[2 * PLANE : 2 * PLANE + 3]
    y_acc, d_acc, gate_ref = refs[-3:]
    outs = refs[-3 - 2 * PLANE - 5 : -3]
    drows, ys = outs[:PLANE], outs[PLANE : 2 * PLANE]
    x_ref, dy_ref, a_ref, dg_ref, du_ref = outs[2 * PLANE :]
    step = pl.program_id(0)
    expert = at[0]
    rows = xs[0].shape[0]
    width = x_ref.shape[1]
    lane = lax.broadcasted_iota(jnp.int32, (rows, LANES), 1)

    @pl.when(step == 0)
    def _():
        for j in range(PLANE):
            span = slice(j * rows, (j + 1) * rows)
            x_ref[span, :] = xs[j][:, :width]
            tail = xs[j][:, width:].astype(f32)
            mine = (lane == expert) | (lane == expert + experts)
            gate = jnp.sum(jnp.where(mine, tail, 0.0), axis=1, keepdims=True)
            gate_ref[span, :] = jnp.broadcast_to(gate, (rows, LANES))
            dy_ref[span, :] = (gate * cs[j][...].astype(f32)).astype(bf16)

    x = x_ref[...]
    dy = dy_ref[...]
    wg, wu, wd = wg_ref[...], wu_ref[...], wd_ref[...]
    g = dot(x, wg)
    u = dot(x, wu)
    sigma = 1.0 / (1.0 + jnp.exp(-g))
    swish = g * sigma
    a = (swish * u).astype(bf16)
    da = dot_nt(dy, wd)
    dg = (da * u * sigma * (1.0 + g * (1.0 - sigma))).astype(bf16)
    du = (da * swish).astype(bf16)
    a_ref[...] = a
    dg_ref[...] = dg
    du_ref[...] = du
    y = dot(a, wd)
    d = dot_nt(dg, wg) + dot_nt(du, wu)

    @pl.when(step == 0)
    def _():
        y_acc[...] = y
        d_acc[...] = d

    @pl.when(step > 0)
    def _():
        y_acc[...] += y
        d_acc[...] += d

    @pl.when(step == pl.num_programs(0) - 1)
    def _():
        for j in range(PLANE):
            span = slice(j * rows, (j + 1) * rows)
            yj = y_acc[span, :].astype(bf16).astype(f32)
            ys[j][...] = (gate_ref[span, 0:1] * yj).astype(bf16)
            dgate = jnp.sum(cs[j][...].astype(f32) * yj, axis=1, keepdims=True)
            high = dgate.astype(bf16).astype(f32)
            tail = jnp.where(lane == expert, high, 0.0) + jnp.where(lane == expert + experts, dgate - high, 0.0)
            drows[j][:, :width] = d_acc[span, :].astype(bf16)
            drows[j][:, width:] = tail.astype(bf16)


def run_expert(index, part, parts, experts, xs, cs, wg, wu, wd, kept):
    rows = xs[0].shape[0]
    width, hidden = wg.shape
    tile = 256
    total = PLANE * rows
    at = jnp.stack([index]).astype(jnp.int32)
    kept = [] if kept is None else list(kept)
    big = [width, width, hidden, hidden, hidden]
    first_out = 2 * PLANE
    return call(
        functools.partial(expert_kernel, experts),
        (hidden // tile,),
        [whole(xs[0].shape)] * PLANE
        + [whole(cs[0].shape)] * PLANE
        + [
            pl.BlockSpec((width, tile), lambda i, *_: (0, i)),
            pl.BlockSpec((width, tile), lambda i, *_: (0, i)),
            pl.BlockSpec((tile, width), lambda i, *_: (i, 0)),
        ]
        + [pl.BlockSpec(memory_space=pl.ANY)] * len(kept),
        [whole((rows, width + LANES))] * PLANE
        + [whole((rows, width))] * PLANE
        + [pl.BlockSpec((total, width), lambda i, *_: (part, 0))] * 2
        + [pl.BlockSpec((total, tile), lambda i, *_: (part, i))] * 3,
        [jax.ShapeDtypeStruct((rows, width + LANES), bf16)] * PLANE
        + [jax.ShapeDtypeStruct((rows, width), bf16)] * PLANE
        + [jax.ShapeDtypeStruct((parts * total, n), bf16) for n in big],
        scratch=[pltpu.VMEM((total, width), f32), pltpu.VMEM((total, width), f32), pltpu.VMEM((total, LANES), f32)],
        prefetch=1,
        flops=12 * total * width * hidden,
        moved=6 * width * hidden + 16 * total * width,
        aliases={1 + 2 * PLANE + 3 + n: first_out + n for n in range(len(kept))},
    )(at, *xs, *cs, wg, wu, wd, *kept)


def after(value, *others):
    return lax.optimization_barrier((value,) + others)[0]


def rope_tables(position):
    half_width = HEAD_DIM // 2
    frequency = ROPE_BASE ** (-jnp.arange(half_width, dtype=f32) / half_width)
    angle = position.astype(f32)[:, None] * frequency[None, :]
    cosine, sine = jnp.cos(angle), jnp.sin(angle)
    return jnp.concatenate([cosine, cosine], axis=1), jnp.concatenate([-sine, sine], axis=1)


def on_device(
    copies,
    experts,
    tokens,
    cotangent,
    segment_ids,
    padding,
    routes,
    placement_order,
    norm_attn,
    w_query,
    w_key,
    w_value,
    w_out,
    norm_ffn,
    w_router,
    w_gate,
    w_up,
    w_down,
):
    planes = experts // PLANE
    paired = copies == 2
    d = lax.axis_index("dp")
    e = lax.axis_index("expert")
    z, q = e // PLANE, lax.rem(e, PLANE)
    core = lax.rem(e, 2)

    def swap(value):
        return lax.ppermute(value, "dp", [(0, 1), (1, 0)])

    def across(value, j):
        return lax.ppermute(value, "expert", [(i, i ^ j) for i in range(experts)])

    def ahead(value):
        return lax.ppermute(value, "expert", [(i, (i + PLANE) % experts) for i in range(experts)])

    def join(own, other, index, axis):
        first = jnp.where(index == 0, own, other)
        second = jnp.where(index == 0, other, own)
        return jnp.concatenate([first, second], axis=axis)

    def gather(own, axis):
        if paired:
            return join(own, swap(own), d, axis)
        return lax.all_gather(own, "dp", axis=axis, tiled=True)

    def gather_shared(own):
        half = own.shape[0] // 2
        got = swap(lax.dynamic_slice_in_dim(own, core * half, half, 0))
        twin = across(got, 1)
        start = (1 - d) * own.shape[0]
        offsets = jnp.stack([d * own.shape[0], start + core * half, start + (1 - core) * half])
        return [own, got, twin], offsets.astype(jnp.int32)

    def assemble(pieces):
        if len(pieces) == 1:
            return pieces[0]
        own, got, twin = pieces
        return join(own, join(got, twin, core, 0), d, 0)

    x = tokens[0]
    tok_count, width = x.shape
    position = d * tok_count + jnp.arange(tok_count, dtype=jnp.int32)
    kv_width = KV_HEADS * HEAD_DIM
    q_width = HEADS * HEAD_DIM

    small_own = jnp.concatenate([norm_attn[None], norm_ffn[None], w_router.T], axis=0)
    small = gather(small_own, 1)
    own_info = jnp.where(padding[0] == 1, segment_ids[0], -1)[None]
    qkv_own = jnp.concatenate([w_query, w_key, w_value], axis=1)
    if paired:
        qkv_pieces, offsets = gather_shared(qkv_own)
        out_pieces, _ = gather_shared(after(w_out, qkv_pieces[1]))
        info = jnp.concatenate([own_info, swap(own_info)], axis=1)
        other_position = (1 - d) * tok_count + jnp.arange(tok_count, dtype=jnp.int32)
        key_place = jnp.concatenate([position, other_position])[None]
        expert_own = after((w_gate[0], w_up[0], w_down[0]), out_pieces[1])
    else:
        qkv_pieces = [lax.all_gather(qkv_own, "dp", axis=0, tiled=True)]
        out_pieces = [lax.all_gather(w_out, "dp", axis=0, tiled=True)]
        offsets = jnp.zeros((1,), jnp.int32)
        info = lax.all_gather(own_info, "dp", axis=1, tiled=True)
        key_place = jnp.arange(copies * tok_count, dtype=jnp.int32)[None]
        expert_own = (w_gate[0], w_up[0], w_down[0])
    gate_matrix = gather(expert_own[0], 0)
    up_matrix = gather(expert_own[1], 0)
    down_matrix = gather(expert_own[2], 1)

    capacity = tok_count * TOP * 9 // (8 * experts)
    rows = (capacity + 15) // 16 * 16
    expert_ids = jnp.arange(experts, dtype=jnp.int32)
    far = tok_count * TOP
    hits = routes[0].T[None] == expert_ids[:, None, None]
    order = jnp.min(jnp.where(hits, placement_order[0].T[None], far), axis=1)
    rank = jnp.sum((order[:, None, :] < order[:, :, None]).astype(jnp.int32), axis=2)
    own_slots = jnp.where((order < far) & (rank < capacity), rank, -1)

    ring_slots = [own_slots]
    ring_cot = [cotangent[0]]
    for _ in range(planes - 1):
        ring_slots.append(ahead(ring_slots[-1]))
        ring_cot.append(ahead(ring_cot[-1]))
    near_slots = [
        jnp.concatenate(
            [lax.dynamic_slice_in_dim(s, z * PLANE + (q ^ j), 1, 0) for j in range(PLANE)], axis=0
        )
        for s in ring_slots
    ]

    def hand_out(block, slots):
        parts = select(slots, block, rows)
        return [parts[0]] + [across(parts[j], j) for j in range(1, PLANE)]

    cots = [hand_out(ring_cot[k], near_slots[k]) for k in range(planes)]

    cosine, sine = rope_tables(position)
    gain_one = small[0:1].astype(f32)
    gain_two = small[1:2].astype(f32)
    qkv, hidden_one = project_qkv(x, gain_one, cosine, sine, offsets, qkv_pieces)
    own_kv = qkv[:, q_width:]
    if paired:
        keys_values = jnp.concatenate([own_kv, swap(own_kv)], axis=0)
    else:
        keys_values = lax.all_gather(own_kv, "dp", axis=0, tiled=True)
    attended, probs = attend(qkv, keys_values, segment_ids[0][:, None], position[:, None], info, key_place)

    router_rows = jnp.pad(small[2:], ((0, LANES - experts), (0, 0)))
    middle, payload, gates = project_out(
        attended, x, gain_two, router_rows, routes[0], offsets, out_pieces, experts
    )

    ring_rows = [payload]
    for _ in range(planes - 1):
        ring_rows.append(ahead(ring_rows[-1]))
    kept = None
    drows, ys = [], []
    for k in range(planes):
        xs = hand_out(ring_rows[k], near_slots[k])
        outs = run_expert(e, k, planes, experts, xs, cots[k], gate_matrix, up_matrix, down_matrix, kept)
        kept = outs[2 * PLANE :]
        drows.append(outs[:PLANE])
        ys.append(outs[PLANE : 2 * PLANE])

    def bring_back(parts):
        return [parts[0]] + [across(parts[j], j) for j in range(1, PLANE)]

    def ring_sum(parts):
        carried = None
        for k in list(range(1, planes)) + [0]:
            last = k == 0
            total = combine(near_slots[k], bring_back(parts[k]), carried, f32 if last else bf16)
            carried = total if last else ahead(total)
        return carried

    back = ring_sum(drows)
    ys = after(ys, back)
    mixture = ring_sum(ys)
    mixed = (middle + mixture).astype(bf16)[None]

    row_all, dy_all, a_all, dg_all, du_all = kept
    grad_gate_local = dot_tn(row_all, dg_all)
    grad_up_local = dot_tn(row_all, du_all)
    grad_down_local = dot_tn(a_all, dy_all)

    def own_half(full, axis):
        if paired:
            size = full.shape[axis] // 2
            away = lax.dynamic_slice_in_dim(full, (1 - d) * size, size, axis).astype(bf16)
            return lax.dynamic_slice_in_dim(full, d * size, size, axis) + swap(away).astype(f32)
        return lax.psum_scatter(full.astype(bf16), "dp", scatter_dimension=axis, tiled=True).astype(f32)

    grad_gate = own_half(grad_gate_local, 0)[None]
    grad_up = own_half(grad_up_local, 0)[None]
    grad_down = own_half(grad_down_local, 1)[None]

    upstream = cotangent[0].astype(f32)
    gates = gates[:, :experts]
    dgates = back[:, width : width + experts] + back[:, width + experts : width + 2 * experts]
    dlogits = (gates * (dgates - jnp.sum(gates * dgates, axis=1, keepdims=True))).astype(bf16)
    hidden_two = payload[:, :width]
    grad_router_local = dot_tn(hidden_two, dlogits)
    dh2 = back[:, :width] + dot(dlogits, small[2:])
    scale_two = lax.rsqrt(jnp.mean(middle * middle, axis=1, keepdims=True) + EPSILON)
    normed_two = middle * scale_two
    grad_norm_ffn_local = jnp.sum(dh2 * normed_two, axis=0)
    e2 = dh2 * gain_two
    dmiddle = upstream + scale_two * (e2 - normed_two * jnp.mean(e2 * normed_two, axis=1, keepdims=True))
    dmb = dmiddle.astype(bf16)
    full_out = assemble(out_pieces)
    grad_out_local = dot_tn(attended, dmb)
    do = dot_nt(dmb, full_out).astype(bf16)

    dqp, dk, dv = attend_back(probs, do, qkv, keys_values, cosine, sine)
    dkv = jnp.concatenate([dk, dv], axis=1)
    if paired:
        dkv = dkv[:tok_count] + swap(dkv[tok_count:].astype(bf16)).astype(f32)
    else:
        dkv = lax.psum_scatter(dkv.astype(bf16), "dp", scatter_dimension=0, tiled=True).astype(f32)

    def unrotate(value):
        turned = jnp.concatenate([value[:, HEAD_DIM // 2 :], value[:, : HEAD_DIM // 2]], axis=1)
        return value * cosine - turned * sine

    dkp = [unrotate(dkv[:, n * HEAD_DIM : (n + 1) * HEAD_DIM]) for n in range(KV_HEADS)]
    dqkv = jnp.concatenate([dqp] + [v.astype(bf16) for v in dkp] + [dkv[:, kv_width:].astype(bf16)], axis=1)
    grad_qkv_local = dot_tn(hidden_one, dqkv)
    full_qkv = assemble(qkv_pieces)
    dh1 = dot_nt(dqkv, full_qkv)
    input_tokens = x.astype(f32)
    scale_one = lax.rsqrt(jnp.mean(input_tokens * input_tokens, axis=1, keepdims=True) + EPSILON)
    normed_one = input_tokens * scale_one
    grad_norm_attn_local = jnp.sum(dh1 * normed_one, axis=0)
    e1 = dh1 * gain_one
    grad_inputs = dmiddle + scale_one * (e1 - normed_one * jnp.mean(e1 * normed_one, axis=1, keepdims=True))

    def reduce_rows(full):
        full = full.astype(bf16)
        columns = full.shape[1]
        if not paired:
            part = lax.psum_scatter(full, "dp", scatter_dimension=0, tiled=True)
            return lax.psum(part, "expert").astype(f32)

        def add(a, b):
            return (a.astype(f32) + b.astype(f32)).astype(bf16)

        def pick(value, index, axis=0):
            return lax.dynamic_index_in_dim(value, index, axis, keepdims=False)

        other_chip = lax.rem(q // 2, 2)
        cut = full.reshape(2, 2, -1, columns)
        part = add(pick(cut, core, 1), across(pick(cut, 1 - core, 1), 1))
        part = add(pick(part, d), swap(pick(part, 1 - d)))
        part = part.reshape(2, -1, columns)
        part = add(pick(part, other_chip), across(pick(part, 1 - other_chip), 2))
        part = part.reshape(planes, -1, columns)
        carried = None
        for k in list(range(1, planes)) + [0]:
            own = pick(part, lax.rem(z + planes - k, planes))
            carried = own if carried is None else add(own, carried)
            if k > 0:
                carried = ahead(carried)
        whole_part = jnp.zeros_like(part)
        for k in range(planes):
            whole_part = lax.dynamic_update_index_in_dim(
                whole_part, carried, lax.rem(z + planes - k, planes), 0
            )
            if k < planes - 1:
                carried = ahead(carried)
        part = whole_part.reshape(-1, columns)
        part = join(part, across(part, 2), other_chip, 0)
        return join(part, across(part, 1), core, 0).astype(f32)

    def pad_columns(value):
        return jnp.pad(value, ((0, 0), (0, LANES - value.shape[1])))

    first = jnp.concatenate(
        [grad_out_local, pad_columns(jnp.concatenate([grad_norm_ffn_local[:, None], grad_router_local], axis=1))],
        axis=1,
    )
    second = jnp.concatenate([grad_qkv_local, pad_columns(grad_norm_attn_local[:, None])], axis=1)
    first = reduce_rows(first)
    second = reduce_rows(second)
    return (
        mixed,
        grad_inputs[None],
        second[:, q_width + 2 * kv_width],
        second[:, :q_width],
        second[:, q_width : q_width + kv_width],
        second[:, q_width + kv_width : q_width + 2 * kv_width],
        first[:, :width],
        first[:, width],
        first[:, width + 1 : width + 1 + experts],
        grad_gate,
        grad_up,
        grad_down,
    )


def solution(mesh):
    rows = P("expert", "dp", None)
    return jax.shard_map(
        functools.partial(on_device, mesh.shape["dp"], mesh.shape["expert"]),
        mesh=mesh,
        in_specs=(
            rows,
            rows,
            P("expert", "dp"),
            P("expert", "dp"),
            rows,
            rows,
            P("dp"),
            P("dp", None),
            P("dp", None),
            P("dp", None),
            P("dp", None),
            P("dp"),
            P("dp", None),
            rows,
            rows,
            P("expert", None, "dp"),
        ),
        out_specs=(
            rows,
            rows,
            P("dp"),
            P("dp", None),
            P("dp", None),
            P("dp", None),
            P("dp", None),
            P("dp"),
            P("dp", None),
            rows,
            rows,
            P("expert", None, "dp"),
        ),
        check_vma=False,
    )
```

```python
import functools
import math

import jax
import jax.numpy as jnp
from jax import lax
from jax.experimental import pallas as pl
from jax.experimental.pallas import tpu as pltpu
from jax.sharding import PartitionSpec as P

HEADS = 12
KV_HEADS = 2
HEAD_DIM = 128
TOP = 4
GROUP = HEADS // KV_HEADS
PLANE = 4
LANES = 128
PIECES = 3

EPSILON = 1e-06
ROPE_BASE = 1000000.0
MASKED = -1e30
MIB = 1024 * 1024

f32 = jnp.float32
bf16 = jnp.bfloat16


def dot(a, b):
    return jnp.dot(a, b, preferred_element_type=f32)


def dot_nt(a, b):
    return lax.dot_general(a, b, (((1,), (1,)), ((), ())), preferred_element_type=f32)


def dot_tn(a, b):
    return lax.dot_general(a, b, (((0,), (0,)), ((), ())), preferred_element_type=f32)


def whole(shape):
    return pl.BlockSpec(shape, lambda *_: (0,) * len(shape))


def call(kernel, grid, in_specs, out_specs, out_shape, scratch=(), prefetch=0, flops=0, moved=0, vmem=48, aliases=None):
    return pl.pallas_call(
        kernel,
        grid_spec=pltpu.PrefetchScalarGridSpec(
            num_scalar_prefetch=prefetch,
            grid=grid,
            in_specs=in_specs,
            out_specs=out_specs,
            scratch_shapes=list(scratch),
        ),
        out_shape=out_shape,
        input_output_aliases=aliases or {},
        cost_estimate=pl.CostEstimate(flops=flops // 64, bytes_accessed=moved // 64, transcendentals=0),
        compiler_params=pltpu.CompilerParams(
            dimension_semantics=("arbitrary",) * len(grid), vmem_limit_bytes=vmem * MIB
        ),
    )


def qkv_kernel(offsets, x_ref, gain_ref, cos_ref, sin_ref, *refs):
    pieces, (out_ref, h_ref) = refs[:-2], refs[-2:]
    step = pl.program_id(0)

    @pl.when(step == 0)
    def _():
        x = x_ref[...].astype(f32)
        r = lax.rsqrt(jnp.mean(x * x, axis=1, keepdims=True) + EPSILON)
        h_ref[...] = (x * r * gain_ref[...]).astype(bf16)

    acc = None
    for n, w_ref in enumerate(pieces):
        rows = w_ref.shape[0]
        start = pl.multiple_of(offsets[n], LANES)
        part = dot(h_ref[:, pl.ds(start, rows)], w_ref[...])
        acc = part if acc is None else acc + part

    rotary = step * out_ref.shape[1] < (HEADS + KV_HEADS) * HEAD_DIM

    @pl.when(rotary)
    def _():
        for n in range(out_ref.shape[1] // HEAD_DIM):
            a = acc[:, n * HEAD_DIM : (n + 1) * HEAD_DIM]
            turned = a * cos_ref[...] + pltpu.roll(a, HEAD_DIM // 2, 1) * sin_ref[...]
            out_ref[:, n * HEAD_DIM : (n + 1) * HEAD_DIM] = turned.astype(bf16)

    @pl.when(jnp.logical_not(rotary))
    def _():
        out_ref[...] = acc.astype(bf16)


def project_qkv(x, gain, cosine, sine, offsets, pieces):
    tokens, width = x.shape
    columns = pieces[0][0].shape[1]
    tile = 256
    return call(
        qkv_kernel,
        (columns // tile,),
        [whole(x.shape), whole(gain.shape), whole(cosine.shape), whole(sine.shape)]
        + [pl.BlockSpec((n, tile), lambda i, *_: (0, i)) for _, n in pieces],
        [pl.BlockSpec((tokens, tile), lambda i, *_: (0, i)), whole(x.shape)],
        [jax.ShapeDtypeStruct((tokens, columns), bf16), jax.ShapeDtypeStruct(x.shape, bf16)],
        prefetch=1,
        flops=2 * tokens * width * columns,
        moved=2 * width * columns + 4 * tokens * columns,
    )(offsets, x, gain, cosine, sine, *[p for p, _ in pieces])


def back_kernel(offsets, x_ref, *refs):
    pieces, (out_ref, acc_ref) = refs[:-2], refs[-2:]
    step = pl.program_id(0)
    for n, w_ref in enumerate(pieces):
        rows = w_ref.shape[0]
        span = pl.ds(pl.multiple_of(offsets[n], LANES), rows)
        part = dot_nt(x_ref[...], w_ref[...])
        acc_ref[:, span] = jnp.where(step == 0, part, acc_ref[:, span] + part)

    @pl.when(step == pl.num_programs(0) - 1)
    def _():
        out_ref[...] = acc_ref[...].astype(out_ref.dtype)


def project_back(x, offsets, pieces, dtype):
    tokens, columns = x.shape
    width = sum(n for _, n in pieces)
    tile = 512
    return call(
        back_kernel,
        (columns // tile,),
        [pl.BlockSpec((tokens, tile), lambda i, *_: (0, i))]
        + [pl.BlockSpec((n, tile), lambda i, *_: (0, i)) for _, n in pieces],
        whole((tokens, width)),
        jax.ShapeDtypeStruct((tokens, width), dtype),
        scratch=[pltpu.VMEM((tokens, width), f32)],
        prefetch=1,
        flops=2 * tokens * width * columns,
        moved=2 * width * columns + 6 * tokens * columns,
    )(offsets, x, *[p for p, _ in pieces])


def weight_grad_kernel(core, x_ref, y_ref, keep_ref, away_ref):
    rows = keep_ref.shape[1]
    for n, out_ref in enumerate((keep_ref, away_ref)):
        part = core[0] if n == 0 else 1 - core[0]
        start = pl.multiple_of(part * rows, LANES)
        out_ref[0] = dot_tn(x_ref[:, pl.ds(start, rows)], y_ref[...]).astype(bf16)


def weight_grad(core, x, y, block=0, blocks=1):
    tokens, width = x.shape
    columns = y.shape[1] // blocks
    half = width // 2
    shape = (2, half // 2, columns)
    return call(
        weight_grad_kernel,
        (2,),
        [
            pl.BlockSpec((tokens, half), lambda i, *_: (0, i)),
            pl.BlockSpec((tokens, columns), lambda i, *_: (0, block)),
        ],
        [pl.BlockSpec((1,) + shape[1:], lambda i, *_: (i, 0, 0))] * 2,
        [jax.ShapeDtypeStruct(shape, bf16)] * 2,
        prefetch=1,
        flops=2 * tokens * width * columns,
        moved=4 * width * columns,
    )(core, x, y)


def attend_kernel(q_ref, k_ref, v_ref, bias_ref, *refs):
    o_ref, p_ref = refs[-2:]
    scores = dot_nt(q_ref[...], k_ref[...]) * (1.0 / math.sqrt(HEAD_DIM)) + bias_ref[...]
    peak = jnp.max(scores, axis=1, keepdims=True)
    exps = jnp.exp(scores - peak)
    probs = (exps * (1.0 / jnp.sum(exps, axis=1, keepdims=True))).astype(bf16)
    p_ref[0] = probs
    o_ref[...] = dot(probs, v_ref[...]).astype(bf16)


def attend(qkv, keys_values, bias, group, kept):
    tokens = qkv.shape[0]
    keys = keys_values.shape[0]
    kept = [] if kept is None else list(kept)
    return call(
        attend_kernel,
        (GROUP,),
        [
            pl.BlockSpec((tokens, HEAD_DIM), lambda h: (0, group * GROUP + h)),
            pl.BlockSpec((keys, HEAD_DIM), lambda h: (0, group)),
            pl.BlockSpec((keys, HEAD_DIM), lambda h: (0, KV_HEADS + group)),
            whole(bias.shape),
        ]
        + [pl.BlockSpec(memory_space=pl.ANY)] * len(kept),
        [
            pl.BlockSpec((tokens, HEAD_DIM), lambda h: (0, group * GROUP + h)),
            pl.BlockSpec((1, tokens, keys), lambda h: (group * GROUP + h, 0, 0)),
        ],
        [
            jax.ShapeDtypeStruct((tokens, HEADS * HEAD_DIM), bf16),
            jax.ShapeDtypeStruct((HEADS, tokens, keys), bf16),
        ],
        flops=4 * GROUP * tokens * keys * HEAD_DIM,
        moved=2 * GROUP * tokens * keys,
        aliases={4 + n: n for n in range(len(kept))},
    )(qkv, keys_values, keys_values, bias, *kept)


def attend_back_kernel(p_ref, do_ref, q_ref, k_ref, v_ref, cos_ref, sin_ref, dq_ref, dk_ref, dv_ref):
    scale = 1.0 / math.sqrt(HEAD_DIM)
    member = lax.rem(pl.program_id(0), GROUP)
    probs = p_ref[0]
    wide = probs.astype(f32)
    do = do_ref[...]
    grad_probs = dot_nt(do, v_ref[...])
    delta = jnp.sum(wide * grad_probs, axis=1, keepdims=True)
    grad_scores = (wide * (grad_probs - delta)).astype(bf16)
    dq = dot(grad_scores, k_ref[...]) * scale
    dq_ref[...] = (dq * cos_ref[...] - pltpu.roll(dq, HEAD_DIM // 2, 1) * sin_ref[...]).astype(bf16)
    dk = dot_tn(grad_scores, q_ref[...]) * scale
    dv = dot_tn(probs, do)

    @pl.when(member == 0)
    def _():
        dk_ref[...] = dk
        dv_ref[...] = dv

    @pl.when(member > 0)
    def _():
        dk_ref[...] += dk
        dv_ref[...] += dv


def attend_back(probs, do, qkv, keys_values, cosine, sine):
    tokens = qkv.shape[0]
    keys = keys_values.shape[0]
    kv_width = KV_HEADS * HEAD_DIM
    return call(
        attend_back_kernel,
        (HEADS,),
        [
            pl.BlockSpec((1, tokens, keys), lambda h: (h, 0, 0)),
            pl.BlockSpec((tokens, HEAD_DIM), lambda h: (0, h)),
            pl.BlockSpec((tokens, HEAD_DIM), lambda h: (0, h)),
            pl.BlockSpec((keys, HEAD_DIM), lambda h: (0, h // GROUP)),
            pl.BlockSpec((keys, HEAD_DIM), lambda h: (0, KV_HEADS + h // GROUP)),
            whole(cosine.shape),
            whole(sine.shape),
        ],
        [
            pl.BlockSpec((tokens, HEAD_DIM), lambda h: (0, h)),
            pl.BlockSpec((keys, HEAD_DIM), lambda h: (0, h // GROUP)),
            pl.BlockSpec((keys, HEAD_DIM), lambda h: (0, h // GROUP)),
        ],
        [
            jax.ShapeDtypeStruct((tokens, HEADS * HEAD_DIM), bf16),
            jax.ShapeDtypeStruct((keys, kv_width), f32),
            jax.ShapeDtypeStruct((keys, kv_width), f32),
        ],
        flops=8 * HEADS * tokens * keys * HEAD_DIM,
        moved=2 * HEADS * tokens * keys,
    )(probs, do, qkv, keys_values, keys_values, cosine, sine)


def middle_kernel(experts, offsets, o_ref, x_ref, gain_ref, router_ref, routes_ref, *refs):
    pieces, (middle_ref, payload_ref, gates_ref) = refs[:-3], refs[-3:]
    step = pl.program_id(0)
    tile = x_ref.shape[1]
    acc = x_ref[...].astype(f32)
    for n, w_ref in enumerate(pieces):
        start = pl.multiple_of(offsets[n], LANES)
        acc = acc + dot(o_ref[:, pl.ds(start, w_ref.shape[0])], w_ref[...])
    middle_ref[:, pl.ds(pl.multiple_of(step * tile, tile), tile)] = acc

    @pl.when(step == pl.num_programs(0) - 1)
    def _():
        middle = middle_ref[...]
        width = middle.shape[1]
        r = lax.rsqrt(jnp.mean(middle * middle, axis=1, keepdims=True) + EPSILON)
        h = (middle * r * gain_ref[...]).astype(bf16)
        payload_ref[:, :width] = h
        logits = dot_nt(h, router_ref[...])
        lane = lax.broadcasted_iota(jnp.int32, logits.shape, 1)
        chosen = lane == routes_ref[:, 0:1]
        for k in range(1, TOP):
            chosen = chosen | (lane == routes_ref[:, k : k + 1])
        logits = jnp.where(chosen, logits, MASKED)
        exps = jnp.where(chosen, jnp.exp(logits - jnp.max(logits, axis=1, keepdims=True)), 0.0)
        gates = exps / jnp.sum(exps, axis=1, keepdims=True)
        gates_ref[...] = gates
        high = gates.astype(bf16).astype(f32)
        payload_ref[:, width:] = (high + pltpu.roll(gates - high, experts, 1)).astype(bf16)


def project_out(o, x, gain, router, routes, offsets, pieces, experts):
    tokens, width = x.shape
    tile = 256
    return call(
        functools.partial(middle_kernel, experts),
        (width // tile,),
        [
            whole(o.shape),
            pl.BlockSpec((tokens, tile), lambda i, *_: (0, i)),
            whole(gain.shape),
            whole(router.shape),
            whole(routes.shape),
        ]
        + [pl.BlockSpec((n, tile), lambda i, *_: (0, i)) for _, n in pieces],
        [whole((tokens, width)), whole((tokens, width + LANES)), whole((tokens, LANES))],
        [
            jax.ShapeDtypeStruct((tokens, width), f32),
            jax.ShapeDtypeStruct((tokens, width + LANES), bf16),
            jax.ShapeDtypeStruct((tokens, LANES), f32),
        ],
        prefetch=1,
        flops=2 * tokens * width * o.shape[1],
        moved=2 * width * o.shape[1] + 10 * tokens * width,
    )(offsets, o, x, gain, router, routes, *[p for p, _ in pieces])


def one_hot(slots_ref, j, rows):
    tokens = slots_ref.shape[1]
    slot = lax.broadcasted_iota(jnp.int32, (rows, tokens), 0)
    return jnp.where(slot == slots_ref[j : j + 1, :], 1.0, 0.0).astype(bf16)


def select_kernel(order, slots_ref, block_ref, own_ref, near_ref, chips_ref):
    rows = own_ref.shape[0]
    picks = jnp.concatenate([one_hot(slots_ref.at[0], j, rows) for j in range(PLANE)], axis=0)
    chosen = dot(picks, block_ref[...]).astype(bf16)
    own_ref[...] = chosen[:rows]
    near_ref[...] = chosen[rows : 2 * rows]
    chips_ref[0] = chosen[2 * rows : 3 * rows]
    chips_ref[1] = chosen[3 * rows :]


def select(slots, blocks, order, rows):
    count, _, tokens = slots.shape
    width = blocks.shape[1]
    shapes = [(count * rows, width), (count * rows, width), (2, count * rows, width)]
    return call(
        select_kernel,
        (count,),
        [
            pl.BlockSpec((1, PLANE, tokens), lambda k, order: (k, 0, 0)),
            pl.BlockSpec((tokens, width), lambda k, order: (order[k], 0)),
        ],
        [
            pl.BlockSpec((rows, width), lambda k, order: (k, 0)),
            pl.BlockSpec((rows, width), lambda k, order: (k, 0)),
            pl.BlockSpec((2, rows, width), lambda k, order: (0, k, 0)),
        ],
        [jax.ShapeDtypeStruct(shape, bf16) for shape in shapes],
        prefetch=1,
        flops=2 * count * PLANE * rows * tokens * width,
        moved=2 * count * (PLANE * rows + tokens) * width,
    )(order, slots, blocks)


def piece_specs(rows, width, part):
    first = pl.BlockSpec((1, rows, width), lambda *_: (0, part, 0))
    second = pl.BlockSpec((1, rows, width), lambda *_: (1, part, 0))
    return [pl.BlockSpec((rows, width), lambda *_: (part, 0)), first, first, second]


def piece_rows(refs):
    return [ref[0] if len(ref.shape) == 3 else ref[...] for ref in refs]


def combine_kernel(slots_ref, *refs):
    parts, rest = refs[:PLANE], refs[PLANE:]
    out = rest[-1]
    rows = parts[0].shape[0]
    picks = jnp.concatenate([one_hot(slots_ref, j, rows) for j in range(PLANE)], axis=0)
    total = dot_tn(picks, jnp.concatenate(piece_rows(parts), axis=0))
    if len(rest) > 1:
        total = total + rest[0][...].astype(f32)
    out[...] = total.astype(out.dtype)


def combine(slots, parts, part, rows, before, dtype):
    tokens = slots.shape[1]
    width = parts[0].shape[1]
    extra = [] if before is None else [before]
    return call(
        combine_kernel,
        (1,),
        [whole(slots.shape)] + piece_specs(rows, width, part) + [whole((tokens, width))] * len(extra),
        whole((tokens, width)),
        jax.ShapeDtypeStruct((tokens, width), dtype),
        flops=2 * PLANE * rows * tokens * width,
        moved=2 * (PLANE * rows + 3 * tokens) * width,
    )(slots, *parts, *extra)


def expert_kernel(experts, count, at, *refs):
    xs, cs = refs[:PLANE], refs[PLANE : 2 * PLANE]
    weights = refs[2 * PLANE : 2 * PLANE + 3 * count]
    wgs, wus, wds = weights[:count], weights[count : 2 * count], weights[2 * count :]
    y_acc, d_acc, gate_ref = refs[-3:]
    outs = refs[-3 - 2 * PIECES - 5 : -3]
    drows, ys = outs[:PIECES], outs[PIECES : 2 * PIECES]
    x_ref, dy_ref, a_ref, dg_ref, du_ref = outs[2 * PIECES :]
    xs = [ref.at[0] if len(ref.shape) == 3 else ref for ref in xs]
    cs = [ref.at[0] if len(ref.shape) == 3 else ref for ref in cs]
    drows = [drows[0], drows[1], drows[2].at[0], drows[2].at[1]]
    ys = [ys[0], ys[1], ys[2].at[0], ys[2].at[1]]
    step = pl.program_id(0)
    expert = at[0]
    rows = xs[0].shape[0]
    width = x_ref.shape[1]
    size = width // count
    lane = lax.broadcasted_iota(jnp.int32, (rows, LANES), 1)
    spans = [pl.ds(pl.multiple_of(at[1 + n], LANES), size) for n in range(count)]

    @pl.when(step == 0)
    def _():
        for j in range(PLANE):
            span = slice(j * rows, (j + 1) * rows)
            x_ref[span, :] = xs[j][:, :width]
            tail = xs[j][:, width:].astype(f32)
            mine = (lane == expert) | (lane == expert + experts)
            gate = jnp.sum(jnp.where(mine, tail, 0.0), axis=1, keepdims=True)
            gate_ref[span, :] = jnp.broadcast_to(gate, (rows, LANES))
            dy_ref[span, :] = (gate * cs[j][...].astype(f32)).astype(bf16)

    def total(values):
        return functools.reduce(lambda a, b: a + b, values)

    g = total([dot(x_ref[:, span], w[...]) for span, w in zip(spans, wgs)])
    u = total([dot(x_ref[:, span], w[...]) for span, w in zip(spans, wus)])
    sigma = 1.0 / (1.0 + jnp.exp(-g))
    swish = g * sigma
    a = (swish * u).astype(bf16)
    da = total([dot_nt(dy_ref[:, span], w[...]) for span, w in zip(spans, wds)])
    dg = (da * u * sigma * (1.0 + g * (1.0 - sigma))).astype(bf16)
    du = (da * swish).astype(bf16)
    a_ref[...] = a
    dg_ref[...] = dg
    du_ref[...] = du
    for span, wg, wu, wd in zip(spans, wgs, wus, wds):
        y = dot(a, wd[...])
        d = dot_nt(dg, wg[...]) + dot_nt(du, wu[...])
        first = step == 0
        y_acc[:, span] = jnp.where(first, y, y_acc[:, span] + y)
        d_acc[:, span] = jnp.where(first, d, d_acc[:, span] + d)

    @pl.when(step == pl.num_programs(0) - 1)
    def _():
        for j in range(PLANE):
            span = slice(j * rows, (j + 1) * rows)
            yj = y_acc[span, :].astype(bf16).astype(f32)
            ys[j][...] = (gate_ref[span, 0:1] * yj).astype(bf16)
            dgate = jnp.sum(cs[j][...].astype(f32) * yj, axis=1, keepdims=True)
            high = dgate.astype(bf16).astype(f32)
            tail = jnp.where(lane == expert, high, 0.0) + jnp.where(lane == expert + experts, dgate - high, 0.0)
            drows[j][:, :width] = d_acc[span, :].astype(bf16)
            drows[j][:, width:] = tail.astype(bf16)


def run_expert(index, starts, part, parts, rows, experts, xs, cs, gates, ups, downs, kept):
    width = cs[0].shape[1]
    count = len(gates)
    size = width // count
    hidden = gates[0][0].shape[1]
    tile = 256
    total = PLANE * rows
    at = jnp.stack([index] + starts).astype(jnp.int32)
    kept = [] if kept is None else list(kept)
    big = [width, width, hidden, hidden, hidden]
    pieces = lambda n, wide: [(n * rows, wide), (n * rows, wide), (2, n * rows, wide)]

    def wide(array, block):
        return pl.BlockSpec((size, tile), lambda i, *_: (block, i))

    def tall(array, block):
        return pl.BlockSpec((tile, size), lambda i, *_: (block * (hidden // tile) + i, 0))

    return call(
        functools.partial(expert_kernel, experts, count),
        (hidden // tile,),
        piece_specs(rows, width + LANES, 0)
        + piece_specs(rows, width, 0)
        + [wide(*w) for w in gates]
        + [wide(*w) for w in ups]
        + [tall(*w) for w in downs]
        + [pl.BlockSpec(memory_space=pl.ANY)] * len(kept),
        [whole(shape) for shape in pieces(1, width + LANES)]
        + [
            pl.BlockSpec((rows, width), lambda i, *_: (part, 0)),
            pl.BlockSpec((rows, width), lambda i, *_: (part, 0)),
            pl.BlockSpec((2, rows, width), lambda i, *_: (0, part, 0)),
        ]
        + [pl.BlockSpec((total, width), lambda i, *_: (part, 0))] * 2
        + [pl.BlockSpec((total, tile), lambda i, *_: (part, i))] * 3,
        [jax.ShapeDtypeStruct(shape, bf16) for shape in pieces(1, width + LANES) + pieces(parts, width)]
        + [jax.ShapeDtypeStruct((parts * total, n), bf16) for n in big],
        scratch=[pltpu.VMEM((total, width), f32), pltpu.VMEM((total, width), f32), pltpu.VMEM((total, LANES), f32)],
        prefetch=1,
        flops=12 * total * width * hidden,
        moved=6 * width * hidden + 16 * total * width,
        aliases={1 + 2 * PLANE + 3 * count + n: PIECES + n for n in range(len(kept))},
    )(at, *xs, *cs, *[w[0] for w in gates + ups + downs], *kept)


def fence(*values):
    leaves, tree = jax.tree.flatten(values)
    arrays = [n for n, leaf in enumerate(leaves) if isinstance(leaf, jax.Array)]
    for n, leaf in zip(arrays, lax.optimization_barrier([leaves[n] for n in arrays])):
        leaves[n] = leaf
    return jax.tree.unflatten(tree, leaves)


def after(value, *others):
    return fence(value, *others)[0]


def rope_tables(position):
    half_width = HEAD_DIM // 2
    frequency = ROPE_BASE ** (-jnp.arange(half_width, dtype=f32) / half_width)
    angle = position.astype(f32)[:, None] * frequency[None, :]
    cosine, sine = jnp.cos(angle), jnp.sin(angle)
    return jnp.concatenate([cosine, cosine], axis=1), jnp.concatenate([-sine, sine], axis=1)


def on_device(
    copies,
    experts,
    tokens,
    cotangent,
    segment_ids,
    padding,
    routes,
    placement_order,
    norm_attn,
    w_query,
    w_key,
    w_value,
    w_out,
    norm_ffn,
    w_router,
    w_gate,
    w_up,
    w_down,
):
    planes = experts // PLANE
    paired = copies == 2
    d = lax.axis_index("dp")
    e = lax.axis_index("expert")
    z, q = e // PLANE, lax.rem(e, PLANE)
    core = lax.rem(e, 2)

    def swap(value):
        return lax.ppermute(value, "dp", [(0, 1), (1, 0)])

    def across(value, j):
        return lax.ppermute(value, "expert", [(i, i ^ j) for i in range(experts)])

    def ahead(value):
        return lax.ppermute(value, "expert", [(i, (i + PLANE) % experts) for i in range(experts)])

    def join(own, other, index, axis):
        first = jnp.where(index == 0, own, other)
        second = jnp.where(index == 0, other, own)
        return jnp.concatenate([first, second], axis=axis)

    def gather(own, axis):
        if paired:
            return join(own, swap(own), d, axis)
        return lax.all_gather(own, "dp", axis=axis, tiled=True)

    def half_rows(own):
        half = own.shape[0] // 2
        return lax.dynamic_slice_in_dim(own, core * half, half, 0)

    def assemble(pieces):
        if len(pieces) == 1:
            return pieces[0]
        own, got, twin = pieces
        return join(own, join(got, twin, core, 0), d, 0)

    def z_send(value, s):
        return lax.ppermute(value, "expert", [(i, (i + s * PLANE) % experts) for i in range(experts)])

    x = tokens[0]
    cot = cotangent[0]
    tok_count, width = x.shape
    position = d * tok_count + jnp.arange(tok_count, dtype=jnp.int32)
    kv_width = KV_HEADS * HEAD_DIM
    q_width = HEADS * HEAD_DIM

    capacity = tok_count * TOP * 9 // (8 * experts)
    rows = (capacity + 15) // 16 * 16
    far = tok_count * TOP
    wishes = jnp.concatenate([routes[0].T, placement_order[0].T], axis=0)
    if paired:
        got_half = jnp.concatenate([half_rows(w_query), half_rows(w_key), half_rows(w_value)], axis=1)
        wishes, got_half = fence(wishes, got_half)
    ring_wishes = jnp.stack([wishes] + [z_send(wishes, k) for k in range(1, planes)])
    near = jnp.stack([z * PLANE + (q ^ j) for j in range(PLANE)]).astype(jnp.int32)
    hits = ring_wishes[:, None, :TOP] == near[None, :, None, None]
    order = jnp.min(jnp.where(hits, ring_wishes[:, None, TOP:], far), axis=2)
    rank = jnp.sum((order[:, :, None, :] < order[:, :, :, None]).astype(jnp.int32), axis=3)
    slots = jnp.where((order < far) & (rank < capacity), rank, -1)

    small_own = jnp.concatenate([norm_attn[None], norm_ffn[None], w_router.T], axis=0)
    own_info = jnp.where(padding[0] == 1, segment_ids[0], -1)[None]
    qkv_own = jnp.concatenate([w_query, w_key, w_value], axis=1)
    cosine, sine = rope_tables(position)
    cot_one = ahead(cot)
    if paired:
        size = w_query.shape[0]
        start = (1 - d) * size
        offsets = jnp.stack([d * size, start + core * size // 2, start + (1 - core) * size // 2]).astype(jnp.int32)
        first_own = jnp.concatenate(
            [small_own, jnp.pad(own_info.astype(bf16), ((0, 0), (0, size - tok_count)))], axis=0
        ).reshape(-1)
        columns = got_half.shape[1]
        first_rows = -(-first_own.shape[0] // (16 * columns)) * 16
        first_count = first_own.shape[0]
        first_own = jnp.pad(first_own, (0, first_rows * columns - first_count)).reshape(first_rows, columns)
        got = swap(jnp.concatenate([got_half, first_own], axis=0))
        first_other = got[size // 2 :].reshape(-1)[:first_count].reshape(-1, size)
        cut = size // 6 // LANES * LANES
        out_half = half_rows(w_out)
        out_late, out_soon = out_half[:cut], out_half[cut:]
        out_offsets = [d * size]
        for begin in (0, cut):
            out_offsets += [start + core * size // 2 + begin, start + (1 - core) * size // 2 + begin]
        out_offsets = jnp.stack(out_offsets).astype(jnp.int32)
        first_own = jnp.concatenate(
            [small_own, jnp.pad(own_info.astype(bf16), ((0, 0), (0, size - tok_count)))], axis=0
        ).reshape(-1)
        columns = got_half.shape[1]
        first_rows = -(-first_own.shape[0] // (16 * columns)) * 16
        first_count = first_own.shape[0]
        first_own = jnp.pad(first_own, (0, first_rows * columns - first_count)).reshape(first_rows, columns)
        got = swap(jnp.concatenate([got_half, first_own], axis=0))
        first_other = got[size // 2 :].reshape(-1)[:first_count].reshape(-1, size)
        cut = size // 6 // LANES * LANES
        out_half = half_rows(w_out)
        out_late, out_soon = out_half[:cut], out_half[cut:]
        out_offsets = [d * size]
        for begin in (0, cut):
            out_offsets += [start + core * size // 2 + begin, start + (1 - core) * size // 2 + begin]
        out_offsets = jnp.stack(out_offsets).astype(jnp.int32)
        small = join(small_own, first_other[:-1], d, 1)
        info = jnp.concatenate([own_info, first_other[-1:, :tok_count].astype(jnp.int32)], axis=1)
        other_position = (1 - d) * tok_count + jnp.arange(tok_count, dtype=jnp.int32)
        key_place = jnp.concatenate([position, other_position])[None]
    else:
        small = gather(small_own, 1)
        offsets = out_offsets = jnp.zeros((1,), jnp.int32)
        out_soon = out_late = ()
        got = lax.all_gather(qkv_own, "dp", axis=0, tiled=True)
        info = lax.all_gather(own_info, "dp", axis=1, tiled=True)
        key_place = jnp.arange(copies * tok_count, dtype=jnp.int32)[None]
    gain_one = small[0:1].astype(f32)
    gain_two = small[1:2].astype(f32)
    router_rows = jnp.pad(small[2:], ((0, LANES - experts), (0, 0)))
    small = small[2:]
    segment, place = segment_ids[0][:, None], position[:, None]
    allowed = (key_place <= place) & (info == segment) | (key_place == place)
    bias = jnp.where(allowed, 0.0, MASKED)

    def exchange(own, near_by, chips):
        return own, near_by, across(chips, 2)

    def relay(parts):
        own, near_by, landed = parts
        near_by = across(jnp.concatenate([near_by[None], landed[1:]], axis=0), 1)
        return [own, near_by, landed, near_by]

    first = jnp.zeros((1,), jnp.int32)

    def hand_out(k, block):
        return exchange(*select(slots[k : k + 1], block, first, rows))

    cots = {0: select(slots[:1], cot, first, rows)}
    expert_own = [w_gate[0], w_up[0], w_down[0]]
    got, slots, qkv_own, out_soon, out_late, cosine, sine, cots[0], cot_one = fence(
        got, slots, qkv_own, out_soon, out_late, cosine, sine, cots[0], cot_one
    )
    cot_two = ahead(cot_one)
    if paired:
        qkv_pieces = [(qkv_own, size), (got, size // 2), (across(got, 1), size // 2)]
        out_soon = swap(out_soon)
    else:
        qkv_pieces = [(got, width)]
        out_soon = lax.all_gather(w_out, "dp", axis=0, tiled=True)
    cots[0] = exchange(*cots[0])
    qkv, hidden_one = project_qkv(x, gain_one, cosine, sine, offsets, qkv_pieces)

    own_kv = qkv[:, q_width:]
    bias, gain_two, router_rows, small = after((bias, gain_two, router_rows, small), own_kv)
    cots[1] = select(slots[1:2], after(cot_one, own_kv), first, rows)
    if paired:
        keys_values = jnp.concatenate([own_kv, swap(own_kv)], axis=0)
    else:
        keys_values = lax.all_gather(own_kv, "dp", axis=0, tiled=True)
    keys_values, out_soon, cots[0], cots[1], bias, gain_two, router_rows, small = fence(
        keys_values, out_soon, cots[0], cots[1], bias, gain_two, router_rows, small
    )
    if paired:
        out_late = swap(after(out_late, keys_values))
        out_pieces = [(out_soon, size // 2 - cut), (across(out_soon, 1), size // 2 - cut)]
        expert_other = [swap(after(expert_own[0], out_late))]
        starts = [d * width // 2, (1 - d) * width // 2]
    else:
        out_pieces = [(out_soon, q_width)]
        starts = [jnp.int32(0)]
    cots[1] = exchange(*cots[1])
    seen = attend(qkv, keys_values, bias, 0, None)
    seen, cot_two, out_late = fence(seen, cot_two, out_late)
    ring_cot = [cot, cot_one, cot_two]
    for _ in range(3, planes):
        ring_cot.append(ahead(ring_cot[-1]))
    if paired:
        out_pieces = [(w_out, size), (out_late, cut), (across(out_late, 1), cut)] + out_pieces
    attended, probs = attend(qkv, keys_values, bias, 1, seen)
    attended, cots[1], out_pieces = fence(attended, cots[1], out_pieces)

    middle, payload, gates = project_out(
        attended, x, gain_two, router_rows, routes[0], out_offsets, out_pieces, experts
    )
    if paired:
        payload, expert_other[0] = fence(payload, expert_other[0])
        expert_other.append(swap(after(expert_own[1], payload)))

    ring = [payload, ahead(payload)]
    xs, drows, kept = {}, {}, None

    def work(k, kept):
        outs = run_expert(e, starts, k, planes, rows, experts, xs[k], cots[k], *expert_weights, kept)
        drows[k] = outs[:PIECES]
        return outs[PIECES:]

    def give_back(k, before, dtype):
        return combine(slots[k], drows[k], 0, rows, before, dtype)

    for k in range(2, planes):
        cots[k] = hand_out(k, after(ring_cot[k], payload))
    cots[0] = relay(after(cots[0], payload))
    cots[1] = relay(after(cots[1], payload))
    if paired:
        ring[1], cots, expert_other = fence(ring[1], cots, expert_other)
        expert_other.append(swap(after(expert_own[2], ring[1])))
        expert_weights = [[(own, 0), (other, 0)] for own, other in zip(expert_own, expert_other)]
    else:
        ring[1], cots = fence(ring[1], cots)
        expert_weights = [
            [(lax.all_gather(w, "dp", axis=axis, tiled=True), 0)] for w, axis in zip(expert_own, (0, 0, 1))
        ]
    ring.append(ahead(ring[1]))
    xs[1] = hand_out(1, ring[1])
    xs[0] = select(slots[:1], after(payload, ring[1]), first, rows)
    for k in range(2, planes):
        cots[k] = relay(cots[k])
    ring[2], xs, cots, expert_weights = fence(ring[2], xs, cots, expert_weights)
    for k in range(3, planes):
        ring.append(ahead(ring[k - 1]))
    xs[1] = relay(xs[1])
    xs[0] = exchange(*xs[0])
    xs[2] = hand_out(2, ring[2])
    kept = work(1, kept)
    drows[1], kept, xs[0] = fence(drows[1], kept, xs[0])
    drows[1] = exchange(*drows[1])
    xs[0] = relay(xs[0])
    kept = work(0, kept)
    back = None
    last = planes - 1
    for k in range(2, planes):
        drows[k - 1], xs[k], kept, back, *ring[k + 1 :] = fence(drows[k - 1], xs[k], kept, back, *ring[k + 1 :])
        drows[k - 1] = relay(drows[k - 1])
        xs[k] = relay(xs[k])
        if k < last:
            back = give_back(k - 1, back, bf16)
            back, xs[k] = fence(back, xs[k])
            back = ahead(back)
            xs[k + 1] = hand_out(k + 1, ring[k + 1])
        kept = work(k, kept)
        drows[k], kept = fence(drows[k], kept)
        drows[k] = exchange(*drows[k])
        if k == last - 1:
            xs[last] = fence(xs[last], kept)[0]
            xs[last] = relay(xs[last])
            kept = work(last, kept)
            drows[last], kept, drows[k], back = fence(drows[last], kept, drows[k], back)
            drows[k] = relay(drows[k])
            back = give_back(k, back, bf16)
            drows[last], kept, drows[0], back = fence(drows[last], kept, drows[0], back)
            back = ahead(back)
            drows[last] = exchange(*drows[last])
            drows[0] = exchange(*drows[0])
            break

    ys, (row_all, dy_all, a_all, dg_all, du_all) = kept[:PIECES], kept[PIECES:]
    grad_gate_local = dot_tn(row_all, dg_all)
    grad_up_local = dot_tn(row_all, du_all)
    grad_down_local = dot_tn(a_all, dy_all)

    def split_half(full, axis):
        size = full.shape[axis] // 2
        away = lax.dynamic_slice_in_dim(full, (1 - d) * size, size, axis).astype(bf16)
        return lax.dynamic_slice_in_dim(full, d * size, size, axis), away

    locals_ = ((grad_gate_local, 0), (grad_up_local, 0), (grad_down_local, 1))
    if paired:
        halves = [split_half(full, axis) for full, axis in locals_]
        kept_halves = [h[0] for h in halves]
        away = [h[1] for h in halves]
        drows, back, away, ys = fence(drows, back, away, ys)
        arrived = [swap(away[0])]
    else:
        drows, back, ys = fence(drows, back, ys)
        grad_gate, grad_up, grad_down = [
            lax.psum_scatter(full.astype(bf16), "dp", scatter_dimension=axis, tiled=True).astype(f32)[None]
            for full, axis in locals_
        ]
    drows[last] = relay(drows[last])
    back = ahead(give_back(last, back, bf16))
    drows[0] = relay(drows[0])
    ys = exchange(*after(ys, drows))
    if paired:
        back, drows[0], arrived[0] = fence(back, drows[0], arrived[0])
        arrived.append(swap(after(away[1], back)))
    else:
        back, drows[0] = fence(back, drows[0])
    back = give_back(0, back, f32)

    upstream = cot.astype(f32)
    gates = gates[:, :experts]
    dgates = back[:, width : width + experts] + back[:, width + experts : width + 2 * experts]
    dlogits = (gates * (dgates - jnp.sum(gates * dgates, axis=1, keepdims=True))).astype(bf16)
    hidden_two = payload[:, :width]
    dh2 = back[:, :width] + dot(dlogits, small)
    scale_two = lax.rsqrt(jnp.mean(middle * middle, axis=1, keepdims=True) + EPSILON)
    normed_two = middle * scale_two
    e2 = dh2 * gain_two
    dmiddle = upstream + scale_two * (e2 - normed_two * jnp.mean(e2 * normed_two, axis=1, keepdims=True))
    dmb = dmiddle.astype(bf16)
    half_index = jnp.stack([core if paired else 0]).astype(jnp.int32)
    grad_out = weight_grad(half_index, attended, dmb)
    do = project_back(dmb, out_offsets, out_pieces, bf16)

    other_chip = lax.rem(q // 2, 2)

    def add(*values):
        return functools.reduce(lambda a, b: a + b, [v.astype(f32) for v in values]).astype(bf16)

    def pick(value, index, axis=0):
        return lax.dynamic_index_in_dim(value, index, axis, keepdims=False)

    def cut_core(parts):
        return parts[0], across(parts[1], 1)

    def cut_dp(part):
        return pick(part, d), swap(pick(part, 1 - d))

    def cut_half(part, bit, j, axis):
        part = part.reshape(part.shape[:axis] + (2, -1, part.shape[-1]))
        return pick(part, bit, axis), across(pick(part, 1 - bit, axis), j)

    def both(part, j):
        return part, across(part, j)

    def sum_all(keep, away):
        both = jnp.concatenate([keep, away], axis=1).reshape(-1, keep.shape[2])
        part = lax.psum_scatter(both, "dp", scatter_dimension=0, tiled=True)
        return lax.psum(part, "expert").astype(f32)

    def unrotate(value):
        turned = jnp.concatenate([value[:, HEAD_DIM // 2 :], value[:, : HEAD_DIM // 2]], axis=1)
        return value * cosine - turned * sine

    if paired:
        low, high = lax.rem(z, 2), z // 2
        sum_out = cut_core(grad_out)
        do, ys, sum_out = fence(do, ys, sum_out)
        ys = relay(ys)
        sum_out = add(*sum_out)
        do, ys, sum_out = fence(do, ys, sum_out)
        sum_out = cut_half(sum_out, other_chip, 2, 1)
        mixture = ahead(combine(slots[1], ys, 1, rows, None, bf16))
    dqp, dk, dv = attend_back(probs, do, qkv, keys_values, cosine, sine)
    dkv = jnp.concatenate([dk, dv], axis=1)
    input_tokens = x.astype(f32)
    scale_one = lax.rsqrt(jnp.mean(input_tokens * input_tokens, axis=1, keepdims=True) + EPSILON)
    normed_one = input_tokens * scale_one
    grad_norm_ffn_local = jnp.sum(dh2 * normed_two, axis=0)
    grad_router_local = lax.dot_general(dlogits, hidden_two, (((0,), (0,)), ((), ())), preferred_element_type=f32)

    def unrotated(dkv):
        dkp = [unrotate(dkv[:, n * HEAD_DIM : (n + 1) * HEAD_DIM]) for n in range(KV_HEADS)]
        dkvp = jnp.concatenate([v.astype(bf16) for v in dkp] + [dkv[:, kv_width:].astype(bf16)], axis=1)
        return jnp.concatenate([dqp, dkvp], axis=1)

    def through_projections(dqkv):
        dh1 = project_back(dqkv, offsets, qkv_pieces, f32)
        grad_norm_attn_local = jnp.sum(dh1 * normed_one, axis=0)
        extra = jnp.concatenate(
            [grad_norm_attn_local[None], grad_norm_ffn_local[None], grad_router_local], axis=0
        ).astype(bf16)
        e1 = dh1 * gain_one
        grad_inputs = dmiddle + scale_one * (
            e1 - normed_one * jnp.mean(e1 * normed_one, axis=1, keepdims=True)
        )
        return extra, grad_inputs

    if paired:
        other_dkv, dqp = fence(dkv[tok_count:].astype(bf16), dqp)
        other_dkv = swap(other_dkv)
        sum_a = cut_core(weight_grad(half_index, hidden_one, dqp, 0, 1))
        sum_a, other_dkv, arrived, sum_out, mixture = fence(sum_a, other_dkv, arrived, sum_out, mixture)
        sum_a = cut_dp(add(*sum_a))
        mixture = ahead(combine(slots[2], ys, 2, rows, mixture, bf16))
        dqkv = unrotated(dkv[:tok_count] + other_dkv.astype(f32))
        sum_b = cut_core(weight_grad(half_index, hidden_one, dqkv[:, q_width:]))
        sum_b, dqkv = fence(sum_b, dqkv)
        sum_b = cut_half(add(*sum_b), other_chip, 2, 1)
        sum_out = cut_half(add(*sum_out), low, 4, 1)
        extra, grad_inputs = through_projections(dqkv)
        sum_a, sum_b, sum_out, extra, mixture = fence(sum_a, sum_b, sum_out, extra, mixture)
        sum_a = cut_half(add(*sum_a), other_chip, 2, 0)
        sum_b = cut_dp(add(*sum_b))
        sum_out = cut_half(add(*sum_out), high, 8, 1)
        extra = both(extra, 1)
        mixture = ahead(combine(slots[3], ys, 3, rows, mixture, bf16))
        arrived.append(swap(after(away[2], sum_a)))
        sum_a, sum_b, sum_out, extra = fence(sum_a, sum_b, sum_out, extra)
        sums = cut_half(jnp.concatenate([add(*sum_a), add(*sum_b)], axis=1), low, 4, 0)
        sum_out = cut_dp(add(*sum_out))
        extra = both(add(*extra), 2)
        sums, sum_out, extra = fence(sums, sum_out, extra)
        sums = cut_half(add(*sums), high, 8, 0)
        sum_out = both(add(*sum_out), 8)
        extra = both(add(*extra), 4)
        sums, sum_out, extra, mixture = fence(sums, sum_out, extra, mixture)
        sums = both(add(*sums), 8)
        sum_out = both(join(*sum_out, high, 0), 4)
        extra = both(add(*extra), 8)
        sums, sum_out, extra = fence(sums, sum_out, extra)
        sums = both(join(*sums, high, 0), 4)
        sum_out = both(join(*sum_out, low, 0), 2)
        extra = add(*extra)
        extra = (extra, swap(extra))
        sums, sum_out, extra, arrived = fence(sums, sum_out, extra, arrived)
        sums = both(join(*sums, low, 0), 2)
        sum_out = both(join(*sum_out, other_chip, 0), 1)
        extra = add(*extra)
        grad_gate, grad_up, grad_down = [
            (own + other.astype(f32))[None] for own, other in zip(kept_halves, arrived)
        ]
        sums, sum_out, extra, mixture, grad_gate, grad_up, grad_down = fence(
            sums, sum_out, extra, mixture, grad_gate, grad_up, grad_down
        )
        sums = both(join(*sums, other_chip, 0), 1)
        sum_out = join(*sum_out, core, 0).astype(f32)
        sums, sum_out = fence(sums, sum_out)
        sum_q, sum_key, sum_value = [
            join(sums[0][:, cols], sums[1][:, cols], core, 0).astype(f32)
            for cols in [
                slice(0, q_width),
                slice(q_width, q_width + kv_width),
                slice(q_width + kv_width, q_width + 2 * kv_width),
            ]
        ]
        extra = lax.dynamic_slice_in_dim(extra, d * size, size, 1).astype(f32)
    else:
        dkv = lax.psum_scatter(dkv.astype(bf16), "dp", scatter_dimension=0, tiled=True).astype(f32)
        dqkv = unrotated(dkv)
        extra, grad_inputs = through_projections(dqkv)
        sum_qkv = sum_all(*weight_grad(half_index, hidden_one, dqkv))
        sum_q, sum_key = sum_qkv[:, :q_width], sum_qkv[:, q_width : q_width + kv_width]
        sum_value = sum_qkv[:, q_width + kv_width :]
        sum_out = sum_all(*grad_out)
        extra = lax.psum_scatter(extra, "dp", scatter_dimension=1, tiled=True)
        extra = lax.psum(extra, "expert").astype(f32)
        ys = relay(ys)
        mixture = None
        for k in range(1, planes):
            mixture = ahead(combine(slots[k], ys, k, rows, mixture, bf16))
    mixture = combine(slots[0], ys, 0, rows, mixture, f32)
    mixed = (middle + mixture).astype(bf16)[None]
    return (
        mixed,
        grad_inputs[None],
        extra[0],
        sum_q,
        sum_key,
        sum_value,
        sum_out,
        extra[1],
        extra[2 : 2 + experts].T,
        grad_gate,
        grad_up,
        grad_down,
    )


def solution(mesh):
    rows = P("expert", "dp", None)
    return jax.shard_map(
        functools.partial(on_device, mesh.shape["dp"], mesh.shape["expert"]),
        mesh=mesh,
        in_specs=(
            rows,
            rows,
            P("expert", "dp"),
            P("expert", "dp"),
            rows,
            rows,
            P("dp"),
            P("dp", None),
            P("dp", None),
            P("dp", None),
            P("dp", None),
            P("dp"),
            P("dp", None),
            rows,
            rows,
            P("expert", None, "dp"),
        ),
        out_specs=(
            rows,
            rows,
            P("dp"),
            P("dp", None),
            P("dp", None),
            P("dp", None),
            P("dp", None),
            P("dp"),
            P("dp", None),
            rows,
            rows,
            P("expert", None, "dp"),
        ),
        check_vma=False,
    )
```

```python
import functools
import math

import jax
import jax.numpy as jnp
from jax import lax
from jax.experimental import pallas as pl
from jax.experimental.pallas import tpu as pltpu
from jax.sharding import PartitionSpec as P

HEADS = 12
KV_HEADS = 2
HEAD_DIM = 128
TOP = 4
GROUP = HEADS // KV_HEADS
PLANE = 4
LANES = 128
PIECES = 3

EPSILON = 1e-06
ROPE_BASE = 1000000.0
MASKED = -1e30
MIB = 1024 * 1024

f32 = jnp.float32
bf16 = jnp.bfloat16


def dot(a, b):
    return jnp.dot(a, b, preferred_element_type=f32)


def dot_nt(a, b):
    return lax.dot_general(a, b, (((1,), (1,)), ((), ())), preferred_element_type=f32)


def dot_tn(a, b):
    return lax.dot_general(a, b, (((0,), (0,)), ((), ())), preferred_element_type=f32)


def whole(shape):
    return pl.BlockSpec(shape, lambda *_: (0,) * len(shape))


def call(kernel, grid, in_specs, out_specs, out_shape, scratch=(), prefetch=0, flops=0, moved=0, vmem=20, aliases=None):
    return pl.pallas_call(
        kernel,
        grid_spec=pltpu.PrefetchScalarGridSpec(
            num_scalar_prefetch=prefetch,
            grid=grid,
            in_specs=in_specs,
            out_specs=out_specs,
            scratch_shapes=list(scratch),
        ),
        out_shape=out_shape,
        input_output_aliases=aliases or {},
        cost_estimate=pl.CostEstimate(flops=flops // 64, bytes_accessed=moved // 64, transcendentals=0),
        compiler_params=pltpu.CompilerParams(
            dimension_semantics=("arbitrary",) * len(grid), vmem_limit_bytes=vmem * MIB
        ),
    )


def qkv_kernel(offsets, x_ref, gain_ref, cos_ref, sin_ref, *refs):
    pieces, (out_ref, h_ref) = refs[:-2], refs[-2:]
    step = pl.program_id(0)

    @pl.when(step == 0)
    def _():
        x = x_ref[...].astype(f32)
        r = lax.rsqrt(jnp.mean(x * x, axis=1, keepdims=True) + EPSILON)
        h_ref[...] = (x * r * gain_ref[...]).astype(bf16)

    acc = None
    for n, w_ref in enumerate(pieces):
        rows = w_ref.shape[0]
        start = pl.multiple_of(offsets[n], LANES)
        part = dot(h_ref[:, pl.ds(start, rows)], w_ref[...])
        acc = part if acc is None else acc + part

    rotary = step * out_ref.shape[1] < (HEADS + KV_HEADS) * HEAD_DIM

    @pl.when(rotary)
    def _():
        for n in range(out_ref.shape[1] // HEAD_DIM):
            a = acc[:, n * HEAD_DIM : (n + 1) * HEAD_DIM]
            turned = a * cos_ref[...] + pltpu.roll(a, HEAD_DIM // 2, 1) * sin_ref[...]
            out_ref[:, n * HEAD_DIM : (n + 1) * HEAD_DIM] = turned.astype(bf16)

    @pl.when(jnp.logical_not(rotary))
    def _():
        out_ref[...] = acc.astype(bf16)


def project_qkv(x, gain, cosine, sine, offsets, pieces):
    tokens, width = x.shape
    columns = pieces[0][0].shape[1]
    tile = 256
    return call(
        qkv_kernel,
        (columns // tile,),
        [whole(x.shape), whole(gain.shape), whole(cosine.shape), whole(sine.shape)]
        + [pl.BlockSpec((n, tile), lambda i, *_: (0, i)) for _, n in pieces],
        [pl.BlockSpec((tokens, tile), lambda i, *_: (0, i)), whole(x.shape)],
        [jax.ShapeDtypeStruct((tokens, columns), bf16), jax.ShapeDtypeStruct(x.shape, bf16)],
        prefetch=1,
        flops=2 * tokens * width * columns,
        moved=2 * width * columns + 4 * tokens * columns,
    )(offsets, x, gain, cosine, sine, *[p for p, _ in pieces])


def back_kernel(offsets, x_ref, *refs):
    pieces, (out_ref, acc_ref) = refs[:-2], refs[-2:]
    step = pl.program_id(0)
    for n, w_ref in enumerate(pieces):
        rows = w_ref.shape[0]
        span = pl.ds(pl.multiple_of(offsets[n], LANES), rows)
        part = dot_nt(x_ref[...], w_ref[...])
        acc_ref[:, span] = jnp.where(step == 0, part, acc_ref[:, span] + part)

    @pl.when(step == pl.num_programs(0) - 1)
    def _():
        out_ref[...] = acc_ref[...].astype(out_ref.dtype)


def project_back(x, offsets, pieces, dtype):
    tokens, columns = x.shape
    width = sum(n for _, n in pieces)
    tile = 512
    return call(
        back_kernel,
        (columns // tile,),
        [pl.BlockSpec((tokens, tile), lambda i, *_: (0, i))]
        + [pl.BlockSpec((n, tile), lambda i, *_: (0, i)) for _, n in pieces],
        whole((tokens, width)),
        jax.ShapeDtypeStruct((tokens, width), dtype),
        scratch=[pltpu.VMEM((tokens, width), f32)],
        prefetch=1,
        flops=2 * tokens * width * columns,
        moved=2 * width * columns + 6 * tokens * columns,
    )(offsets, x, *[p for p, _ in pieces])


def weight_grad_kernel(core, x_ref, y_ref, keep_ref, away_ref):
    rows = keep_ref.shape[1]
    for n, out_ref in enumerate((keep_ref, away_ref)):
        part = core[0] if n == 0 else 1 - core[0]
        start = pl.multiple_of(part * rows, LANES)
        out_ref[0] = dot_tn(x_ref[:, pl.ds(start, rows)], y_ref[...]).astype(bf16)


def weight_grad(core, x, y, block=0, blocks=1):
    tokens, width = x.shape
    columns = y.shape[1] // blocks
    half = width // 2
    shape = (2, half // 2, columns)
    return call(
        weight_grad_kernel,
        (2,),
        [
            pl.BlockSpec((tokens, half), lambda i, *_: (0, i)),
            pl.BlockSpec((tokens, columns), lambda i, *_: (0, block)),
        ],
        [pl.BlockSpec((1,) + shape[1:], lambda i, *_: (i, 0, 0))] * 2,
        [jax.ShapeDtypeStruct(shape, bf16)] * 2,
        prefetch=1,
        flops=2 * tokens * width * columns,
        moved=4 * width * columns,
    )(core, x, y)


def attend_kernel(q_ref, k_ref, v_ref, bias_ref, o_ref, p_ref):
    scores = dot_nt(q_ref[...], k_ref[...]) * (1.0 / math.sqrt(HEAD_DIM)) + bias_ref[...]
    peak = jnp.max(scores, axis=1, keepdims=True)
    exps = jnp.exp(scores - peak)
    probs = (exps * (1.0 / jnp.sum(exps, axis=1, keepdims=True))).astype(bf16)
    p_ref[0] = probs
    o_ref[...] = dot(probs, v_ref[...]).astype(bf16)


def attend(qkv, keys_values, bias):
    tokens = qkv.shape[0]
    keys = keys_values.shape[0]
    return call(
        attend_kernel,
        (HEADS,),
        [
            pl.BlockSpec((tokens, HEAD_DIM), lambda h: (0, h)),
            pl.BlockSpec((keys, HEAD_DIM), lambda h: (0, h // GROUP)),
            pl.BlockSpec((keys, HEAD_DIM), lambda h: (0, KV_HEADS + h // GROUP)),
            whole(bias.shape),
        ],
        [
            pl.BlockSpec((tokens, HEAD_DIM), lambda h: (0, h)),
            pl.BlockSpec((1, tokens, keys), lambda h: (h, 0, 0)),
        ],
        [
            jax.ShapeDtypeStruct((tokens, HEADS * HEAD_DIM), bf16),
            jax.ShapeDtypeStruct((HEADS, tokens, keys), bf16),
        ],
        flops=4 * HEADS * tokens * keys * HEAD_DIM,
        moved=2 * HEADS * tokens * keys,
        vmem=20 * max(1, keys // 1024),
    )(qkv, keys_values, keys_values, bias)


def attend_back_kernel(p_ref, do_ref, q_ref, k_ref, v_ref, cos_ref, sin_ref, dq_ref, dk_ref, dv_ref):
    scale = 1.0 / math.sqrt(HEAD_DIM)
    member = lax.rem(pl.program_id(0), GROUP)
    probs = p_ref[0]
    wide = probs.astype(f32)
    do = do_ref[...]
    grad_probs = dot_nt(do, v_ref[...])
    delta = jnp.sum(wide * grad_probs, axis=1, keepdims=True)
    grad_scores = (wide * (grad_probs - delta)).astype(bf16)
    dq = dot(grad_scores, k_ref[...]) * scale
    dq_ref[...] = (dq * cos_ref[...] - pltpu.roll(dq, HEAD_DIM // 2, 1) * sin_ref[...]).astype(bf16)
    dk = dot_tn(grad_scores, q_ref[...]) * scale
    dv = dot_tn(probs, do)

    @pl.when(member == 0)
    def _():
        dk_ref[...] = dk
        dv_ref[...] = dv

    @pl.when(member > 0)
    def _():
        dk_ref[...] += dk
        dv_ref[...] += dv


def attend_back(probs, do, qkv, keys_values, cosine, sine):
    tokens = qkv.shape[0]
    keys = keys_values.shape[0]
    kv_width = KV_HEADS * HEAD_DIM
    return call(
        attend_back_kernel,
        (HEADS,),
        [
            pl.BlockSpec((1, tokens, keys), lambda h: (h, 0, 0)),
            pl.BlockSpec((tokens, HEAD_DIM), lambda h: (0, h)),
            pl.BlockSpec((tokens, HEAD_DIM), lambda h: (0, h)),
            pl.BlockSpec((keys, HEAD_DIM), lambda h: (0, h // GROUP)),
            pl.BlockSpec((keys, HEAD_DIM), lambda h: (0, KV_HEADS + h // GROUP)),
            whole(cosine.shape),
            whole(sine.shape),
        ],
        [
            pl.BlockSpec((tokens, HEAD_DIM), lambda h: (0, h)),
            pl.BlockSpec((keys, HEAD_DIM), lambda h: (0, h // GROUP)),
            pl.BlockSpec((keys, HEAD_DIM), lambda h: (0, h // GROUP)),
        ],
        [
            jax.ShapeDtypeStruct((tokens, HEADS * HEAD_DIM), bf16),
            jax.ShapeDtypeStruct((keys, kv_width), f32),
            jax.ShapeDtypeStruct((keys, kv_width), f32),
        ],
        flops=8 * HEADS * tokens * keys * HEAD_DIM,
        moved=2 * HEADS * tokens * keys,
        vmem=20 * max(1, keys // 1024),
    )(probs, do, qkv, keys_values, keys_values, cosine, sine)


def middle_kernel(experts, offsets, o_ref, x_ref, gain_ref, router_ref, routes_ref, *refs):
    pieces, (middle_ref, payload_ref, gates_ref) = refs[:-3], refs[-3:]
    step = pl.program_id(0)
    tile = x_ref.shape[1]
    acc = x_ref[...].astype(f32)
    for n, w_ref in enumerate(pieces):
        start = pl.multiple_of(offsets[n], LANES)
        acc = acc + dot(o_ref[:, pl.ds(start, w_ref.shape[0])], w_ref[...])
    middle_ref[:, pl.ds(pl.multiple_of(step * tile, tile), tile)] = acc

    @pl.when(step == pl.num_programs(0) - 1)
    def _():
        middle = middle_ref[...]
        width = middle.shape[1]
        r = lax.rsqrt(jnp.mean(middle * middle, axis=1, keepdims=True) + EPSILON)
        h = (middle * r * gain_ref[...]).astype(bf16)
        payload_ref[:, :width] = h
        logits = dot_nt(h, router_ref[...])
        lane = lax.broadcasted_iota(jnp.int32, logits.shape, 1)
        chosen = lane == routes_ref[:, 0:1]
        for k in range(1, TOP):
            chosen = chosen | (lane == routes_ref[:, k : k + 1])
        logits = jnp.where(chosen, logits, MASKED)
        exps = jnp.where(chosen, jnp.exp(logits - jnp.max(logits, axis=1, keepdims=True)), 0.0)
        gates = exps / jnp.sum(exps, axis=1, keepdims=True)
        gates_ref[...] = gates
        high = gates.astype(bf16).astype(f32)
        payload_ref[:, width:] = (high + pltpu.roll(gates - high, experts, 1)).astype(bf16)


def project_out(o, x, gain, router, routes, offsets, pieces, experts):
    tokens, width = x.shape
    tile = 256
    return call(
        functools.partial(middle_kernel, experts),
        (width // tile,),
        [
            whole(o.shape),
            pl.BlockSpec((tokens, tile), lambda i, *_: (0, i)),
            whole(gain.shape),
            whole(router.shape),
            whole(routes.shape),
        ]
        + [pl.BlockSpec((n, tile), lambda i, *_: (0, i)) for _, n in pieces],
        [whole((tokens, width)), whole((tokens, width + LANES)), whole((tokens, LANES))],
        [
            jax.ShapeDtypeStruct((tokens, width), f32),
            jax.ShapeDtypeStruct((tokens, width + LANES), bf16),
            jax.ShapeDtypeStruct((tokens, LANES), f32),
        ],
        prefetch=1,
        flops=2 * tokens * width * o.shape[1],
        moved=2 * width * o.shape[1] + 10 * tokens * width,
    )(offsets, o, x, gain, router, routes, *[p for p, _ in pieces])


def one_hot(slots_ref, j, rows):
    tokens = slots_ref.shape[1]
    slot = lax.broadcasted_iota(jnp.int32, (rows, tokens), 0)
    return jnp.where(slot == slots_ref[j : j + 1, :], 1.0, 0.0).astype(bf16)


def select_kernel(order, slots_ref, block_ref, own_ref, near_ref, chips_ref):
    rows = own_ref.shape[0]
    picks = jnp.concatenate([one_hot(slots_ref.at[0], j, rows) for j in range(PLANE)], axis=0)
    chosen = dot(picks, block_ref[...]).astype(bf16)
    own_ref[...] = chosen[:rows]
    near_ref[...] = chosen[rows : 2 * rows]
    chips_ref[0] = chosen[2 * rows : 3 * rows]
    chips_ref[1] = chosen[3 * rows :]


def select(slots, blocks, order, rows):
    count, _, tokens = slots.shape
    width = blocks.shape[1]
    shapes = [(count * rows, width), (count * rows, width), (2, count * rows, width)]
    return call(
        select_kernel,
        (count,),
        [
            pl.BlockSpec((1, PLANE, tokens), lambda k, order: (k, 0, 0)),
            pl.BlockSpec((tokens, width), lambda k, order: (order[k], 0)),
        ],
        [
            pl.BlockSpec((rows, width), lambda k, order: (k, 0)),
            pl.BlockSpec((rows, width), lambda k, order: (k, 0)),
            pl.BlockSpec((2, rows, width), lambda k, order: (0, k, 0)),
        ],
        [jax.ShapeDtypeStruct(shape, bf16) for shape in shapes],
        prefetch=1,
        flops=2 * count * PLANE * rows * tokens * width,
        moved=2 * count * (PLANE * rows + tokens) * width,
    )(order, slots, blocks)


def piece_specs(rows, width):
    first = pl.BlockSpec((1, rows, width), lambda *_: (0, 0, 0))
    second = pl.BlockSpec((1, rows, width), lambda *_: (1, 0, 0))
    return [whole((rows, width)), first, first, second]


def piece_rows(refs):
    return [ref[0] if len(ref.shape) == 3 else ref[...] for ref in refs]


def combine_kernel(slots_ref, *refs):
    parts, rest = refs[:PLANE], refs[PLANE:]
    out = rest[-1]
    rows = parts[0].shape[0]
    picks = jnp.concatenate([one_hot(slots_ref, j, rows) for j in range(PLANE)], axis=0)
    total = dot_tn(picks, jnp.concatenate(piece_rows(parts), axis=0))
    if len(rest) > 1:
        total = total + rest[0][...].astype(f32)
    out[...] = total.astype(out.dtype)


def combine(slots, parts, rows, before, dtype):
    tokens = slots.shape[1]
    width = parts[0].shape[1]
    extra = [] if before is None else [before]
    return call(
        combine_kernel,
        (1,),
        [whole(slots.shape)] + piece_specs(rows, width) + [whole((tokens, width))] * len(extra),
        whole((tokens, width)),
        jax.ShapeDtypeStruct((tokens, width), dtype),
        flops=2 * PLANE * rows * tokens * width,
        moved=2 * (PLANE * rows + 3 * tokens) * width,
    )(slots, *parts, *extra)


def expert_kernel(experts, counts, at, *refs):
    xs, cs = refs[:PLANE], refs[PLANE : 2 * PLANE]
    groups, used = [], 2 * PLANE
    for axis, count in zip((0, 0, 1), counts):
        group = refs[used : used + count]
        starts = [pl.multiple_of(at[1 + used - 2 * PLANE + n], LANES) for n in range(count)]
        groups.append([(pl.ds(start, w.shape[axis]), w) for start, w in zip(starts, group)])
        used += count
    wgs, wus, wds = groups
    y_acc, d_acc, gate_ref = refs[-3:]
    outs = refs[-3 - 2 * PIECES - 5 : -3]
    drows, ys = outs[:PIECES], outs[PIECES : 2 * PIECES]
    x_ref, dy_ref, a_ref, dg_ref, du_ref = outs[2 * PIECES :]
    xs = [ref.at[0] if len(ref.shape) == 3 else ref for ref in xs]
    cs = [ref.at[0] if len(ref.shape) == 3 else ref for ref in cs]
    drows = [drows[0], drows[1], drows[2].at[0], drows[2].at[1]]
    ys = [ys[0], ys[1], ys[2].at[0], ys[2].at[1]]
    step = pl.program_id(0)
    expert = at[0]
    rows = xs[0].shape[0]
    width = x_ref.shape[1]
    lane = lax.broadcasted_iota(jnp.int32, (rows, LANES), 1)

    @pl.when(step == 0)
    def _():
        for j in range(PLANE):
            span = slice(j * rows, (j + 1) * rows)
            x_ref[span, :] = xs[j][:, :width]
            tail = xs[j][:, width:].astype(f32)
            mine = (lane == expert) | (lane == expert + experts)
            gate = jnp.sum(jnp.where(mine, tail, 0.0), axis=1, keepdims=True)
            gate_ref[span, :] = jnp.broadcast_to(gate, (rows, LANES))
            dy_ref[span, :] = (gate * cs[j][...].astype(f32)).astype(bf16)

    def total(values):
        return functools.reduce(lambda a, b: a + b, values)

    g = total([dot(x_ref[:, span], w[...]) for span, w in wgs])
    u = total([dot(x_ref[:, span], w[...]) for span, w in wus])
    sigma = 1.0 / (1.0 + jnp.exp(-g))
    swish = g * sigma
    a = (swish * u).astype(bf16)
    da = total([dot_nt(dy_ref[:, span], w[...]) for span, w in wds])
    dg = (da * u * sigma * (1.0 + g * (1.0 - sigma))).astype(bf16)
    du = (da * swish).astype(bf16)
    a_ref[...] = a
    dg_ref[...] = dg
    du_ref[...] = du
    first = step == 0
    for span, w in wds:
        y = dot(a, w[...])
        y_acc[:, span] = jnp.where(first, y, y_acc[:, span] + y)
    for span, w in wgs:
        d = dot_nt(dg, w[...])
        d_acc[:, span] = jnp.where(first, d, d_acc[:, span] + d)
    for span, w in wus:
        d_acc[:, span] += dot_nt(du, w[...])

    @pl.when(step == pl.num_programs(0) - 1)
    def _():
        for j in range(PLANE):
            span = slice(j * rows, (j + 1) * rows)
            yj = y_acc[span, :].astype(bf16).astype(f32)
            ys[j][...] = (gate_ref[span, 0:1] * yj).astype(bf16)
            dgate = jnp.sum(cs[j][...].astype(f32) * yj, axis=1, keepdims=True)
            high = dgate.astype(bf16).astype(f32)
            tail = jnp.where(lane == expert, high, 0.0) + jnp.where(lane == expert + experts, dgate - high, 0.0)
            drows[j][:, :width] = d_acc[span, :].astype(bf16)
            drows[j][:, width:] = tail.astype(bf16)


def halves_kernel(order, x_ref, y_ref, own_ref, away_ref):
    part = dot_tn(x_ref[...], y_ref[...])

    @pl.when(pl.program_id(0) == 0)
    def _():
        own_ref[...] = part

    @pl.when(pl.program_id(0) == 1)
    def _():
        away_ref[...] = part.astype(bf16)


def grad_halves(order, x, y, cut_y):
    rows = x.shape[0]
    wide = (rows, (y if cut_y else x).shape[1] // 2)
    cut = pl.BlockSpec(wide, lambda i, order: (0, order[i]))
    shape = (x.shape[1], wide[1]) if cut_y else (wide[1], y.shape[1])
    return call(
        halves_kernel,
        (2,),
        [whole(x.shape), cut] if cut_y else [cut, whole(y.shape)],
        [whole(shape), whole(shape)],
        [jax.ShapeDtypeStruct(shape, f32), jax.ShapeDtypeStruct(shape, bf16)],
        prefetch=1,
        flops=2 * rows * x.shape[1] * y.shape[1],
        moved=2 * rows * (x.shape[1] + y.shape[1]) + 6 * shape[0] * shape[1],
        vmem=60,
    )(order, x, y)


def run_expert(index, part, parts, rows, experts, xs, cs, gates, ups, downs, kept):
    width = cs[0].shape[1]
    weights = gates + ups + downs
    hidden = gates[0][0].shape[1]
    tile = 256
    total = PLANE * rows
    at = jnp.stack([index] + [jnp.asarray(w[3]) for w in weights]).astype(jnp.int32)
    kept = [] if kept is None else list(kept)
    big = [width, width, hidden, hidden, hidden]
    shapes = [(rows, wide) if n < 2 else (2, rows, wide) for wide in (width + LANES, width) for n in range(PIECES)]

    return call(
        functools.partial(expert_kernel, experts, (len(gates), len(ups), len(downs))),
        (hidden // tile,),
        piece_specs(rows, width + LANES)
        + piece_specs(rows, width)
        + [pl.BlockSpec((w[1], tile), lambda i, *_, block=w[2]: (block, i)) for w in gates + ups]
        + [pl.BlockSpec((tile, w[1]), lambda i, *_, block=w[2]: (i, block)) for w in downs]
        + [pl.BlockSpec(memory_space=pl.ANY)] * len(kept),
        [whole(shape) for shape in shapes]
        + [pl.BlockSpec((total, width), lambda i, *_: (part, 0))] * 2
        + [pl.BlockSpec((total, tile), lambda i, *_: (part, i))] * 3,
        [jax.ShapeDtypeStruct(shape, bf16) for shape in shapes]
        + [jax.ShapeDtypeStruct((parts * total, n), bf16) for n in big],
        scratch=[pltpu.VMEM((total, width), f32), pltpu.VMEM((total, width), f32), pltpu.VMEM((total, LANES), f32)],
        prefetch=1,
        flops=12 * total * width * hidden,
        moved=6 * width * hidden + 16 * total * width,
        vmem=60,
        aliases={1 + 2 * PLANE + len(weights) + n: 2 * PIECES + n for n in range(len(kept))},
    )(at, *xs, *cs, *[w[0] for w in weights], *kept)


def fence(*values):
    leaves, tree = jax.tree.flatten(values)
    arrays = [n for n, leaf in enumerate(leaves) if isinstance(leaf, jax.Array)]
    for n, leaf in zip(arrays, lax.optimization_barrier([leaves[n] for n in arrays])):
        leaves[n] = leaf
    return jax.tree.unflatten(tree, leaves)


def after(value, *others):
    return fence(value, *others)[0]


def rope_tables(position):
    half_width = HEAD_DIM // 2
    frequency = ROPE_BASE ** (-jnp.arange(half_width, dtype=f32) / half_width)
    angle = position.astype(f32)[:, None] * frequency[None, :]
    cosine, sine = jnp.cos(angle), jnp.sin(angle)
    return jnp.concatenate([cosine, cosine], axis=1), jnp.concatenate([-sine, sine], axis=1)


def on_device(
    copies,
    experts,
    tokens,
    cotangent,
    segment_ids,
    padding,
    routes,
    placement_order,
    norm_attn,
    w_query,
    w_key,
    w_value,
    w_out,
    norm_ffn,
    w_router,
    w_gate,
    w_up,
    w_down,
):
    planes = experts // PLANE
    paired = copies == 2
    d = lax.axis_index("dp")
    e = lax.axis_index("expert")
    z, q = e // PLANE, lax.rem(e, PLANE)
    core = lax.rem(e, 2)

    def swap(value):
        return lax.ppermute(value, "dp", [(0, 1), (1, 0)])

    def across(value, j):
        return lax.ppermute(value, "expert", [(i, i ^ j) for i in range(experts)])

    def ahead(value):
        return lax.ppermute(value, "expert", [(i, (i + PLANE) % experts) for i in range(experts)])

    def join(own, other, index, axis):
        first = jnp.where(index == 0, own, other)
        second = jnp.where(index == 0, other, own)
        return jnp.concatenate([first, second], axis=axis)

    def gather(own, axis):
        if paired:
            return join(own, swap(own), d, axis)
        return lax.all_gather(own, "dp", axis=axis, tiled=True)

    def half_rows(own):
        half = own.shape[0] // 2
        return lax.dynamic_slice_in_dim(own, core * half, half, 0)

    def assemble(pieces):
        if len(pieces) == 1:
            return pieces[0]
        own, got, twin = pieces
        return join(own, join(got, twin, core, 0), d, 0)

    def z_send(value, s):
        return lax.ppermute(value, "expert", [(i, (i + s * PLANE) % experts) for i in range(experts)])

    x = tokens[0]
    cot = cotangent[0]
    tok_count, width = x.shape
    position = d * tok_count + jnp.arange(tok_count, dtype=jnp.int32)
    kv_width = KV_HEADS * HEAD_DIM
    q_width = HEADS * HEAD_DIM

    capacity = tok_count * TOP * 9 // (8 * experts)
    rows = (capacity + 15) // 16 * 16
    far = tok_count * TOP
    wishes = jnp.concatenate([routes[0].T, placement_order[0].T], axis=0)
    if paired:
        size = w_query.shape[0]
        got_half = jnp.concatenate([half_rows(w_query), half_rows(w_key), half_rows(w_value)], axis=1)
        small_own = jnp.concatenate([norm_attn[None], norm_ffn[None], w_router.T], axis=0)
        own_info = jnp.where(padding[0] == 1, segment_ids[0], -1)[None]
        first_own = jnp.concatenate(
            [small_own, jnp.pad(own_info.astype(bf16), ((0, 0), (0, size - tok_count)))], axis=0
        )
        first_rows = first_own.shape[0]
        first_own = jnp.pad(first_own, ((0, -first_rows % 16), (0, got_half.shape[1] - size)))
        wishes, got_half = fence(wishes, jnp.concatenate([got_half, first_own], axis=0))
    ring_wishes = jnp.stack([wishes] + [z_send(wishes, k) for k in range(1, planes)])
    near = jnp.stack([z * PLANE + (q ^ j) for j in range(PLANE)]).astype(jnp.int32)
    hits = ring_wishes[:, None, :TOP] == near[None, :, None, None]
    order = jnp.min(jnp.where(hits, ring_wishes[:, None, TOP:], far), axis=2)
    rank = jnp.sum((order[:, :, None, :] < order[:, :, :, None]).astype(jnp.int32), axis=3)
    slots = jnp.where((order < far) & (rank < capacity), rank, -1)

    qkv_own = jnp.concatenate([w_query, w_key, w_value], axis=1)
    cosine, sine = rope_tables(position)
    if paired:
        start = (1 - d) * size
        offsets = jnp.stack([d * size, start + core * size // 2, start + (1 - core) * size // 2]).astype(jnp.int32)
        cut = size // 6 // LANES * LANES
        cut_offsets = [d * size]
        for begin in (0, cut):
            cut_offsets += [start + core * size // 2 + begin, start + (1 - core) * size // 2 + begin]
        cut_offsets = jnp.stack(cut_offsets).astype(jnp.int32)
        got = swap(got_half)
        cot_one = ahead(cot)
        out_half = half_rows(w_out)
        out_late, out_got = out_half[:cut], out_half[cut:]
        first_other = got[size // 2 : size // 2 + first_rows, :size]
        small = join(small_own, first_other[:-1], d, 1)
        info = jnp.concatenate([own_info, first_other[-1:, :tok_count].astype(jnp.int32)], axis=1)
        other_position = (1 - d) * tok_count + jnp.arange(tok_count, dtype=jnp.int32)
        key_place = jnp.concatenate([position, other_position])[None]
    else:
        small = gather(jnp.concatenate([norm_attn[None], norm_ffn[None], w_router.T], axis=0), 1)
        cot_one = ahead(cot)
        offsets = cut_offsets = jnp.zeros((1,), jnp.int32)
        out_late = out_got = ()
        got = lax.all_gather(qkv_own, "dp", axis=0, tiled=True)
        own_info = jnp.where(padding[0] == 1, segment_ids[0], -1)[None]
        info = lax.all_gather(own_info, "dp", axis=1, tiled=True)
        key_place = jnp.arange(copies * tok_count, dtype=jnp.int32)[None]
    gain_one = small[0:1].astype(f32)
    gain_two = small[1:2].astype(f32)
    router_rows = jnp.pad(small[2:], ((0, LANES - experts), (0, 0)))
    small = small[2:]
    segment, place = segment_ids[0][:, None], position[:, None]
    allowed = (key_place <= place) & (info == segment) | (key_place == place)
    bias = jnp.where(allowed, 0.0, MASKED)

    def exchange(own, near_by, chips):
        return own, near_by, across(chips, 2)

    def relay(parts):
        own, near_by, landed = parts
        near_by = across(jnp.concatenate([near_by[None], landed[1:]], axis=0), 1)
        return [own, near_by, landed, near_by]

    first = jnp.zeros((1,), jnp.int32)

    def hand_out(k, block):
        return exchange(*select(slots[k : k + 1], block, first, rows))

    cots = {0: hand_out(0, cot)}
    expert_own = [w_gate[0], w_up[0], w_down[0]]
    got, slots, qkv_own, out_late, out_got, cosine, sine, cots[0], cut_offsets = fence(
        got, slots, qkv_own, out_late, out_got, cosine, sine, cots[0], cut_offsets
    )
    cot_two = ahead(cot_one)
    if paired:
        qkv_pieces = [(qkv_own, size), (got, size // 2), (across(got, 1), size // 2)]
        out_got = swap(out_got)
    else:
        qkv_pieces = [(got, width)]
        out_got = lax.all_gather(w_out, "dp", axis=0, tiled=True)
    qkv, hidden_one = project_qkv(x, gain_one, cosine, sine, offsets, qkv_pieces)

    own_kv = qkv[:, q_width:]
    bias, gain_two, router_rows, small = after((bias, gain_two, router_rows, small), own_kv)
    cots[0] = relay(after(cots[0], own_kv))
    cots[1] = select(slots[1:2], after(cot_one, own_kv), first, rows)
    if paired:
        keys_values = jnp.concatenate([own_kv, swap(own_kv)], axis=0)
    else:
        keys_values = lax.all_gather(own_kv, "dp", axis=0, tiled=True)
    keys_values, out_got, cots[0], cots[1], bias, gain_two, router_rows, small, cot_two = fence(
        keys_values, out_got, cots[0], cots[1], bias, gain_two, router_rows, small, cot_two
    )
    ring_cot = [cot, cot_one, cot_two]
    for _ in range(3, planes):
        ring_cot.append(ahead(ring_cot[-1]))
    if paired:
        out_late = swap(after(out_late, keys_values))
        out_pieces = [(out_got, size // 2 - cut), (across(out_got, 1), size // 2 - cut)]
        gate_first = swap(after(expert_own[0][: size // 2], keys_values))
    else:
        out_pieces = [(out_got, q_width)]
    cots[1] = exchange(*cots[1])
    attended, probs = attend(qkv, keys_values, bias)
    if paired:
        out_late = after(out_late, attended)
        out_pieces = [(w_out, size), (out_late, cut), (across(out_late, 1), cut)] + out_pieces

    middle, payload, gates = project_out(
        attended, x, gain_two, router_rows, routes[0], cut_offsets, out_pieces, experts
    )
    if paired:
        payload, gate_first, ring_cot, cots[1] = fence(payload, gate_first, ring_cot, cots[1])
        gate_up = swap(after(jnp.concatenate([expert_own[0][size // 2 :], expert_own[1]], axis=0), payload))

    ring = [payload, ahead(payload)]
    xs, drows, ys, kept = {}, {}, {}, None
    turns = list(range(1, planes)) + [0]

    def work(k, kept):
        outs = run_expert(e, k, planes, rows, experts, xs[k], cots[k], *expert_weights, kept)
        drows[k] = outs[:PIECES]
        ys[k] = outs[PIECES : 2 * PIECES]
        return outs[2 * PIECES :]

    def give_back(k, before, dtype):
        return combine(slots[k], drows[k], rows, before, dtype)

    def mix(k, before, dtype):
        return combine(slots[k], ys[k], rows, before, dtype)

    cots[1] = relay(after(cots[1], payload))
    for k in range(2, planes):
        cots[k] = hand_out(k, after(ring_cot[k], payload))
    if paired:
        ring[1], gate_up, cots = fence(ring[1], gate_up, cots)
        down = swap(after(expert_own[2], ring[1]))
        other = (1 - d) * size
        expert_weights = [
            [(expert_own[0], size, 0, d * size), (gate_first, size // 2, 0, other), (gate_up, size // 2, 0, other + size // 2)],
            [(expert_own[1], size, 0, d * size), (gate_up, size // 2, 1, other), (gate_up, size // 2, 2, other + size // 2)],
            [(expert_own[2], size, 0, d * size), (down, size, 0, other)],
        ]
        ring.append(ahead(ring[1]))
        xs[1] = hand_out(1, ring[1])
        ring[2], xs[1], cots, expert_weights = fence(ring[2], xs[1], cots, expert_weights)
        ring.append(ahead(ring[2]))
        xs[1] = relay(xs[1])
        cots[2], cots[3] = relay(cots[2]), relay(cots[3])
        xs[2] = select(slots[2:3], ring[2], first, rows)
        xs[1], xs[2] = fence(xs[1], xs[2])
        xs[2] = exchange(*xs[2])
        kept = work(1, kept)
        drows[1], kept = fence(drows[1], kept)
        drows[1] = exchange(*drows[1])
        xs[2], kept = fence(xs[2], kept)
        xs[2] = relay(xs[2])
        kept = work(2, kept)
        drows[1], drows[2], kept, ring[3] = fence(drows[1], drows[2], kept, ring[3])
        drows[1] = relay(drows[1])
        back = give_back(1, None, bf16)
        back, drows[2] = fence(back, drows[2])
        back = ahead(back)
        drows[2] = exchange(*drows[2])
        xs[3] = select(slots[3:4], ring[3], first, rows)
        xs[0] = select(slots[:1], after(payload, ring[3]), first, rows)
        xs[3], xs[0], drows[2], kept = fence(xs[3], xs[0], drows[2], kept)
        xs[3] = exchange(*xs[3])
        drows[2] = relay(drows[2])
        back, drows[2] = fence(back, drows[2])
        back = give_back(2, back, bf16)
        back, kept = fence(back, kept)
        back = ahead(back)
        xs[3] = fence(xs[3], kept)[0]
        xs[0] = exchange(*after(xs[0], xs[3]))
        xs[3] = relay(xs[3])
        kept = work(3, kept)
        drows[3], xs[0], kept = fence(drows[3], xs[0], kept)
        drows[3] = exchange(*drows[3])
        xs[0] = relay(xs[0])
        kept = work(0, kept)
        drows[0], drows[3], kept, back = fence(drows[0], drows[3], kept, back)
        drows[3] = relay(drows[3])
        back = give_back(3, back, bf16)

        back, drows[0], kept, ys = fence(back, drows[0], kept, ys)
        back = ahead(back)
        drows[0] = exchange(*drows[0])
        ys[1] = exchange(*ys[1])
    else:
        expert_weights = [
            [(lax.all_gather(w, "dp", axis=axis, tiled=True), width, 0, 0)]
            for w, axis in zip(expert_own, (0, 0, 1))
        ]
        for k in range(2, planes):
            cots[k] = relay(cots[k])
            ring.append(ahead(ring[-1]))
        back = None
        for k in turns:
            xs[k] = relay(hand_out(k, ring[k]))
            kept = work(k, kept)
            drows[k] = relay(exchange(*drows[k]))
            if k > 0:
                back = ahead(give_back(k, back, bf16))

    row_all, dy_all, a_all, dg_all, du_all = kept
    if paired:
        halves = jnp.stack([d, 1 - d]).astype(jnp.int32)
        keep_gate, away_gate = grad_halves(halves, row_all, dg_all, False)
        keep_up, away_up = grad_halves(halves, row_all, du_all, False)
        keep_down, away_down = grad_halves(halves, a_all, dy_all, True)
        drows[0], ys, away_gate, away_up, away_down, back = fence(
            drows[0], ys, away_gate, away_up, away_down, back
        )
        drows[0] = relay(drows[0])
        back, drows[0] = fence(back, drows[0])
        ys[1] = relay(ys[1])
        back = give_back(0, back, f32)
        mixture = ahead(mix(1, None, bf16))
        middle_row = away_up.shape[0] // 2
        arrived_gate = swap(after(away_gate, back))
        arrived_up = []
        ys[2], ys[3] = exchange(*after(ys[2], back)), exchange(*after(ys[3], back))
    else:
        grad_gate, grad_up, grad_down = [
            lax.psum_scatter(full.astype(bf16), "dp", scatter_dimension=axis, tiled=True).astype(f32)[None]
            for full, axis in (
                (dot_tn(row_all, dg_all), 0),
                (dot_tn(row_all, du_all), 0),
                (dot_tn(a_all, dy_all), 1),
            )
        ]
        back = give_back(0, back, f32)

    upstream = cot.astype(f32)
    gates = gates[:, :experts]
    dgates = back[:, width : width + experts] + back[:, width + experts : width + 2 * experts]
    dlogits = (gates * (dgates - jnp.sum(gates * dgates, axis=1, keepdims=True))).astype(bf16)
    hidden_two = payload[:, :width]
    dh2 = back[:, :width] + dot(dlogits, small)
    scale_two = lax.rsqrt(jnp.mean(middle * middle, axis=1, keepdims=True) + EPSILON)
    normed_two = middle * scale_two
    e2 = dh2 * gain_two
    dmiddle = upstream + scale_two * (e2 - normed_two * jnp.mean(e2 * normed_two, axis=1, keepdims=True))
    dmb = dmiddle.astype(bf16)
    half_index = jnp.stack([core if paired else 0]).astype(jnp.int32)
    do = project_back(dmb, cut_offsets, out_pieces, bf16)
    grad_out = weight_grad(half_index, attended, dmb)

    other_chip = lax.rem(q // 2, 2)

    def add(*values):
        return functools.reduce(lambda a, b: a + b, [v.astype(f32) for v in values]).astype(bf16)

    def pick(value, index, axis=0):
        return lax.dynamic_index_in_dim(value, index, axis, keepdims=False)

    def halve(parts, index, send, axis=0):
        parts = [p.reshape(p.shape[:axis] + (2, -1, p.shape[-1])) for p in parts]
        away = add(*[pick(p, 1 - index, axis) for p in parts])
        return [pick(p, index, axis) for p in parts] + [send(away)]

    def over(j):
        return lambda value: across(value, j)

    def cut_core(parts):
        return [parts[0], across(parts[1], 1)]

    def both(part, j):
        return part, across(part, j)

    def sum_all(keep, away):
        both = jnp.concatenate([keep, away], axis=1).reshape(-1, keep.shape[2])
        part = lax.psum_scatter(both, "dp", scatter_dimension=0, tiled=True)
        return lax.psum(part, "expert").astype(f32)

    def unrotate(value):
        turned = jnp.concatenate([value[:, HEAD_DIM // 2 :], value[:, : HEAD_DIM // 2]], axis=1)
        return value * cosine - turned * sine

    dqp, dk, dv = attend_back(probs, do, qkv, keys_values, cosine, sine)
    dkv = jnp.concatenate([dk, dv], axis=1)
    input_tokens = x.astype(f32)
    scale_one = lax.rsqrt(jnp.mean(input_tokens * input_tokens, axis=1, keepdims=True) + EPSILON)
    normed_one = input_tokens * scale_one
    grad_norm_ffn_local = jnp.sum(dh2 * normed_two, axis=0)
    grad_router_local = lax.dot_general(dlogits, hidden_two, (((0,), (0,)), ((), ())), preferred_element_type=f32)

    def unrotated(dkv):
        dkp = [unrotate(dkv[:, n * HEAD_DIM : (n + 1) * HEAD_DIM]) for n in range(KV_HEADS)]
        dkvp = jnp.concatenate([v.astype(bf16) for v in dkp] + [dkv[:, kv_width:].astype(bf16)], axis=1)
        return jnp.concatenate([dqp, dkvp], axis=1)

    def through_projections(dqkv):
        dh1 = project_back(dqkv, offsets, qkv_pieces, f32)
        grad_norm_attn_local = jnp.sum(dh1 * normed_one, axis=0)
        extra = jnp.concatenate(
            [grad_norm_attn_local[None], grad_norm_ffn_local[None], grad_router_local], axis=0
        )
        extra = extra.astype(bf16)
        e1 = dh1 * gain_one
        grad_inputs = dmiddle + scale_one * (
            e1 - normed_one * jnp.mean(e1 * normed_one, axis=1, keepdims=True)
        )
        return extra, grad_inputs

    if paired:
        low, high = lax.rem(z, 2), z // 2
        away_dkv = dkv[tok_count:].astype(bf16)
        away_dkv, dqp, ys, arrived_gate, mixture = fence(away_dkv, dqp, ys, arrived_gate, mixture)
        other_dkv = swap(away_dkv)
        ys[2] = relay(ys[2])
        sum_a = weight_grad(half_index, hidden_one, dqp)
        grad_out = weight_grad(half_index, after(attended, sum_a), dmb)
        sum_a, other_dkv, grad_out = fence(sum_a, other_dkv, grad_out)
        sum_a, sum_out = cut_core(sum_a), cut_core(grad_out)
        ys[3] = relay(ys[3])
        dqkv = unrotated(dkv[:tok_count] + other_dkv.astype(f32))
        sum_b = weight_grad(half_index, hidden_one, dqkv[:, q_width:])
        mixture = mix(2, mixture, bf16)
        sum_a, sum_out, sum_b, dqkv, ys, mixture = fence(sum_a, sum_out, sum_b, dqkv, ys, mixture)
        sum_a = halve(sum_a, d, swap)
        sum_out = halve(sum_out, other_chip, over(2), 1)
        sum_b = cut_core(sum_b)
        mixture = ahead(mixture)
        extra, grad_inputs = through_projections(dqkv)
        sum_a, sum_out, sum_b, mixture, extra = fence(sum_a, sum_out, sum_b, mixture, extra)
        sum_a = halve(sum_a, other_chip, over(2))
        sum_b = halve(sum_b, d, swap)
        sum_out = halve(sum_out, low, over(4), 1)
        extra = both(extra, 1)
        sum_a, sum_out, sum_b, extra = fence(sum_a, sum_out, sum_b, extra)
        sum_b = halve(sum_b, other_chip, over(2))
        sum_out = halve(sum_out, high, over(8), 1)
        extra = both(add(*extra), 2)
        arrived_up.append(swap(after(away_up[:middle_row], sum_a)))
        sum_a, sum_out, sum_b, arrived_up, extra = fence(sum_a, sum_out, sum_b, arrived_up, extra)
        sums = halve([jnp.concatenate([add(*sum_a), add(*sum_b)], axis=1)], low, over(4))
        sum_out = halve(sum_out, d, swap)
        arrived_up.append(swap(after(away_up[middle_row:], sum_a)))
        ys[0] = exchange(*after(ys[0], sum_a))
        extra = both(add(*extra), 4)
        sums, sum_out, arrived_up, ys[0], extra = fence(sums, sum_out, arrived_up, ys[0], extra)
        sums = halve(sums, high, over(8))
        sum_out = both(add(*sum_out).reshape(-1, width), 8)
        arrived_down = [swap(after(away_down[:middle_row], ys[0]))]
        extra = both(add(*extra), 8)
        sums, sum_out, arrived_down, extra = fence(sums, sum_out, arrived_down, extra)
        sums = both(add(*sums), 8)
        arrived_down.append(swap(after(away_down[middle_row:], sum_out)))
        ys[0] = relay(ys[0])
        sum_out = both(join(*sum_out, high, 0), 4)
        extra = add(*extra)
        extra = (extra, swap(extra))
        sums, sum_out, arrived_down, ys[0], extra = fence(sums, sum_out, arrived_down, ys[0], extra)
        sums = both(join(*sums, high, 0), 4)
        sum_out = both(join(*sum_out, low, 0), 2)
        mixture = mix(3, mixture, bf16)
        sums, sum_out, mixture = fence(sums, sum_out, mixture)
        sums = both(join(*sums, low, 0), 2)
        sum_out = both(join(*sum_out, other_chip, 0), 1)
        mixture = ahead(mixture)
        grad_gate = (keep_gate + arrived_gate.astype(f32))[None]
        grad_up = (keep_up + jnp.concatenate(arrived_up, axis=0).astype(f32))[None]
        grad_down = (keep_down + jnp.concatenate(arrived_down, axis=0).astype(f32))[None]
        sums, sum_out, grad_gate, grad_up, grad_down, mixture = fence(
            sums, sum_out, grad_gate, grad_up, grad_down, mixture
        )
        sums = both(join(*sums, other_chip, 0), 1)
        sum_out = join(*sum_out, core, 0).astype(f32)
        mixed = (middle + mix(0, mixture, f32)).astype(bf16)[None]
        sums, sum_out, mixed = fence(sums, sum_out, mixed)
        extra = lax.dynamic_slice_in_dim(add(*extra), d * size, size, 1).astype(f32)
        sum_q, sum_key, sum_value = [
            join(sums[0][:, cols], sums[1][:, cols], core, 0).astype(f32)
            for cols in [
                slice(0, q_width),
                slice(q_width, q_width + kv_width),
                slice(q_width + kv_width, q_width + 2 * kv_width),
            ]
        ]
    else:
        dkv = lax.psum_scatter(dkv.astype(bf16), "dp", scatter_dimension=0, tiled=True).astype(f32)
        dqkv = unrotated(dkv)
        extra, grad_inputs = through_projections(dqkv)
        sum_qkv = sum_all(*weight_grad(half_index, hidden_one, dqkv))
        sum_q, sum_key = sum_qkv[:, :q_width], sum_qkv[:, q_width : q_width + kv_width]
        sum_value = sum_qkv[:, q_width + kv_width :]
        sum_out = sum_all(*grad_out)
        extra = lax.psum_scatter(extra, "dp", scatter_dimension=1, tiled=True)
        extra = lax.psum(extra, "expert").astype(f32)
        ys = {k: relay(exchange(*y)) for k, y in ys.items()}
        mixture = None
        for k in turns[:-1]:
            mixture = ahead(mix(k, mixture, bf16))
        mixed = (middle + mix(0, mixture, f32)).astype(bf16)[None]
    return (
        mixed,
        grad_inputs[None],
        extra[0],
        sum_q,
        sum_key,
        sum_value,
        sum_out,
        extra[1],
        extra[2 : 2 + experts].T,
        grad_gate,
        grad_up,
        grad_down,
    )


def solution(mesh):
    rows = P("expert", "dp", None)
    return jax.shard_map(
        functools.partial(on_device, mesh.shape["dp"], mesh.shape["expert"]),
        mesh=mesh,
        in_specs=(
            rows,
            rows,
            P("expert", "dp"),
            P("expert", "dp"),
            rows,
            rows,
            P("dp"),
            P("dp", None),
            P("dp", None),
            P("dp", None),
            P("dp", None),
            P("dp"),
            P("dp", None),
            rows,
            rows,
            P("expert", None, "dp"),
        ),
        out_specs=(
            rows,
            rows,
            P("dp"),
            P("dp", None),
            P("dp", None),
            P("dp", None),
            P("dp", None),
            P("dp"),
            P("dp", None),
            rows,
            rows,
            P("expert", None, "dp"),
        ),
        check_vma=False,
    )
```

```python
import functools
import math

import jax
import jax.numpy as jnp
from jax import lax
from jax.experimental import pallas as pl
from jax.experimental.pallas import tpu as pltpu
from jax.sharding import PartitionSpec as P

HEADS = 12
KV_HEADS = 2
HEAD_DIM = 128
TOP = 4
GROUP = HEADS // KV_HEADS
PLANE = 4
LANES = 128
PIECES = 3

EPSILON = 1e-06
ROPE_BASE = 1000000.0
MASKED = -1e30
MIB = 1024 * 1024

f32 = jnp.float32
bf16 = jnp.bfloat16


def dot(a, b):
    return jnp.dot(a, b, preferred_element_type=f32)


def dot_nt(a, b):
    return lax.dot_general(a, b, (((1,), (1,)), ((), ())), preferred_element_type=f32)


def dot_tn(a, b):
    return lax.dot_general(a, b, (((0,), (0,)), ((), ())), preferred_element_type=f32)


def whole(shape):
    return pl.BlockSpec(shape, lambda *_: (0,) * len(shape))


def call(kernel, grid, in_specs, out_specs, out_shape, scratch=(), prefetch=0, flops=0, moved=0, vmem=20, aliases=None):
    return pl.pallas_call(
        kernel,
        grid_spec=pltpu.PrefetchScalarGridSpec(
            num_scalar_prefetch=prefetch,
            grid=grid,
            in_specs=in_specs,
            out_specs=out_specs,
            scratch_shapes=list(scratch),
        ),
        out_shape=out_shape,
        input_output_aliases=aliases or {},
        cost_estimate=pl.CostEstimate(flops=flops // 64, bytes_accessed=moved // 64, transcendentals=0),
        compiler_params=pltpu.CompilerParams(
            dimension_semantics=("arbitrary",) * len(grid), vmem_limit_bytes=vmem * MIB
        ),
    )


def qkv_kernel(offsets, x_ref, gain_ref, cos_ref, sin_ref, *refs):
    pieces, (out_ref, h_ref) = refs[:-2], refs[-2:]
    step = pl.program_id(0)

    @pl.when(step == 0)
    def _():
        x = x_ref[...].astype(f32)
        r = lax.rsqrt(jnp.mean(x * x, axis=1, keepdims=True) + EPSILON)
        h_ref[...] = (x * r * gain_ref[...]).astype(bf16)

    acc = None
    for n, w_ref in enumerate(pieces):
        rows = w_ref.shape[0]
        start = pl.multiple_of(offsets[n], LANES)
        part = dot(h_ref[:, pl.ds(start, rows)], w_ref[...])
        acc = part if acc is None else acc + part

    rotary = step * out_ref.shape[1] < (HEADS + KV_HEADS) * HEAD_DIM

    @pl.when(rotary)
    def _():
        for n in range(out_ref.shape[1] // HEAD_DIM):
            a = acc[:, n * HEAD_DIM : (n + 1) * HEAD_DIM]
            turned = a * cos_ref[...] + pltpu.roll(a, HEAD_DIM // 2, 1) * sin_ref[...]
            out_ref[:, n * HEAD_DIM : (n + 1) * HEAD_DIM] = turned.astype(bf16)

    @pl.when(jnp.logical_not(rotary))
    def _():
        out_ref[...] = acc.astype(bf16)


def project_qkv(x, gain, cosine, sine, offsets, pieces):
    tokens, width = x.shape
    columns = pieces[0][0].shape[1]
    tile = 256
    return call(
        qkv_kernel,
        (columns // tile,),
        [whole(x.shape), whole(gain.shape), whole(cosine.shape), whole(sine.shape)]
        + [pl.BlockSpec((n, tile), lambda i, *_: (0, i)) for _, n in pieces],
        [pl.BlockSpec((tokens, tile), lambda i, *_: (0, i)), whole(x.shape)],
        [jax.ShapeDtypeStruct((tokens, columns), bf16), jax.ShapeDtypeStruct(x.shape, bf16)],
        prefetch=1,
        flops=2 * tokens * width * columns,
        moved=2 * width * columns + 4 * tokens * columns,
    )(offsets, x, gain, cosine, sine, *[p for p, _ in pieces])


def back_kernel(offsets, x_ref, *refs):
    pieces, (out_ref, acc_ref) = refs[:-2], refs[-2:]
    step = pl.program_id(0)
    for n, w_ref in enumerate(pieces):
        rows = w_ref.shape[0]
        span = pl.ds(pl.multiple_of(offsets[n], LANES), rows)
        part = dot_nt(x_ref[...], w_ref[...])
        acc_ref[:, span] = jnp.where(step == 0, part, acc_ref[:, span] + part)

    @pl.when(step == pl.num_programs(0) - 1)
    def _():
        out_ref[...] = acc_ref[...].astype(out_ref.dtype)


def project_back(x, offsets, pieces, dtype):
    tokens, columns = x.shape
    width = sum(n for _, n in pieces)
    tile = 512
    return call(
        back_kernel,
        (columns // tile,),
        [pl.BlockSpec((tokens, tile), lambda i, *_: (0, i))]
        + [pl.BlockSpec((n, tile), lambda i, *_: (0, i)) for _, n in pieces],
        whole((tokens, width)),
        jax.ShapeDtypeStruct((tokens, width), dtype),
        scratch=[pltpu.VMEM((tokens, width), f32)],
        prefetch=1,
        flops=2 * tokens * width * columns,
        moved=2 * width * columns + 6 * tokens * columns,
    )(offsets, x, *[p for p, _ in pieces])


def weight_grad_kernel(core, x_ref, y_ref, keep_ref, away_ref):
    rows = keep_ref.shape[1]
    for n, out_ref in enumerate((keep_ref, away_ref)):
        part = core[0] if n == 0 else 1 - core[0]
        start = pl.multiple_of(part * rows, LANES)
        out_ref[0] = dot_tn(x_ref[:, pl.ds(start, rows)], y_ref[...]).astype(bf16)


def weight_grad(core, x, y, block=0, blocks=1):
    tokens, width = x.shape
    columns = y.shape[1] // blocks
    half = width // 2
    shape = (2, half // 2, columns)
    return call(
        weight_grad_kernel,
        (2,),
        [
            pl.BlockSpec((tokens, half), lambda i, *_: (0, i)),
            pl.BlockSpec((tokens, columns), lambda i, *_: (0, block)),
        ],
        [pl.BlockSpec((1,) + shape[1:], lambda i, *_: (i, 0, 0))] * 2,
        [jax.ShapeDtypeStruct(shape, bf16)] * 2,
        prefetch=1,
        flops=2 * tokens * width * columns,
        moved=4 * width * columns,
    )(core, x, y)


def attend_kernel(q_ref, k_ref, v_ref, bias_ref, o_ref, p_ref):
    scores = dot_nt(q_ref[...], k_ref[...]) * (math.log2(math.e) / math.sqrt(HEAD_DIM)) + bias_ref[...]
    peak = jnp.max(scores, axis=1, keepdims=True)
    exps = jnp.exp2(scores - peak)
    probs = (exps * (1.0 / jnp.sum(exps, axis=1, keepdims=True))).astype(bf16)
    p_ref[0] = probs
    o_ref[...] = dot(probs, v_ref[...]).astype(bf16)


def attend(qkv, keys_values, bias):
    tokens = qkv.shape[0]
    keys = keys_values.shape[0]
    return call(
        attend_kernel,
        (HEADS,),
        [
            pl.BlockSpec((tokens, HEAD_DIM), lambda h: (0, h)),
            pl.BlockSpec((keys, HEAD_DIM), lambda h: (0, h // GROUP)),
            pl.BlockSpec((keys, HEAD_DIM), lambda h: (0, KV_HEADS + h // GROUP)),
            whole(bias.shape),
        ],
        [
            pl.BlockSpec((tokens, HEAD_DIM), lambda h: (0, h)),
            pl.BlockSpec((1, tokens, keys), lambda h: (h, 0, 0)),
        ],
        [
            jax.ShapeDtypeStruct((tokens, HEADS * HEAD_DIM), bf16),
            jax.ShapeDtypeStruct((HEADS, tokens, keys), bf16),
        ],
        flops=4 * HEADS * tokens * keys * HEAD_DIM,
        moved=2 * HEADS * tokens * keys,
        vmem=20 * max(1, keys // 1024),
    )(qkv, keys_values, keys_values, bias)


def attend_back_kernel(p_ref, do_ref, q_ref, k_ref, v_ref, cos_ref, sin_ref, dq_ref, dk_ref, dv_ref):
    scale = 1.0 / math.sqrt(HEAD_DIM)
    member = lax.rem(pl.program_id(0), GROUP)
    probs = p_ref[0]
    wide = probs.astype(f32)
    do = do_ref[...]
    grad_probs = dot_nt(do, v_ref[...])
    delta = jnp.sum(wide * grad_probs, axis=1, keepdims=True)
    grad_scores = (wide * (grad_probs - delta)).astype(bf16)
    dq = dot(grad_scores, k_ref[...]) * scale
    dq_ref[...] = (dq * cos_ref[...] - pltpu.roll(dq, HEAD_DIM // 2, 1) * sin_ref[...]).astype(bf16)
    dk = dot_tn(grad_scores, q_ref[...]) * scale
    dv = dot_tn(probs, do)

    @pl.when(member == 0)
    def _():
        dk_ref[...] = dk
        dv_ref[...] = dv

    @pl.when(member > 0)
    def _():
        dk_ref[...] += dk
        dv_ref[...] += dv


def attend_back(probs, do, qkv, keys_values, cosine, sine):
    tokens = qkv.shape[0]
    keys = keys_values.shape[0]
    kv_width = KV_HEADS * HEAD_DIM
    return call(
        attend_back_kernel,
        (HEADS,),
        [
            pl.BlockSpec((1, tokens, keys), lambda h: (h, 0, 0)),
            pl.BlockSpec((tokens, HEAD_DIM), lambda h: (0, h)),
            pl.BlockSpec((tokens, HEAD_DIM), lambda h: (0, h)),
            pl.BlockSpec((keys, HEAD_DIM), lambda h: (0, h // GROUP)),
            pl.BlockSpec((keys, HEAD_DIM), lambda h: (0, KV_HEADS + h // GROUP)),
            whole(cosine.shape),
            whole(sine.shape),
        ],
        [
            pl.BlockSpec((tokens, HEAD_DIM), lambda h: (0, h)),
            pl.BlockSpec((keys, HEAD_DIM), lambda h: (0, h // GROUP)),
            pl.BlockSpec((keys, HEAD_DIM), lambda h: (0, h // GROUP)),
        ],
        [
            jax.ShapeDtypeStruct((tokens, HEADS * HEAD_DIM), bf16),
            jax.ShapeDtypeStruct((keys, kv_width), f32),
            jax.ShapeDtypeStruct((keys, kv_width), f32),
        ],
        flops=8 * HEADS * tokens * keys * HEAD_DIM,
        moved=2 * HEADS * tokens * keys,
        vmem=20 * max(1, keys // 1024),
    )(probs, do, qkv, keys_values, keys_values, cosine, sine)


def middle_kernel(experts, offsets, o_ref, x_ref, gain_ref, router_ref, routes_ref, *refs):
    pieces, (middle_ref, payload_ref, gates_ref) = refs[:-3], refs[-3:]
    step = pl.program_id(0)
    tile = x_ref.shape[1]
    acc = x_ref[...].astype(f32)
    for n, w_ref in enumerate(pieces):
        start = pl.multiple_of(offsets[n], LANES)
        acc = acc + dot(o_ref[:, pl.ds(start, w_ref.shape[0])], w_ref[...])
    middle_ref[:, pl.ds(pl.multiple_of(step * tile, tile), tile)] = acc

    @pl.when(step == pl.num_programs(0) - 1)
    def _():
        middle = middle_ref[...]
        width = middle.shape[1]
        r = lax.rsqrt(jnp.mean(middle * middle, axis=1, keepdims=True) + EPSILON)
        h = (middle * r * gain_ref[...]).astype(bf16)
        payload_ref[:, :width] = h
        logits = dot_nt(h, router_ref[...])
        lane = lax.broadcasted_iota(jnp.int32, logits.shape, 1)
        chosen = lane == routes_ref[:, 0:1]
        for k in range(1, TOP):
            chosen = chosen | (lane == routes_ref[:, k : k + 1])
        logits = jnp.where(chosen, logits, MASKED)
        exps = jnp.where(chosen, jnp.exp(logits - jnp.max(logits, axis=1, keepdims=True)), 0.0)
        gates = exps / jnp.sum(exps, axis=1, keepdims=True)
        gates_ref[...] = gates
        high = gates.astype(bf16).astype(f32)
        payload_ref[:, width:] = (high + pltpu.roll(gates - high, experts, 1)).astype(bf16)


def project_out(o, x, gain, router, routes, offsets, pieces, experts):
    tokens, width = x.shape
    tile = 256
    return call(
        functools.partial(middle_kernel, experts),
        (width // tile,),
        [
            whole(o.shape),
            pl.BlockSpec((tokens, tile), lambda i, *_: (0, i)),
            whole(gain.shape),
            whole(router.shape),
            whole(routes.shape),
        ]
        + [pl.BlockSpec((n, tile), lambda i, *_: (0, i)) for _, n in pieces],
        [whole((tokens, width)), whole((tokens, width + LANES)), whole((tokens, LANES))],
        [
            jax.ShapeDtypeStruct((tokens, width), f32),
            jax.ShapeDtypeStruct((tokens, width + LANES), bf16),
            jax.ShapeDtypeStruct((tokens, LANES), f32),
        ],
        prefetch=1,
        flops=2 * tokens * width * o.shape[1],
        moved=2 * width * o.shape[1] + 10 * tokens * width,
    )(offsets, o, x, gain, router, routes, *[p for p, _ in pieces])


def one_hot(slots_ref, j, rows):
    tokens = slots_ref.shape[1]
    slot = lax.broadcasted_iota(jnp.int32, (rows, tokens), 0)
    return jnp.where(slot == slots_ref[j : j + 1, :], 1.0, 0.0).astype(bf16)


def select_kernel(slots_ref, block_ref, *outs):
    rows = outs[0].shape[0]
    picks = jnp.concatenate([one_hot(slots_ref, j, rows) for j in range(PLANE)], axis=0)
    chosen = dot(picks, block_ref[...]).astype(bf16)
    outs = outs if len(outs) == PLANE else [outs[0], outs[1], outs[2].at[0], outs[2].at[1]]
    for j, out in enumerate(outs):
        out[...] = chosen[j * rows : (j + 1) * rows]


def piece_shapes(rows, width, stacked):
    return [(rows, width)] * 2 + [(2, rows, width)] if stacked else [(rows, width)] * PLANE


def select(slots, block, rows, stacked):
    tokens, width = block.shape
    shapes = piece_shapes(rows, width, stacked)
    return call(
        select_kernel,
        (1,),
        [whole(slots.shape), whole(block.shape)],
        [whole(shape) for shape in shapes],
        [jax.ShapeDtypeStruct(shape, bf16) for shape in shapes],
        flops=2 * PLANE * rows * tokens * width,
        moved=2 * (PLANE * rows + tokens) * width,
    )(slots, block)


def piece_specs(parts):
    rows, width = parts[0].shape
    flat = whole((rows, width))
    if parts[1].ndim == 2:
        return [flat] * PLANE
    first = pl.BlockSpec((1, rows, width), lambda *_: (0, 0, 0))
    second = pl.BlockSpec((1, rows, width), lambda *_: (1, 0, 0))
    return [flat, first, first, second]


def piece_rows(refs):
    return [ref[0] if len(ref.shape) == 3 else ref[...] for ref in refs]


def combine_kernel(slots_ref, *refs):
    parts, rest = refs[:PLANE], refs[PLANE:]
    out = rest[-1]
    rows = parts[0].shape[0]
    picks = jnp.concatenate([one_hot(slots_ref, j, rows) for j in range(PLANE)], axis=0)
    total = dot_tn(picks, jnp.concatenate(piece_rows(parts), axis=0))
    for before in rest[:-1]:
        total = total + before[...].astype(f32)
    out[...] = total.astype(out.dtype)


def combine(slots, parts, rows, extra, dtype):
    tokens = slots.shape[1]
    width = parts[0].shape[1]
    extra = [value for value in extra if value is not None]
    return call(
        combine_kernel,
        (1,),
        [whole(slots.shape)] + piece_specs(parts) + [whole((tokens, width))] * len(extra),
        whole((tokens, width)),
        jax.ShapeDtypeStruct((tokens, width), dtype),
        flops=2 * PLANE * rows * tokens * width,
        moved=2 * (PLANE * rows + 3 * tokens) * width,
    )(slots, *parts, *extra)


def expert_kernel(experts, part, counts, at, *refs):
    xs, cs = refs[:PLANE], refs[PLANE : 2 * PLANE]
    groups, used = [], 2 * PLANE
    for axis, count in zip((0, 0, 1), counts):
        group = refs[used : used + count]
        starts = [pl.multiple_of(at[1 + used - 2 * PLANE + n], LANES) for n in range(count)]
        groups.append([(pl.ds(start, w.shape[axis]), w) for start, w in zip(starts, group)])
        used += count
    wgs, wus, wds = groups
    x_ref, dy_ref, y_acc, d_acc, gate_ref, sems = refs[-6:]
    outs = refs[-6 - PLANE - PIECES - 5 : -6]
    drows, ys = outs[:PLANE], outs[PLANE : PLANE + PIECES]
    rows_out, dy_out, a_ref, dg_ref, du_ref = outs[PLANE + PIECES :]
    xs = [ref.at[0] if len(ref.shape) == 3 else ref for ref in xs]
    cs = [ref.at[0] if len(ref.shape) == 3 else ref for ref in cs]
    ys = [ys[0], ys[1], ys[2].at[0], ys[2].at[1]]
    step = pl.program_id(0)
    expert = at[0]
    rows = xs[0].shape[0]
    width = x_ref.shape[1]
    lane = lax.broadcasted_iota(jnp.int32, (rows, LANES), 1)
    keep = [
        pltpu.make_async_copy(src, dst.at[pl.ds(part * PLANE * rows, PLANE * rows)], sems.at[n])
        for n, (src, dst) in enumerate(((x_ref, rows_out), (dy_ref, dy_out)))
    ]

    @pl.when(step == 0)
    def _():
        for j in range(PLANE):
            span = slice(j * rows, (j + 1) * rows)
            x_ref[span, :] = xs[j][:, :width]
            tail = xs[j][:, width:].astype(f32)
            mine = (lane == expert) | (lane == expert + experts)
            gate = jnp.sum(jnp.where(mine, tail, 0.0), axis=1, keepdims=True)
            gate_ref[span, :] = jnp.broadcast_to(gate, (rows, LANES))
            dy_ref[span, :] = (gate * cs[j][...].astype(f32)).astype(bf16)
        for copy in keep:
            copy.start()

    def total(values):
        return functools.reduce(lambda a, b: a + b, values)

    g = total([dot(x_ref[:, span], w[...]) for span, w in wgs])
    u = total([dot(x_ref[:, span], w[...]) for span, w in wus])
    sigma = 1.0 / (1.0 + jnp.exp(-g))
    swish = g * sigma
    a = (swish * u).astype(bf16)
    da = total([dot_nt(dy_ref[:, span], w[...]) for span, w in wds])
    dg = (da * u * sigma * (1.0 + g * (1.0 - sigma))).astype(bf16)
    du = (da * swish).astype(bf16)
    a_ref[...] = a
    dg_ref[...] = dg
    du_ref[...] = du
    first = step == 0
    for span, w in wds:
        y = dot(a, w[...])
        y_acc[:, span] = jnp.where(first, y, y_acc[:, span] + y)
    for span, w in wgs:
        d = dot_nt(dg, w[...])
        d_acc[:, span] = jnp.where(first, d, d_acc[:, span] + d)
    for span, w in wus:
        d_acc[:, span] += dot_nt(du, w[...])

    @pl.when(step == pl.num_programs(0) - 1)
    def _():
        for j in range(PLANE):
            span = slice(j * rows, (j + 1) * rows)
            yj = y_acc[span, :].astype(bf16).astype(f32)
            ys[j][...] = (gate_ref[span, 0:1] * yj).astype(bf16)
            dgate = jnp.sum(cs[j][...].astype(f32) * yj, axis=1, keepdims=True)
            high = dgate.astype(bf16).astype(f32)
            tail = jnp.where(lane == expert, high, 0.0) + jnp.where(lane == expert + experts, dgate - high, 0.0)
            drows[j][:, :width] = d_acc[span, :].astype(bf16)
            drows[j][:, width:] = tail.astype(bf16)
        for copy in keep:
            copy.wait()


def run_expert(index, part, parts, rows, experts, xs, cs, gates, ups, downs, kept):
    width = cs[0].shape[1]
    weights = gates + ups + downs
    hidden = gates[0][0].shape[1]
    tile = 256
    total = PLANE * rows
    at = jnp.stack([index] + [jnp.asarray(w[3]) for w in weights]).astype(jnp.int32)
    kept = [] if kept is None else list(kept)
    big = [width, width, hidden, hidden, hidden]
    shapes = piece_shapes(rows, width + LANES, False) + piece_shapes(rows, width, True)

    return call(
        functools.partial(expert_kernel, experts, part, (len(gates), len(ups), len(downs))),
        (hidden // tile,),
        piece_specs(xs)
        + piece_specs(cs)
        + [pl.BlockSpec((w[1], tile), lambda i, *_, block=w[2]: (block, i)) for w in gates + ups]
        + [pl.BlockSpec((tile, w[1]), lambda i, *_, block=w[2]: (i, block)) for w in downs]
        + [pl.BlockSpec(memory_space=pl.ANY)] * len(kept),
        [whole(shape) for shape in shapes]
        + [pl.BlockSpec(memory_space=pl.ANY)] * 2
        + [pl.BlockSpec((total, tile), lambda i, *_: (part, i))] * 3,
        [jax.ShapeDtypeStruct(shape, bf16) for shape in shapes]
        + [jax.ShapeDtypeStruct((parts * total, n), bf16) for n in big],
        scratch=[
            pltpu.VMEM((total, width), bf16),
            pltpu.VMEM((total, width), bf16),
            pltpu.VMEM((total, width), f32),
            pltpu.VMEM((total, width), f32),
            pltpu.VMEM((total, LANES), f32),
            pltpu.SemaphoreType.DMA((2,)),
        ],
        prefetch=1,
        flops=12 * total * width * hidden,
        moved=6 * width * hidden + 16 * total * width,
        vmem=60,
        aliases={1 + 2 * PLANE + len(weights) + n: PLANE + PIECES + n for n in range(len(kept))},
    )(at, *xs, *cs, *[w[0] for w in weights], *kept)


def halves_kernel(order, x_ref, y_ref, own_ref, away_ref):
    part = dot_tn(x_ref[...], y_ref[...])

    @pl.when(pl.program_id(0) == 0)
    def _():
        own_ref[...] = part

    @pl.when(pl.program_id(0) == 1)
    def _():
        away_ref[...] = part.astype(bf16)


def grad_halves(order, x, y, cut_y):
    rows = x.shape[0]
    wide = (rows, (y if cut_y else x).shape[1] // 2)
    cut = pl.BlockSpec(wide, lambda i, order: (0, order[i]))
    shape = (x.shape[1], wide[1]) if cut_y else (wide[1], y.shape[1])
    return call(
        halves_kernel,
        (2,),
        [whole(x.shape), cut] if cut_y else [cut, whole(y.shape)],
        [whole(shape), whole(shape)],
        [jax.ShapeDtypeStruct(shape, f32), jax.ShapeDtypeStruct(shape, bf16)],
        prefetch=1,
        flops=2 * rows * x.shape[1] * y.shape[1],
        moved=2 * rows * (x.shape[1] + y.shape[1]) + 6 * shape[0] * shape[1],
        vmem=60,
    )(order, x, y)


def fence(*values):
    leaves, tree = jax.tree.flatten(values)
    arrays = [n for n, leaf in enumerate(leaves) if isinstance(leaf, jax.Array)]
    for n, leaf in zip(arrays, lax.optimization_barrier([leaves[n] for n in arrays])):
        leaves[n] = leaf
    return jax.tree.unflatten(tree, leaves)


def after(value, *others):
    return fence(value, *others)[0]


def rope_tables(position):
    half_width = HEAD_DIM // 2
    frequency = ROPE_BASE ** (-jnp.arange(half_width, dtype=f32) / half_width)
    angle = position.astype(f32)[:, None] * frequency[None, :]
    cosine, sine = jnp.cos(angle), jnp.sin(angle)
    return jnp.concatenate([cosine, cosine], axis=1), jnp.concatenate([-sine, sine], axis=1)


def on_device(
    copies,
    experts,
    tokens,
    cotangent,
    segment_ids,
    padding,
    routes,
    placement_order,
    norm_attn,
    w_query,
    w_key,
    w_value,
    w_out,
    norm_ffn,
    w_router,
    w_gate,
    w_up,
    w_down,
):
    planes = experts // PLANE
    paired = copies == 2
    d = lax.axis_index("dp")
    e = lax.axis_index("expert")
    z, q = e // PLANE, lax.rem(e, PLANE)
    core = lax.rem(e, 2)

    def swap(value):
        return lax.ppermute(value, "dp", [(0, 1), (1, 0)])

    def across(value, j):
        return lax.ppermute(value, "expert", [(i, i ^ j) for i in range(experts)])

    def ahead(value):
        return lax.ppermute(value, "expert", [(i, (i + PLANE) % experts) for i in range(experts)])

    def join(own, other, index, axis):
        first = jnp.where(index == 0, own, other)
        second = jnp.where(index == 0, other, own)
        return jnp.concatenate([first, second], axis=axis)

    def gather(own, axis):
        if paired:
            return join(own, swap(own), d, axis)
        return lax.all_gather(own, "dp", axis=axis, tiled=True)

    def half_rows(own):
        half = own.shape[0] // 2
        return lax.dynamic_slice_in_dim(own, core * half, half, 0)

    def assemble(pieces):
        if len(pieces) == 1:
            return pieces[0]
        own, got, twin = pieces
        return join(own, join(got, twin, core, 0), d, 0)

    def z_send(value, s):
        return lax.ppermute(value, "expert", [(i, (i + s * PLANE) % experts) for i in range(experts)])

    x = tokens[0]
    cot = cotangent[0]
    tok_count, width = x.shape
    position = d * tok_count + jnp.arange(tok_count, dtype=jnp.int32)
    kv_width = KV_HEADS * HEAD_DIM
    q_width = HEADS * HEAD_DIM

    capacity = tok_count * TOP * 9 // (8 * experts)
    rows = (capacity + 15) // 16 * 16
    far = tok_count * TOP
    wishes = jnp.concatenate([routes[0].T, placement_order[0].T], axis=0)
    if paired:
        size = w_query.shape[0]
        got_half = jnp.concatenate([half_rows(w_query), half_rows(w_key), half_rows(w_value)], axis=1)
        small_own = jnp.concatenate([norm_attn[None], norm_ffn[None], w_router.T], axis=0)
        own_info = jnp.where(padding[0] == 1, segment_ids[0], -1)[None]
        first_own = jnp.concatenate(
            [small_own, jnp.pad(own_info.astype(bf16), ((0, 0), (0, size - tok_count)))], axis=0
        )
        first_rows = first_own.shape[0]
        first_own = jnp.pad(first_own, ((0, -first_rows % 16), (0, got_half.shape[1] - size)))
        wishes, got_half = fence(wishes, jnp.concatenate([got_half, first_own], axis=0))
    ring_wishes = jnp.stack([wishes] + [z_send(wishes, k) for k in range(1, planes)])
    near = jnp.stack([z * PLANE + (q ^ j) for j in range(PLANE)]).astype(jnp.int32)
    hits = ring_wishes[:, None, :TOP] == near[None, :, None, None]
    order = jnp.min(jnp.where(hits, ring_wishes[:, None, TOP:], far), axis=2)
    rank = jnp.sum((order[:, :, None, :] < order[:, :, :, None]).astype(jnp.int32), axis=3)
    slots = jnp.where((order < far) & (rank < capacity), rank, -1)

    qkv_own = jnp.concatenate([w_query, w_key, w_value], axis=1)
    cosine, sine = rope_tables(position)
    if paired:
        start = (1 - d) * size
        offsets = jnp.stack([d * size, start + core * size // 2, start + (1 - core) * size // 2]).astype(jnp.int32)
        cut = size // 6 // LANES * LANES
        cut_offsets = [d * size]
        for begin in (0, cut):
            cut_offsets += [start + core * size // 2 + begin, start + (1 - core) * size // 2 + begin]
        cut_offsets = jnp.stack(cut_offsets).astype(jnp.int32)
        got = swap(got_half)
        cot_one = ahead(cot)
        out_half = half_rows(w_out)
        out_late, out_got = out_half[:cut], out_half[cut:]
        first_other = got[size // 2 : size // 2 + first_rows, :size]
        small = join(small_own, first_other[:-1], d, 1)
        info = jnp.concatenate([own_info, first_other[-1:, :tok_count].astype(jnp.int32)], axis=1)
        other_position = (1 - d) * tok_count + jnp.arange(tok_count, dtype=jnp.int32)
        key_place = jnp.concatenate([position, other_position])[None]
    else:
        small = gather(jnp.concatenate([norm_attn[None], norm_ffn[None], w_router.T], axis=0), 1)
        cot_one = ahead(cot)
        offsets = cut_offsets = jnp.zeros((1,), jnp.int32)
        out_late = out_got = ()
        got = lax.all_gather(qkv_own, "dp", axis=0, tiled=True)
        own_info = jnp.where(padding[0] == 1, segment_ids[0], -1)[None]
        info = lax.all_gather(own_info, "dp", axis=1, tiled=True)
        key_place = jnp.arange(copies * tok_count, dtype=jnp.int32)[None]
    gain_one = small[0:1].astype(f32)
    gain_two = small[1:2].astype(f32)
    router_rows = jnp.pad(small[2:], ((0, LANES - experts), (0, 0)))
    small = small[2:]
    segment, place = segment_ids[0][:, None], position[:, None]
    allowed = (key_place <= place) & (info == segment) | (key_place == place)
    bias = jnp.where(allowed, 0.0, MASKED)

    def exchange(own, near_by, chips):
        return own, near_by, across(chips, 2)

    def direct(parts):
        return [parts[0]] + [across(parts[j], j) for j in range(1, PLANE)]

    def relay(parts):
        own, near_by, landed = parts
        near_by = across(jnp.concatenate([near_by[None], landed[1:]], axis=0), 1)
        return [own, near_by, landed, near_by]

    def hand_out(k, block):
        return exchange(*select(slots[k], block, rows, True))

    cots = {0: hand_out(0, cot)}
    expert_own = [w_gate[0], w_up[0], w_down[0]]
    got, slots, qkv_own, out_late, out_got, cosine, sine, cots[0], cut_offsets = fence(
        got, slots, qkv_own, out_late, out_got, cosine, sine, cots[0], cut_offsets
    )
    cot_two = ahead(cot_one)
    if paired:
        qkv_pieces = [(qkv_own, size), (got, size // 2), (across(got, 1), size // 2)]
        out_got = swap(out_got)
    else:
        qkv_pieces = [(got, width)]
        out_got = lax.all_gather(w_out, "dp", axis=0, tiled=True)
    qkv, hidden_one = project_qkv(x, gain_one, cosine, sine, offsets, qkv_pieces)

    own_kv = qkv[:, q_width:]
    bias, gain_two, router_rows, small = after((bias, gain_two, router_rows, small), own_kv)
    cots[0] = relay(after(cots[0], own_kv))
    cots[1] = select(slots[1], after(cot_one, own_kv), rows, True)
    if paired:
        keys_values = jnp.concatenate([own_kv, swap(own_kv)], axis=0)
    else:
        keys_values = lax.all_gather(own_kv, "dp", axis=0, tiled=True)
    keys_values, out_got, cots[0], cots[1], bias, gain_two, router_rows, small, cot_two = fence(
        keys_values, out_got, cots[0], cots[1], bias, gain_two, router_rows, small, cot_two
    )
    ring_cot = [cot, cot_one, cot_two]
    for _ in range(3, planes):
        ring_cot.append(ahead(ring_cot[-1]))
    if paired:
        out_late = swap(after(out_late, keys_values))
        out_pieces = [(out_got, size // 2 - cut), (across(out_got, 1), size // 2 - cut)]
        gate_first = swap(after(expert_own[0][: size // 2], keys_values))
    else:
        out_pieces = [(out_got, q_width)]
    cots[1] = exchange(*cots[1])
    attended, probs = attend(qkv, keys_values, bias)
    if paired:
        out_late, gate_first, _ = fence(out_late, gate_first, attended)
        gate_up = swap(jnp.concatenate([after(expert_own[0][size // 2 :], gate_first), expert_own[1]], axis=0))
        out_pieces = [(w_out, size), (out_late, cut), (across(out_late, 1), cut)] + out_pieces

    middle, payload, gates = project_out(
        attended, x, gain_two, router_rows, routes[0], cut_offsets, out_pieces, experts
    )
    if paired:
        payload, ring_cot, cots[1] = fence(payload, ring_cot, cots[1])

    ring = [payload, ahead(payload)]
    xs, drows, ys, kept = {}, {}, {}, None
    turns = list(range(1, planes)) + [0]

    def work(k, kept):
        outs = run_expert(e, k, planes, rows, experts, xs[k], cots[k], *expert_weights, kept)
        drows[k] = outs[:PLANE]
        ys[k] = outs[PLANE : PLANE + PIECES]
        return outs[PLANE + PIECES :]

    def give_back(k, before, dtype):
        return combine(slots[k], drows[k], rows, [before], dtype)

    def mix(k, *before):
        return combine(slots[k], ys[k], rows, before, bf16)

    cots[1] = relay(after(cots[1], payload))
    for k in range(2, planes):
        cots[k] = hand_out(k, after(ring_cot[k], payload))
    if paired:
        ring[1], gate_up, cots = fence(ring[1], gate_up, cots)
        down = swap(after(expert_own[2], ring[1]))
        other = (1 - d) * size
        expert_weights = [
            [(expert_own[0], size, 0, d * size), (gate_first, size // 2, 0, other), (gate_up, size // 2, 0, other + size // 2)],
            [(expert_own[1], size, 0, d * size), (gate_up, size // 2, 1, other), (gate_up, size // 2, 2, other + size // 2)],
            [(expert_own[2], size, 0, d * size), (down, size, 0, other)],
        ]
        ring.append(ahead(ring[1]))
        xs[1] = direct(select(slots[1], ring[1], rows, False))
        ring[2], xs[1], cots, expert_weights = fence(ring[2], xs[1], cots, expert_weights)
        ring.append(ahead(ring[2]))
        xs[2] = select(slots[2], ring[2], rows, False)
        xs[1], xs[2] = fence(xs[1], xs[2])
        xs[2] = direct(xs[2])
        kept = work(1, kept)
        drows[1], kept, xs[2] = fence(drows[1], kept, xs[2])
        drows[1] = direct(drows[1])
        cots[2], cots[3] = [relay(after(cots[k], kept)) for k in (2, 3)]
        kept = work(2, kept)
        drows[1], drows[2], kept, ring[3] = fence(drows[1], drows[2], kept, ring[3])
        back = give_back(1, None, bf16)
        back, drows[2] = fence(back, drows[2])
        back = ahead(back)
        drows[2] = direct(drows[2])
        xs[3] = exchange(*select(slots[3], ring[3], rows, True))
        xs[0] = select(slots[0], after(payload, ring[3]), rows, True)
        xs[0], xs[3], drows[2], back, kept = fence(xs[0], xs[3], drows[2], back, kept)
        back = give_back(2, back, bf16)
        xs[3] = relay(xs[3])
        back, kept, xs[3] = fence(back, kept, xs[3])
        back = ahead(back)
        xs[0] = exchange(*xs[0])
        kept = work(3, kept)
        drows[3], xs[0], kept = fence(drows[3], xs[0], kept)
        drows[3] = direct(drows[3])
        xs[0] = relay(xs[0])
        kept = work(0, kept)
        drows[0], drows[3], kept, back = fence(drows[0], drows[3], kept, back)
        back = give_back(3, back, bf16)

        back, drows[0], kept, ys = fence(back, drows[0], kept, ys)
        back = ahead(back)
        drows[0] = direct(drows[0])
        ys[1] = exchange(*ys[1])
    else:
        expert_weights = [
            [(lax.all_gather(w, "dp", axis=axis, tiled=True), width, 0, 0)]
            for w, axis in zip(expert_own, (0, 0, 1))
        ]
        for k in range(2, planes):
            cots[k] = relay(cots[k])
            ring.append(ahead(ring[-1]))
        back = None
        for k in turns:
            xs[k] = direct(select(slots[k], ring[k], rows, False))
            kept = work(k, kept)
            drows[k] = direct(drows[k])
            if k > 0:
                back = ahead(give_back(k, back, bf16))

    row_all, dy_all, a_all, dg_all, du_all = kept
    if paired:
        halves = jnp.stack([d, 1 - d]).astype(jnp.int32)
        keep_gate, away_gate = grad_halves(halves, row_all, dg_all, False)
        keep_up, away_up = grad_halves(halves, row_all, du_all, False)
        keep_down, away_down = grad_halves(halves, a_all, dy_all, True)
        drows[0], ys, away_gate, away_up, away_down, back = fence(
            drows[0], ys, away_gate, away_up, away_down, back
        )
        ys[1] = relay(ys[1])
        back = give_back(0, back, f32)
        back, ys = fence(back, ys)
        mixture = ahead(mix(1))
        middle_row = away_up.shape[0] // 2
        arrived_gate = swap(after(away_gate, back))
        arrived_up = []
        ys[2], ys[3] = exchange(*after(ys[2], back)), exchange(*after(ys[3], back))
    else:
        grad_gate, grad_up, grad_down = [
            lax.psum_scatter(full.astype(bf16), "dp", scatter_dimension=axis, tiled=True).astype(f32)[None]
            for full, axis in (
                (dot_tn(row_all, dg_all), 0),
                (dot_tn(row_all, du_all), 0),
                (dot_tn(a_all, dy_all), 1),
            )
        ]
        back = give_back(0, back, f32)

    upstream = cot.astype(f32)
    gates = gates[:, :experts]
    dgates = back[:, width : width + experts] + back[:, width + experts : width + 2 * experts]
    dlogits = (gates * (dgates - jnp.sum(gates * dgates, axis=1, keepdims=True))).astype(bf16)
    hidden_two = payload[:, :width]
    dh2 = back[:, :width] + dot(dlogits, small)
    scale_two = lax.rsqrt(jnp.mean(middle * middle, axis=1, keepdims=True) + EPSILON)
    normed_two = middle * scale_two
    e2 = dh2 * gain_two
    dmiddle = upstream + scale_two * (e2 - normed_two * jnp.mean(e2 * normed_two, axis=1, keepdims=True))
    dmb = dmiddle.astype(bf16)
    half_index = jnp.stack([core if paired else 0]).astype(jnp.int32)
    do = project_back(dmb, cut_offsets, out_pieces, bf16)
    grad_out = weight_grad(half_index, attended, dmb)

    other_chip = lax.rem(q // 2, 2)

    def add(*values):
        return functools.reduce(lambda a, b: a + b, [v.astype(f32) for v in values]).astype(bf16)

    def pick(value, index, axis=0):
        return lax.dynamic_index_in_dim(value, index, axis, keepdims=False)

    def halve(parts, index, send, axis=0):
        parts = [p.reshape(p.shape[:axis] + (2, -1, p.shape[-1])) for p in parts]
        away = add(*[pick(p, 1 - index, axis) for p in parts])
        return [pick(p, index, axis) for p in parts] + [send(away)]

    def over(j):
        return lambda value: across(value, j)

    def cut_core(parts):
        return [parts[0], across(parts[1], 1)]

    def both(part, j):
        return part, across(part, j)

    def sum_all(keep, away):
        both = jnp.concatenate([keep, away], axis=1).reshape(-1, keep.shape[2])
        part = lax.psum_scatter(both, "dp", scatter_dimension=0, tiled=True)
        return lax.psum(part, "expert").astype(f32)

    def unrotate(value):
        turned = jnp.concatenate([value[:, HEAD_DIM // 2 :], value[:, : HEAD_DIM // 2]], axis=1)
        return value * cosine - turned * sine

    dqp, dk, dv = attend_back(probs, do, qkv, keys_values, cosine, sine)
    dkv = jnp.concatenate([dk, dv], axis=1)
    input_tokens = x.astype(f32)
    scale_one = lax.rsqrt(jnp.mean(input_tokens * input_tokens, axis=1, keepdims=True) + EPSILON)
    normed_one = input_tokens * scale_one
    grad_norm_ffn_local = jnp.sum(dh2 * normed_two, axis=0)
    grad_router_local = lax.dot_general(dlogits, hidden_two, (((0,), (0,)), ((), ())), preferred_element_type=f32)

    def unrotated(dkv):
        dkp = [unrotate(dkv[:, n * HEAD_DIM : (n + 1) * HEAD_DIM]) for n in range(KV_HEADS)]
        dkvp = jnp.concatenate([v.astype(bf16) for v in dkp] + [dkv[:, kv_width:].astype(bf16)], axis=1)
        return jnp.concatenate([dqp, dkvp], axis=1)

    def through_projections(dqkv):
        dh1 = project_back(dqkv, offsets, qkv_pieces, f32)
        grad_norm_attn_local = jnp.sum(dh1 * normed_one, axis=0)
        extra = jnp.concatenate(
            [grad_norm_attn_local[None], grad_norm_ffn_local[None], grad_router_local], axis=0
        )
        extra = extra.astype(bf16)
        e1 = dh1 * gain_one
        grad_inputs = dmiddle + scale_one * (
            e1 - normed_one * jnp.mean(e1 * normed_one, axis=1, keepdims=True)
        )
        return extra, grad_inputs

    if paired:
        low, high = lax.rem(z, 2), z // 2
        away_dkv = dkv[tok_count:].astype(bf16)
        away_dkv, dqp, ys, arrived_gate, mixture = fence(away_dkv, dqp, ys, arrived_gate, mixture)
        other_dkv = swap(away_dkv)
        ys[2] = relay(ys[2])
        sum_a = weight_grad(half_index, hidden_one, dqp)
        grad_out = weight_grad(half_index, after(attended, sum_a), dmb)
        sum_a, other_dkv, grad_out = fence(sum_a, other_dkv, grad_out)
        sum_a, sum_out = cut_core(sum_a), cut_core(grad_out)
        ys[3] = relay(ys[3])
        dqkv = unrotated(dkv[:tok_count] + other_dkv.astype(f32))
        sum_b = weight_grad(half_index, hidden_one, dqkv[:, q_width:])
        mixture = mix(2, mixture)
        sum_a, sum_out, sum_b, dqkv, ys, mixture = fence(sum_a, sum_out, sum_b, dqkv, ys, mixture)
        sum_a = halve(sum_a, d, swap)
        sum_out = halve(sum_out, other_chip, over(2), 1)
        sum_b = cut_core(sum_b)
        mixture = ahead(mixture)
        extra, grad_inputs = through_projections(after(dqkv, sum_b))
        sum_a, sum_out, sum_b, mixture, extra = fence(sum_a, sum_out, sum_b, mixture, extra)
        sum_a = halve(sum_a, other_chip, over(2))
        sum_b = halve(sum_b, d, swap)
        sum_out = halve(sum_out, low, over(4), 1)
        extra = both(extra, 1)
        sum_a, sum_out, sum_b, extra = fence(sum_a, sum_out, sum_b, extra)
        sum_b = halve(sum_b, other_chip, over(2))
        sum_out = halve(sum_out, high, over(8), 1)
        extra = both(add(*extra), 2)
        arrived_up.append(swap(after(away_up[:middle_row], sum_a)))
        sum_a, sum_out, sum_b, arrived_up, extra = fence(sum_a, sum_out, sum_b, arrived_up, extra)
        sums = halve([jnp.concatenate([add(*sum_a), add(*sum_b)], axis=1)], low, over(4))
        sum_out = halve(sum_out, d, swap)
        extra = both(add(*extra), 4)
        sums, sum_out, extra = fence(sums, sum_out, extra)
        sums = halve(sums, high, lambda value: value)
        sum_out = both(after(add(*sum_out).reshape(-1, width), sums[-1]), 8)
        sums[-1] = across(sums[-1], 8)
        sums, sum_out = fence(sums, sum_out)
        sums = both(add(*sums), 8)
        ys[0] = exchange(*after(ys[0], sum_out))
        sum_out = both(join(*sum_out, high, 0), 4)
        extra = both(after(add(*extra), sum_out[0]), 8)
        arrived_up.append(swap(after(away_up[middle_row:], sums[0])))
        sums, sum_out, ys[0], extra, arrived_up = fence(sums, sum_out, ys[0], extra, arrived_up)
        sums = both(join(*sums, high, 0), 4)
        sum_out = both(join(*sum_out, low, 0), 2)
        ys[0] = relay(ys[0])
        extra = add(*extra)
        extra = (extra, swap(extra))
        mixture = mix(3, mixture)
        sums, mixture, extra = fence(sums, mixture, extra)
        sums = both(join(*sums, low, 0), 2)
        arrived_down = swap(after(away_down, mixture))
        mixture = ahead(mixture)
        grad_gate = (keep_gate + arrived_gate.astype(f32))[None]
        grad_up = (keep_up + jnp.concatenate(arrived_up, axis=0).astype(f32))[None]
        sums, sum_out, grad_gate, grad_up, arrived_down, mixture = fence(
            sums, sum_out, grad_gate, grad_up, arrived_down, mixture
        )
        sums = both(join(*sums, other_chip, 0), 1)
        sum_out = both(join(*sum_out, other_chip, 0), 1)
        sum_out = join(*sum_out, core, 0).astype(f32)
        grad_down = (keep_down + arrived_down.astype(f32))[None]
        mixed = mix(0, mixture, middle)[None]
        extra = lax.dynamic_slice_in_dim(add(*extra), d * size, size, 1).astype(f32)
        sum_q, sum_key, sum_value = [
            join(sums[0][:, cols], sums[1][:, cols], core, 0).astype(f32)
            for cols in [
                slice(0, q_width),
                slice(q_width, q_width + kv_width),
                slice(q_width + kv_width, q_width + 2 * kv_width),
            ]
        ]
    else:
        dkv = lax.psum_scatter(dkv.astype(bf16), "dp", scatter_dimension=0, tiled=True).astype(f32)
        dqkv = unrotated(dkv)
        extra, grad_inputs = through_projections(dqkv)
        sum_qkv = sum_all(*weight_grad(half_index, hidden_one, dqkv))
        sum_q, sum_key = sum_qkv[:, :q_width], sum_qkv[:, q_width : q_width + kv_width]
        sum_value = sum_qkv[:, q_width + kv_width :]
        sum_out = sum_all(*grad_out)
        extra = lax.psum_scatter(extra, "dp", scatter_dimension=1, tiled=True)
        extra = lax.psum(extra, "expert").astype(f32)
        ys = {k: relay(exchange(*y)) for k, y in ys.items()}
        mixture = None
        for k in turns[:-1]:
            mixture = ahead(mix(k, mixture))
        mixed = mix(0, mixture, middle)[None]
    return (
        mixed,
        grad_inputs[None],
        extra[0],
        sum_q,
        sum_key,
        sum_value,
        sum_out,
        extra[1],
        extra[2 : 2 + experts].T,
        grad_gate,
        grad_up,
        grad_down,
    )


def solution(mesh):
    rows = P("expert", "dp", None)
    return jax.shard_map(
        functools.partial(on_device, mesh.shape["dp"], mesh.shape["expert"]),
        mesh=mesh,
        in_specs=(
            rows,
            rows,
            P("expert", "dp"),
            P("expert", "dp"),
            rows,
            rows,
            P("dp"),
            P("dp", None),
            P("dp", None),
            P("dp", None),
            P("dp", None),
            P("dp"),
            P("dp", None),
            rows,
            rows,
            P("expert", None, "dp"),
        ),
        out_specs=(
            rows,
            rows,
            P("dp"),
            P("dp", None),
            P("dp", None),
            P("dp", None),
            P("dp", None),
            P("dp"),
            P("dp", None),
            rows,
            rows,
            P("expert", None, "dp"),
        ),
        check_vma=False,
    )
```

```python
import functools
import math

import jax
import jax.numpy as jnp
from jax import lax
from jax.experimental import pallas as pl
from jax.experimental.pallas import tpu as pltpu
from jax.sharding import PartitionSpec as P

HEADS = 12
KV_HEADS = 2
HEAD_DIM = 128
TOP = 4
GROUP = HEADS // KV_HEADS
PLANE = 4
LANES = 128
PIECES = 3

EPSILON = 1e-06
ROPE_BASE = 1000000.0
MASKED = -1e30
MIB = 1024 * 1024

f32 = jnp.float32
bf16 = jnp.bfloat16


def dot(a, b):
    return jnp.dot(a, b, preferred_element_type=f32)


def dot_nt(a, b):
    return lax.dot_general(a, b, (((1,), (1,)), ((), ())), preferred_element_type=f32)


def dot_tn(a, b):
    return lax.dot_general(a, b, (((0,), (0,)), ((), ())), preferred_element_type=f32)


def whole(shape):
    return pl.BlockSpec(shape, lambda *_: (0,) * len(shape))


def call(kernel, grid, in_specs, out_specs, out_shape, scratch=(), prefetch=0, flops=0, moved=0, vmem=20, aliases=None):
    return pl.pallas_call(
        kernel,
        grid_spec=pltpu.PrefetchScalarGridSpec(
            num_scalar_prefetch=prefetch,
            grid=grid,
            in_specs=in_specs,
            out_specs=out_specs,
            scratch_shapes=list(scratch),
        ),
        out_shape=out_shape,
        input_output_aliases=aliases or {},
        cost_estimate=pl.CostEstimate(flops=flops // 64, bytes_accessed=moved // 64, transcendentals=0),
        compiler_params=pltpu.CompilerParams(
            dimension_semantics=("arbitrary",) * len(grid), vmem_limit_bytes=vmem * MIB
        ),
    )


def qkv_kernel(offsets, x_ref, gain_ref, cos_ref, sin_ref, *refs):
    pieces, (out_ref, h_ref) = refs[:-2], refs[-2:]
    step = pl.program_id(0)

    @pl.when(step == 0)
    def _():
        x = x_ref[...].astype(f32)
        r = lax.rsqrt(jnp.mean(x * x, axis=1, keepdims=True) + EPSILON)
        h_ref[...] = (x * r * gain_ref[...]).astype(bf16)

    acc = None
    for n, w_ref in enumerate(pieces):
        rows = w_ref.shape[0]
        start = pl.multiple_of(offsets[n], LANES)
        part = dot(h_ref[:, pl.ds(start, rows)], w_ref[...])
        acc = part if acc is None else acc + part

    rotary = step * out_ref.shape[1] < (HEADS + KV_HEADS) * HEAD_DIM

    @pl.when(rotary)
    def _():
        for n in range(out_ref.shape[1] // HEAD_DIM):
            a = acc[:, n * HEAD_DIM : (n + 1) * HEAD_DIM]
            turned = a * cos_ref[...] + pltpu.roll(a, HEAD_DIM // 2, 1) * sin_ref[...]
            out_ref[:, n * HEAD_DIM : (n + 1) * HEAD_DIM] = turned.astype(bf16)

    @pl.when(jnp.logical_not(rotary))
    def _():
        out_ref[...] = acc.astype(bf16)


def project_qkv(x, gain, cosine, sine, offsets, pieces):
    tokens, width = x.shape
    columns = pieces[0][0].shape[1]
    tile = 256
    return call(
        qkv_kernel,
        (columns // tile,),
        [whole(x.shape), whole(gain.shape), whole(cosine.shape), whole(sine.shape)]
        + [pl.BlockSpec((n, tile), lambda i, *_: (0, i)) for _, n in pieces],
        [pl.BlockSpec((tokens, tile), lambda i, *_: (0, i)), whole(x.shape)],
        [jax.ShapeDtypeStruct((tokens, columns), bf16), jax.ShapeDtypeStruct(x.shape, bf16)],
        prefetch=1,
        flops=2 * tokens * width * columns,
        moved=2 * width * columns + 4 * tokens * columns,
    )(offsets, x, gain, cosine, sine, *[p for p, _ in pieces])


def back_kernel(offsets, x_ref, *refs):
    pieces, (out_ref, acc_ref) = refs[:-2], refs[-2:]
    step = pl.program_id(0)
    for n, w_ref in enumerate(pieces):
        rows = w_ref.shape[0]
        span = pl.ds(pl.multiple_of(offsets[n], LANES), rows)
        part = dot_nt(x_ref[...], w_ref[...])
        acc_ref[:, span] = jnp.where(step == 0, part, acc_ref[:, span] + part)

    @pl.when(step == pl.num_programs(0) - 1)
    def _():
        out_ref[...] = acc_ref[...].astype(out_ref.dtype)


def project_back(x, offsets, pieces, dtype):
    tokens, columns = x.shape
    width = sum(n for _, n in pieces)
    tile = 512
    return call(
        back_kernel,
        (columns // tile,),
        [pl.BlockSpec((tokens, tile), lambda i, *_: (0, i))]
        + [pl.BlockSpec((n, tile), lambda i, *_: (0, i)) for _, n in pieces],
        whole((tokens, width)),
        jax.ShapeDtypeStruct((tokens, width), dtype),
        scratch=[pltpu.VMEM((tokens, width), f32)],
        prefetch=1,
        flops=2 * tokens * width * columns,
        moved=2 * width * columns + 6 * tokens * columns,
    )(offsets, x, *[p for p, _ in pieces])


def weight_grad_kernel(core, x_ref, y_ref, keep_ref, away_ref):
    rows = keep_ref.shape[1]
    for n, out_ref in enumerate((keep_ref, away_ref)):
        part = core[0] if n == 0 else 1 - core[0]
        start = pl.multiple_of(part * rows, LANES)
        out_ref[0] = dot_tn(x_ref[:, pl.ds(start, rows)], y_ref[...]).astype(bf16)


def weight_grad(core, x, y, block=0, blocks=1):
    tokens, width = x.shape
    columns = y.shape[1] // blocks
    half = width // 2
    shape = (2, half // 2, columns)
    return call(
        weight_grad_kernel,
        (2,),
        [
            pl.BlockSpec((tokens, half), lambda i, *_: (0, i)),
            pl.BlockSpec((tokens, columns), lambda i, *_: (0, block)),
        ],
        [pl.BlockSpec((1,) + shape[1:], lambda i, *_: (i, 0, 0))] * 2,
        [jax.ShapeDtypeStruct(shape, bf16)] * 2,
        prefetch=1,
        flops=2 * tokens * width * columns,
        moved=4 * width * columns,
    )(core, x, y)


def heads_together(keys):
    return 2 if keys <= 1024 else 1


def attend_kernel(q_ref, k_ref, v_ref, bias_ref, o_ref, p_ref):
    for n in range(p_ref.shape[0]):
        span = slice(n * HEAD_DIM, (n + 1) * HEAD_DIM)
        scores = dot_nt(q_ref[:, span], k_ref[...]) * (math.log2(math.e) / math.sqrt(HEAD_DIM)) + bias_ref[...]
        peak = jnp.max(scores, axis=1, keepdims=True)
        exps = jnp.exp2(scores - peak)
        probs = (exps * (1.0 / jnp.sum(exps, axis=1, keepdims=True))).astype(bf16)
        p_ref[n] = probs
        o_ref[:, span] = dot(probs, v_ref[...]).astype(bf16)


def attend(qkv, keys_values, bias):
    tokens = qkv.shape[0]
    keys = keys_values.shape[0]
    heads = heads_together(keys)
    wide = (tokens, heads * HEAD_DIM)
    return call(
        attend_kernel,
        (HEADS // heads,),
        [
            pl.BlockSpec(wide, lambda h: (0, h)),
            pl.BlockSpec((keys, HEAD_DIM), lambda h: (0, h * heads // GROUP)),
            pl.BlockSpec((keys, HEAD_DIM), lambda h: (0, KV_HEADS + h * heads // GROUP)),
            whole(bias.shape),
        ],
        [
            pl.BlockSpec(wide, lambda h: (0, h)),
            pl.BlockSpec((heads, tokens, keys), lambda h: (h, 0, 0)),
        ],
        [
            jax.ShapeDtypeStruct((tokens, HEADS * HEAD_DIM), bf16),
            jax.ShapeDtypeStruct((HEADS, tokens, keys), bf16),
        ],
        flops=4 * HEADS * tokens * keys * HEAD_DIM,
        moved=2 * HEADS * tokens * keys,
        vmem=24 * max(1, keys // 1536),
    )(qkv, keys_values, keys_values, bias)


def attend_back_kernel(p_ref, do_ref, q_ref, k_ref, v_ref, cos_ref, sin_ref, dq_ref, dk_ref, dv_ref):
    scale = 1.0 / math.sqrt(HEAD_DIM)
    heads = p_ref.shape[0]
    member = lax.rem(pl.program_id(0), GROUP // heads)
    dk, dv = None, None
    for n in range(heads):
        span = slice(n * HEAD_DIM, (n + 1) * HEAD_DIM)
        probs = p_ref[n]
        wide = probs.astype(f32)
        do = do_ref[:, span]
        grad_probs = dot_nt(do, v_ref[...])
        delta = jnp.sum(wide * grad_probs, axis=1, keepdims=True)
        grad_scores = (wide * (grad_probs - delta)).astype(bf16)
        dq = dot(grad_scores, k_ref[...]) * scale
        dq_ref[:, span] = (dq * cos_ref[...] - pltpu.roll(dq, HEAD_DIM // 2, 1) * sin_ref[...]).astype(bf16)
        dk_part, dv_part = dot_tn(grad_scores, q_ref[:, span]), dot_tn(probs, do)
        dk, dv = (dk_part, dv_part) if n == 0 else (dk + dk_part, dv + dv_part)
    dk = dk * scale

    @pl.when(member == 0)
    def _():
        dk_ref[...] = dk
        dv_ref[...] = dv

    @pl.when(member > 0)
    def _():
        dk_ref[...] += dk
        dv_ref[...] += dv


def attend_back(probs, do, qkv, keys_values, cosine, sine):
    tokens = qkv.shape[0]
    keys = keys_values.shape[0]
    kv_width = KV_HEADS * HEAD_DIM
    heads = heads_together(keys)
    wide = (tokens, heads * HEAD_DIM)
    return call(
        attend_back_kernel,
        (HEADS // heads,),
        [
            pl.BlockSpec((heads, tokens, keys), lambda h: (h, 0, 0)),
            pl.BlockSpec(wide, lambda h: (0, h)),
            pl.BlockSpec(wide, lambda h: (0, h)),
            pl.BlockSpec((keys, HEAD_DIM), lambda h: (0, h * heads // GROUP)),
            pl.BlockSpec((keys, HEAD_DIM), lambda h: (0, KV_HEADS + h * heads // GROUP)),
            whole(cosine.shape),
            whole(sine.shape),
        ],
        [
            pl.BlockSpec(wide, lambda h: (0, h)),
            pl.BlockSpec((keys, HEAD_DIM), lambda h: (0, h * heads // GROUP)),
            pl.BlockSpec((keys, HEAD_DIM), lambda h: (0, h * heads // GROUP)),
        ],
        [
            jax.ShapeDtypeStruct((tokens, HEADS * HEAD_DIM), bf16),
            jax.ShapeDtypeStruct((keys, kv_width), f32),
            jax.ShapeDtypeStruct((keys, kv_width), f32),
        ],
        flops=8 * HEADS * tokens * keys * HEAD_DIM,
        moved=2 * HEADS * tokens * keys,
        vmem=24 * max(1, keys // 1536),
    )(probs, do, qkv, keys_values, keys_values, cosine, sine)


def middle_kernel(experts, offsets, o_ref, x_ref, gain_ref, router_ref, routes_ref, *refs):
    pieces, (middle_ref, payload_ref, gates_ref) = refs[:-3], refs[-3:]
    step = pl.program_id(0)
    tile = x_ref.shape[1]
    acc = x_ref[...].astype(f32)
    for n, w_ref in enumerate(pieces):
        start = pl.multiple_of(offsets[n], LANES)
        acc = acc + dot(o_ref[:, pl.ds(start, w_ref.shape[0])], w_ref[...])
    middle_ref[:, pl.ds(pl.multiple_of(step * tile, tile), tile)] = acc

    @pl.when(step == pl.num_programs(0) - 1)
    def _():
        middle = middle_ref[...]
        width = middle.shape[1]
        r = lax.rsqrt(jnp.mean(middle * middle, axis=1, keepdims=True) + EPSILON)
        h = (middle * r * gain_ref[...]).astype(bf16)
        payload_ref[:, :width] = h
        logits = dot_nt(h, router_ref[...])
        lane = lax.broadcasted_iota(jnp.int32, logits.shape, 1)
        chosen = lane == routes_ref[:, 0:1]
        for k in range(1, TOP):
            chosen = chosen | (lane == routes_ref[:, k : k + 1])
        logits = jnp.where(chosen, logits, MASKED)
        exps = jnp.where(chosen, jnp.exp(logits - jnp.max(logits, axis=1, keepdims=True)), 0.0)
        gates = exps / jnp.sum(exps, axis=1, keepdims=True)
        gates_ref[...] = gates
        high = gates.astype(bf16).astype(f32)
        payload_ref[:, width:] = (high + pltpu.roll(gates - high, experts, 1)).astype(bf16)


def project_out(o, x, gain, router, routes, offsets, pieces, experts):
    tokens, width = x.shape
    tile = 256
    return call(
        functools.partial(middle_kernel, experts),
        (width // tile,),
        [
            whole(o.shape),
            pl.BlockSpec((tokens, tile), lambda i, *_: (0, i)),
            whole(gain.shape),
            whole(router.shape),
            whole(routes.shape),
        ]
        + [pl.BlockSpec((n, tile), lambda i, *_: (0, i)) for _, n in pieces],
        [whole((tokens, width)), whole((tokens, width + LANES)), whole((tokens, LANES))],
        [
            jax.ShapeDtypeStruct((tokens, width), f32),
            jax.ShapeDtypeStruct((tokens, width + LANES), bf16),
            jax.ShapeDtypeStruct((tokens, LANES), f32),
        ],
        prefetch=1,
        flops=2 * tokens * width * o.shape[1],
        moved=2 * width * o.shape[1] + 10 * tokens * width,
    )(offsets, o, x, gain, router, routes, *[p for p, _ in pieces])


def one_hot(slots_ref, j, rows):
    tokens = slots_ref.shape[1]
    slot = lax.broadcasted_iota(jnp.int32, (rows, tokens), 0)
    return jnp.where(slot == slots_ref[j : j + 1, :], 1.0, 0.0).astype(bf16)


def select_kernel(slots_ref, block_ref, *outs):
    rows = outs[0].shape[0]
    picks = jnp.concatenate([one_hot(slots_ref, j, rows) for j in range(PLANE)], axis=0)
    chosen = dot(picks, block_ref[...]).astype(bf16)
    outs = outs if len(outs) == PLANE else [outs[0], outs[1], outs[2].at[0], outs[2].at[1]]
    for j, out in enumerate(outs):
        out[...] = chosen[j * rows : (j + 1) * rows]


def piece_shapes(rows, width, stacked):
    return [(rows, width)] * 2 + [(2, rows, width)] if stacked else [(rows, width)] * PLANE


def select(slots, block, rows, stacked):
    tokens, width = block.shape
    shapes = piece_shapes(rows, width, stacked)
    return call(
        select_kernel,
        (1,),
        [whole(slots.shape), whole(block.shape)],
        [whole(shape) for shape in shapes],
        [jax.ShapeDtypeStruct(shape, bf16) for shape in shapes],
        flops=2 * PLANE * rows * tokens * width,
        moved=2 * (PLANE * rows + tokens) * width,
    )(slots, block)


def piece_specs(parts):
    rows, width = parts[0].shape
    flat = whole((rows, width))
    if parts[1].ndim == 2:
        return [flat] * PLANE
    first = pl.BlockSpec((1, rows, width), lambda *_: (0, 0, 0))
    second = pl.BlockSpec((1, rows, width), lambda *_: (1, 0, 0))
    return [flat, first, first, second]


def piece_rows(refs):
    return [ref[0] if len(ref.shape) == 3 else ref[...] for ref in refs]


def combine_kernel(slots_ref, *refs):
    parts, rest = refs[:PLANE], refs[PLANE:]
    out = rest[-1]
    rows = parts[0].shape[0]
    picks = jnp.concatenate([one_hot(slots_ref, j, rows) for j in range(PLANE)], axis=0)
    total = dot_tn(picks, jnp.concatenate(piece_rows(parts), axis=0))
    for before in rest[:-1]:
        total = total + before[...].astype(f32)
    out[...] = total.astype(out.dtype)


def combine(slots, parts, rows, extra, dtype):
    tokens = slots.shape[1]
    width = parts[0].shape[1]
    extra = [value for value in extra if value is not None]
    return call(
        combine_kernel,
        (1,),
        [whole(slots.shape)] + piece_specs(parts) + [whole((tokens, width))] * len(extra),
        whole((tokens, width)),
        jax.ShapeDtypeStruct((tokens, width), dtype),
        flops=2 * PLANE * rows * tokens * width,
        moved=2 * (PLANE * rows + 3 * tokens) * width,
    )(slots, *parts, *extra)


def expert_kernel(experts, part, counts, at, *refs):
    xs, cs = refs[:PLANE], refs[PLANE : 2 * PLANE]
    groups, used = [], 2 * PLANE
    for axis, count in zip((0, 0, 1), counts):
        group = refs[used : used + count]
        starts = [pl.multiple_of(at[1 + used - 2 * PLANE + n], LANES) for n in range(count)]
        groups.append([(pl.ds(start, w.shape[axis]), w) for start, w in zip(starts, group)])
        used += count
    wgs, wus, wds = groups
    x_ref, dy_ref, y_acc, d_acc, gate_ref, sems = refs[-6:]
    outs = refs[-6 - PLANE - PIECES - 5 : -6]
    drows, ys = outs[:PLANE], outs[PLANE : PLANE + PIECES]
    rows_out, dy_out, a_ref, dg_ref, du_ref = outs[PLANE + PIECES :]
    xs = [ref.at[0] if len(ref.shape) == 3 else ref for ref in xs]
    cs = [ref.at[0] if len(ref.shape) == 3 else ref for ref in cs]
    ys = [ys[0], ys[1], ys[2].at[0], ys[2].at[1]]
    step = pl.program_id(0)
    expert = at[0]
    rows = xs[0].shape[0]
    width = x_ref.shape[1]
    lane = lax.broadcasted_iota(jnp.int32, (rows, LANES), 1)
    keep = [
        pltpu.make_async_copy(src, dst.at[pl.ds(part * PLANE * rows, PLANE * rows)], sems.at[n])
        for n, (src, dst) in enumerate(((x_ref, rows_out), (dy_ref, dy_out)))
    ]

    @pl.when(step == 0)
    def _():
        for j in range(PLANE):
            span = slice(j * rows, (j + 1) * rows)
            x_ref[span, :] = xs[j][:, :width]
            tail = xs[j][:, width:].astype(f32)
            mine = (lane == expert) | (lane == expert + experts)
            gate = jnp.sum(jnp.where(mine, tail, 0.0), axis=1, keepdims=True)
            gate_ref[span, :] = jnp.broadcast_to(gate, (rows, LANES))
            dy_ref[span, :] = (gate * cs[j][...].astype(f32)).astype(bf16)
        for copy in keep:
            copy.start()

    def total(values):
        return functools.reduce(lambda a, b: a + b, values)

    g = total([dot(x_ref[:, span], w[...]) for span, w in wgs])
    u = total([dot(x_ref[:, span], w[...]) for span, w in wus])
    sigma = 1.0 / (1.0 + jnp.exp(-g))
    swish = g * sigma
    a = (swish * u).astype(bf16)
    da = total([dot_nt(dy_ref[:, span], w[...]) for span, w in wds])
    dg = (da * u * sigma * (1.0 + g * (1.0 - sigma))).astype(bf16)
    du = (da * swish).astype(bf16)
    a_ref[...] = a
    dg_ref[...] = dg
    du_ref[...] = du
    first = step == 0
    for span, w in wds:
        y = dot(a, w[...])
        y_acc[:, span] = jnp.where(first, y, y_acc[:, span] + y)
    for span, w in wgs:
        d = dot_nt(dg, w[...])
        d_acc[:, span] = jnp.where(first, d, d_acc[:, span] + d)
    for span, w in wus:
        d_acc[:, span] += dot_nt(du, w[...])

    @pl.when(step == pl.num_programs(0) - 1)
    def _():
        for j in range(PLANE):
            span = slice(j * rows, (j + 1) * rows)
            yj = y_acc[span, :].astype(bf16).astype(f32)
            ys[j][...] = (gate_ref[span, 0:1] * yj).astype(bf16)
            dgate = jnp.sum(cs[j][...].astype(f32) * yj, axis=1, keepdims=True)
            high = dgate.astype(bf16).astype(f32)
            tail = jnp.where(lane == expert, high, 0.0) + jnp.where(lane == expert + experts, dgate - high, 0.0)
            drows[j][:, :width] = d_acc[span, :].astype(bf16)
            drows[j][:, width:] = tail.astype(bf16)
        for copy in keep:
            copy.wait()


def run_expert(index, part, parts, rows, experts, xs, cs, gates, ups, downs, kept):
    width = cs[0].shape[1]
    weights = gates + ups + downs
    hidden = gates[0][0].shape[1]
    tile = 256
    total = PLANE * rows
    at = jnp.stack([index] + [jnp.asarray(w[3]) for w in weights]).astype(jnp.int32)
    kept = [] if kept is None else list(kept)
    big = [width, width, hidden, hidden, hidden]
    shapes = piece_shapes(rows, width + LANES, False) + piece_shapes(rows, width, True)

    return call(
        functools.partial(expert_kernel, experts, part, (len(gates), len(ups), len(downs))),
        (hidden // tile,),
        piece_specs(xs)
        + piece_specs(cs)
        + [pl.BlockSpec((w[1], tile), lambda i, *_, block=w[2]: (block, i)) for w in gates + ups]
        + [pl.BlockSpec((tile, w[1]), lambda i, *_, block=w[2]: (i, block)) for w in downs]
        + [pl.BlockSpec(memory_space=pl.ANY)] * len(kept),
        [whole(shape) for shape in shapes]
        + [pl.BlockSpec(memory_space=pl.ANY)] * 2
        + [pl.BlockSpec((total, tile), lambda i, *_: (part, i))] * 3,
        [jax.ShapeDtypeStruct(shape, bf16) for shape in shapes]
        + [jax.ShapeDtypeStruct((parts * total, n), bf16) for n in big],
        scratch=[
            pltpu.VMEM((total, width), bf16),
            pltpu.VMEM((total, width), bf16),
            pltpu.VMEM((total, width), f32),
            pltpu.VMEM((total, width), f32),
            pltpu.VMEM((total, LANES), f32),
            pltpu.SemaphoreType.DMA((2,)),
        ],
        prefetch=1,
        flops=12 * total * width * hidden,
        moved=6 * width * hidden + 16 * total * width,
        vmem=60,
        aliases={1 + 2 * PLANE + len(weights) + n: PLANE + PIECES + n for n in range(len(kept))},
    )(at, *xs, *cs, *[w[0] for w in weights], *kept)


def halves_kernel(order, x_ref, y_ref, own_ref, away_ref):
    part = dot_tn(x_ref[...], y_ref[...])

    @pl.when(pl.program_id(0) == 0)
    def _():
        own_ref[...] = part

    @pl.when(pl.program_id(0) == 1)
    def _():
        away_ref[...] = part.astype(bf16)


def grad_halves(order, x, y, cut_y):
    rows = x.shape[0]
    wide = (rows, (y if cut_y else x).shape[1] // 2)
    cut = pl.BlockSpec(wide, lambda i, order: (0, order[i]))
    shape = (x.shape[1], wide[1]) if cut_y else (wide[1], y.shape[1])
    return call(
        halves_kernel,
        (2,),
        [whole(x.shape), cut] if cut_y else [cut, whole(y.shape)],
        [whole(shape), whole(shape)],
        [jax.ShapeDtypeStruct(shape, f32), jax.ShapeDtypeStruct(shape, bf16)],
        prefetch=1,
        flops=2 * rows * x.shape[1] * y.shape[1],
        moved=2 * rows * (x.shape[1] + y.shape[1]) + 6 * shape[0] * shape[1],
        vmem=28,
    )(order, x, y)


def fence(*values):
    leaves, tree = jax.tree.flatten(values)
    arrays = [n for n, leaf in enumerate(leaves) if isinstance(leaf, jax.Array)]
    for n, leaf in zip(arrays, lax.optimization_barrier([leaves[n] for n in arrays])):
        leaves[n] = leaf
    return jax.tree.unflatten(tree, leaves)


def after(value, *others):
    return fence(value, *others)[0]


def rope_tables(position):
    half_width = HEAD_DIM // 2
    frequency = ROPE_BASE ** (-jnp.arange(half_width, dtype=f32) / half_width)
    angle = position.astype(f32)[:, None] * frequency[None, :]
    cosine, sine = jnp.cos(angle), jnp.sin(angle)
    return jnp.concatenate([cosine, cosine], axis=1), jnp.concatenate([-sine, sine], axis=1)


def on_device(
    copies,
    experts,
    tokens,
    cotangent,
    segment_ids,
    padding,
    routes,
    placement_order,
    norm_attn,
    w_query,
    w_key,
    w_value,
    w_out,
    norm_ffn,
    w_router,
    w_gate,
    w_up,
    w_down,
):
    planes = experts // PLANE
    paired = copies == 2
    d = lax.axis_index("dp")
    e = lax.axis_index("expert")
    z, q = e // PLANE, lax.rem(e, PLANE)
    core = lax.rem(e, 2)

    def swap(value):
        return lax.ppermute(value, "dp", [(0, 1), (1, 0)])

    def across(value, j):
        return lax.ppermute(value, "expert", [(i, i ^ j) for i in range(experts)])

    def ahead(value):
        return lax.ppermute(value, "expert", [(i, (i + PLANE) % experts) for i in range(experts)])

    def join(own, other, index, axis):
        first = jnp.where(index == 0, own, other)
        second = jnp.where(index == 0, other, own)
        return jnp.concatenate([first, second], axis=axis)

    def gather(own, axis):
        if paired:
            return join(own, swap(own), d, axis)
        return lax.all_gather(own, "dp", axis=axis, tiled=True)

    def half_rows(own):
        half = own.shape[0] // 2
        return lax.dynamic_slice_in_dim(own, core * half, half, 0)

    def assemble(pieces):
        if len(pieces) == 1:
            return pieces[0]
        own, got, twin = pieces
        return join(own, join(got, twin, core, 0), d, 0)

    def z_send(value, s):
        return lax.ppermute(value, "expert", [(i, (i + s * PLANE) % experts) for i in range(experts)])

    x = tokens[0]
    cot = cotangent[0]
    tok_count, width = x.shape
    position = d * tok_count + jnp.arange(tok_count, dtype=jnp.int32)
    kv_width = KV_HEADS * HEAD_DIM
    q_width = HEADS * HEAD_DIM

    capacity = tok_count * TOP * 9 // (8 * experts)
    rows = (capacity + 15) // 16 * 16
    far = tok_count * TOP
    wishes = jnp.concatenate([routes[0].T, placement_order[0].T], axis=0)
    if paired:
        size = w_query.shape[0]
        got_half = jnp.concatenate([half_rows(w_query), half_rows(w_key), half_rows(w_value)], axis=1)
        small_own = jnp.concatenate([norm_attn[None], norm_ffn[None], w_router.T], axis=0)
        own_info = jnp.where(padding[0] == 1, segment_ids[0], -1)[None]
        first_own = jnp.concatenate(
            [small_own, jnp.pad(own_info.astype(bf16), ((0, 0), (0, size - tok_count)))], axis=0
        )
        first_rows = first_own.shape[0]
        first_own = jnp.pad(first_own, ((0, -first_rows % 16), (0, got_half.shape[1] - size)))
        wishes, got_half = fence(wishes, jnp.concatenate([got_half, first_own], axis=0))
    ring_wishes = jnp.stack([wishes] + [z_send(wishes, k) for k in range(1, planes)])
    near = jnp.stack([z * PLANE + (q ^ j) for j in range(PLANE)]).astype(jnp.int32)
    hits = ring_wishes[:, None, :TOP] == near[None, :, None, None]
    order = jnp.min(jnp.where(hits, ring_wishes[:, None, TOP:], far), axis=2)
    rank = jnp.sum((order[:, :, None, :] < order[:, :, :, None]).astype(jnp.int32), axis=3)
    slots = jnp.where((order < far) & (rank < capacity), rank, -1)

    qkv_own = jnp.concatenate([w_query, w_key, w_value], axis=1)
    cosine, sine = rope_tables(position)
    if paired:
        start = (1 - d) * size
        offsets = jnp.stack([d * size, start + core * size // 2, start + (1 - core) * size // 2]).astype(jnp.int32)
        cut = size // 6 // LANES * LANES
        cut_offsets = [d * size]
        for begin in (0, cut):
            cut_offsets += [start + core * size // 2 + begin, start + (1 - core) * size // 2 + begin]
        cut_offsets = jnp.stack(cut_offsets).astype(jnp.int32)
        got = swap(got_half)
        cot_one = ahead(cot)
        out_half = half_rows(w_out)
        out_late, out_got = out_half[:cut], out_half[cut:]
        first_other = got[size // 2 : size // 2 + first_rows, :size]
        small = join(small_own, first_other[:-1], d, 1)
        info = jnp.concatenate([own_info, first_other[-1:, :tok_count].astype(jnp.int32)], axis=1)
        other_position = (1 - d) * tok_count + jnp.arange(tok_count, dtype=jnp.int32)
        key_place = jnp.concatenate([position, other_position])[None]
    else:
        small = gather(jnp.concatenate([norm_attn[None], norm_ffn[None], w_router.T], axis=0), 1)
        cot_one = ahead(cot)
        offsets = cut_offsets = jnp.zeros((1,), jnp.int32)
        out_late = out_got = ()
        got = lax.all_gather(qkv_own, "dp", axis=0, tiled=True)
        own_info = jnp.where(padding[0] == 1, segment_ids[0], -1)[None]
        info = lax.all_gather(own_info, "dp", axis=1, tiled=True)
        key_place = jnp.arange(copies * tok_count, dtype=jnp.int32)[None]
    gain_one = small[0:1].astype(f32)
    gain_two = small[1:2].astype(f32)
    router_rows = jnp.pad(small[2:], ((0, LANES - experts), (0, 0)))
    small = small[2:]
    segment, place = segment_ids[0][:, None], position[:, None]
    allowed = (key_place <= place) & (info == segment) | (key_place == place)
    bias = jnp.where(allowed, 0.0, MASKED)

    def exchange(own, near_by, chips):
        return own, near_by, across(chips, 2)

    def direct(parts):
        return [parts[0]] + [across(parts[j], j) for j in range(1, PLANE)]

    def relay(parts):
        own, near_by, landed = parts
        near_by = across(jnp.concatenate([near_by[None], landed[1:]], axis=0), 1)
        return [own, near_by, landed, near_by]

    def hand_out(k, block):
        return exchange(*select(slots[k], block, rows, True))

    cots = {0: hand_out(0, cot)}
    expert_own = [w_gate[0], w_up[0], w_down[0]]
    got, slots, qkv_own, out_late, out_got, cosine, sine, cots[0], cut_offsets = fence(
        got, slots, qkv_own, out_late, out_got, cosine, sine, cots[0], cut_offsets
    )
    cot_two = ahead(cot_one)
    if paired:
        qkv_pieces = [(qkv_own, size), (got, size // 2), (across(got, 1), size // 2)]
        out_got = swap(out_got)
    else:
        qkv_pieces = [(got, width)]
        out_got = lax.all_gather(w_out, "dp", axis=0, tiled=True)
    qkv, hidden_one = project_qkv(x, gain_one, cosine, sine, offsets, qkv_pieces)

    own_kv = qkv[:, q_width:]
    bias, gain_two, router_rows, small = after((bias, gain_two, router_rows, small), own_kv)
    cots[0] = relay(after(cots[0], own_kv))
    cots[1] = select(slots[1], after(cot_one, own_kv), rows, True)
    if paired:
        keys_values = jnp.concatenate([own_kv, swap(own_kv)], axis=0)
    else:
        keys_values = lax.all_gather(own_kv, "dp", axis=0, tiled=True)
    keys_values, out_got, cots[0], cots[1], bias, gain_two, router_rows, small, cot_two = fence(
        keys_values, out_got, cots[0], cots[1], bias, gain_two, router_rows, small, cot_two
    )
    ring_cot = [cot, cot_one, cot_two]
    for _ in range(3, planes):
        ring_cot.append(ahead(ring_cot[-1]))
    if paired:
        out_late = swap(after(out_late, keys_values))
        out_pieces = [(out_got, size // 2 - cut), (across(out_got, 1), size // 2 - cut)]
    else:
        out_pieces = [(out_got, q_width)]
    cots[1] = exchange(*cots[1])
    attended, probs = attend(qkv, keys_values, bias)
    if paired:
        out_late, _ = fence(out_late, attended)
        gate_up = swap(after(jnp.concatenate(expert_own[:2], axis=0), out_late))
        out_pieces = [(w_out, size), (out_late, cut), (across(out_late, 1), cut)] + out_pieces

    middle, payload, gates = project_out(
        attended, x, gain_two, router_rows, routes[0], cut_offsets, out_pieces, experts
    )
    if paired:
        payload, ring_cot, cots[1] = fence(payload, ring_cot, cots[1])

    ring = [payload, ahead(payload)]
    xs, drows, ys, kept = {}, {}, {}, None
    turns = list(range(1, planes)) + [0]

    def work(k, kept):
        outs = run_expert(e, k, planes, rows, experts, xs[k], cots[k], *expert_weights, kept)
        drows[k] = outs[:PLANE]
        ys[k] = outs[PLANE : PLANE + PIECES]
        return outs[PLANE + PIECES :]

    def give_back(k, before, dtype):
        return combine(slots[k], drows[k], rows, [before], dtype)

    def mix(k, *before):
        return combine(slots[k], ys[k], rows, before, bf16)

    cots[1] = relay(after(cots[1], payload))
    for k in range(2, planes):
        cots[k] = hand_out(k, after(ring_cot[k], payload))
    if paired:
        ring[1], gate_up, cots = fence(ring[1], gate_up, cots)
        down = swap(after(expert_own[2], ring[1]))
        other = (1 - d) * size
        expert_weights = [
            [(expert_own[0], size, 0, d * size), (gate_up, size, 0, other)],
            [(expert_own[1], size, 0, d * size), (gate_up, size, 1, other)],
            [(expert_own[2], size, 0, d * size), (down, size, 0, other)],
        ]
        ring.append(ahead(ring[1]))
        xs[1] = direct(select(slots[1], ring[1], rows, False))
        ring[2], xs[1], cots, expert_weights = fence(ring[2], xs[1], cots, expert_weights)
        ring.append(ahead(ring[2]))
        xs[2] = select(slots[2], ring[2], rows, False)
        xs[1], xs[2] = fence(xs[1], xs[2])
        xs[2] = direct(xs[2])
        kept = work(1, kept)
        drows[1], kept, xs[2] = fence(drows[1], kept, xs[2])
        drows[1] = direct(drows[1])
        cots[2], cots[3] = [relay(after(cots[k], kept)) for k in (2, 3)]
        kept = work(2, kept)
        drows[1], drows[2], kept, ring[3] = fence(drows[1], drows[2], kept, ring[3])
        back = give_back(1, None, bf16)
        back, drows[2] = fence(back, drows[2])
        back = ahead(back)
        drows[2] = direct(drows[2])
        xs[3] = exchange(*select(slots[3], ring[3], rows, True))
        xs[0] = select(slots[0], after(payload, ring[3]), rows, True)
        xs[0], xs[3], drows[2], back, kept = fence(xs[0], xs[3], drows[2], back, kept)
        back = give_back(2, back, bf16)
        xs[3] = relay(xs[3])
        back, kept, xs[3] = fence(back, kept, xs[3])
        back = ahead(back)
        xs[0] = exchange(*xs[0])
        kept = work(3, kept)
        drows[3], xs[0], kept = fence(drows[3], xs[0], kept)
        drows[3] = direct(drows[3])
        xs[0] = relay(xs[0])
        kept = work(0, kept)
        drows[0], drows[3], kept, back = fence(drows[0], drows[3], kept, back)
        back = give_back(3, back, bf16)

        back, drows[0], kept, ys = fence(back, drows[0], kept, ys)
        back = ahead(back)
        drows[0] = direct(drows[0])
        ys[1] = exchange(*ys[1])
    else:
        expert_weights = [
            [(lax.all_gather(w, "dp", axis=axis, tiled=True), width, 0, 0)]
            for w, axis in zip(expert_own, (0, 0, 1))
        ]
        for k in range(2, planes):
            cots[k] = relay(cots[k])
            ring.append(ahead(ring[-1]))
        back = None
        for k in turns:
            xs[k] = direct(select(slots[k], ring[k], rows, False))
            kept = work(k, kept)
            drows[k] = direct(drows[k])
            if k > 0:
                back = ahead(give_back(k, back, bf16))

    row_all, dy_all, a_all, dg_all, du_all = kept
    if paired:
        halves = jnp.stack([d, 1 - d]).astype(jnp.int32)
        keep_gate, away_gate = grad_halves(halves, row_all, dg_all, False)
        keep_up, away_up = grad_halves(halves, row_all, du_all, False)
        keep_down, away_down = grad_halves(halves, a_all, dy_all, True)
        drows[0], ys, away_gate, away_up, away_down, back = fence(
            drows[0], ys, away_gate, away_up, away_down, back
        )
        arrived_gate = swap(away_gate)
        ys[2], ys[3] = exchange(*ys[2]), exchange(*ys[3])
        ys[1] = relay(ys[1])
        mixture = mix(1)
        back, mixture = fence(back, mixture)
        mixture = ahead(mixture)
        back = give_back(0, back, f32)
        middle_row = away_up.shape[0] // 2
        arrived_up = []
    else:
        grad_gate, grad_up, grad_down = [
            lax.psum_scatter(full.astype(bf16), "dp", scatter_dimension=axis, tiled=True).astype(f32)[None]
            for full, axis in (
                (dot_tn(row_all, dg_all), 0),
                (dot_tn(row_all, du_all), 0),
                (dot_tn(a_all, dy_all), 1),
            )
        ]
        back = give_back(0, back, f32)

    upstream = cot.astype(f32)
    gates = gates[:, :experts]
    dgates = back[:, width : width + experts] + back[:, width + experts : width + 2 * experts]
    dlogits = (gates * (dgates - jnp.sum(gates * dgates, axis=1, keepdims=True))).astype(bf16)
    hidden_two = payload[:, :width]
    dh2 = back[:, :width] + dot(dlogits, small)
    scale_two = lax.rsqrt(jnp.mean(middle * middle, axis=1, keepdims=True) + EPSILON)
    normed_two = middle * scale_two
    e2 = dh2 * gain_two
    dmiddle = upstream + scale_two * (e2 - normed_two * jnp.mean(e2 * normed_two, axis=1, keepdims=True))
    dmb = dmiddle.astype(bf16)
    half_index = jnp.stack([core if paired else 0]).astype(jnp.int32)
    do = project_back(dmb, cut_offsets, out_pieces, bf16)
    grad_out = weight_grad(half_index, attended, dmb)

    other_chip = lax.rem(q // 2, 2)

    def add(*values):
        return functools.reduce(lambda a, b: a + b, [v.astype(f32) for v in values]).astype(bf16)

    def pick(value, index, axis=0):
        return lax.dynamic_index_in_dim(value, index, axis, keepdims=False)

    def halve(parts, index, send, axis=0):
        parts = [p.reshape(p.shape[:axis] + (2, -1, p.shape[-1])) for p in parts]
        away = add(*[pick(p, 1 - index, axis) for p in parts])
        return [pick(p, index, axis) for p in parts] + [send(away)]

    def over(j):
        return lambda value: across(value, j)

    def cut_core(parts):
        return [parts[0], across(parts[1], 1)]

    def both(part, j):
        return part, across(part, j)

    def sum_all(keep, away):
        both = jnp.concatenate([keep, away], axis=1).reshape(-1, keep.shape[2])
        part = lax.psum_scatter(both, "dp", scatter_dimension=0, tiled=True)
        return lax.psum(part, "expert").astype(f32)

    def unrotate(value):
        turned = jnp.concatenate([value[:, HEAD_DIM // 2 :], value[:, : HEAD_DIM // 2]], axis=1)
        return value * cosine - turned * sine

    dqp, dk, dv = attend_back(probs, do, qkv, keys_values, cosine, sine)
    dkv = jnp.concatenate([dk, dv], axis=1)
    input_tokens = x.astype(f32)
    scale_one = lax.rsqrt(jnp.mean(input_tokens * input_tokens, axis=1, keepdims=True) + EPSILON)
    normed_one = input_tokens * scale_one
    grad_norm_ffn_local = jnp.sum(dh2 * normed_two, axis=0)
    grad_router_local = lax.dot_general(dlogits, hidden_two, (((0,), (0,)), ((), ())), preferred_element_type=f32)

    def unrotated(dkv):
        dkp = [unrotate(dkv[:, n * HEAD_DIM : (n + 1) * HEAD_DIM]) for n in range(KV_HEADS)]
        dkvp = jnp.concatenate([v.astype(bf16) for v in dkp] + [dkv[:, kv_width:].astype(bf16)], axis=1)
        return jnp.concatenate([dqp, dkvp], axis=1)

    def through_projections(dqkv):
        dh1 = project_back(dqkv, offsets, qkv_pieces, f32)
        grad_norm_attn_local = jnp.sum(dh1 * normed_one, axis=0)
        extra = jnp.concatenate(
            [grad_norm_attn_local[None], grad_norm_ffn_local[None], grad_router_local], axis=0
        )
        extra = extra.astype(bf16)
        e1 = dh1 * gain_one
        grad_inputs = dmiddle + scale_one * (
            e1 - normed_one * jnp.mean(e1 * normed_one, axis=1, keepdims=True)
        )
        return extra, grad_inputs

    if paired:
        low, high = lax.rem(z, 2), z // 2
        away_dkv = dkv[tok_count:].astype(bf16)
        away_dkv, dqp, ys, arrived_gate, mixture = fence(away_dkv, dqp, ys, arrived_gate, mixture)
        other_dkv = swap(away_dkv)
        ys[2] = relay(ys[2])
        sum_a = weight_grad(half_index, hidden_one, dqp)
        grad_out = weight_grad(half_index, after(attended, sum_a), dmb)
        sum_a, other_dkv, grad_out = fence(sum_a, other_dkv, grad_out)
        sum_a, sum_out = cut_core(sum_a), cut_core(grad_out)
        ys[3] = relay(ys[3])
        dqkv = unrotated(dkv[:tok_count] + other_dkv.astype(f32))
        sum_b = weight_grad(half_index, hidden_one, dqkv[:, q_width:])
        mixture = mix(2, mixture)
        sum_a, sum_out, sum_b, dqkv, ys, mixture = fence(sum_a, sum_out, sum_b, dqkv, ys, mixture)
        sum_a = halve(sum_a, d, swap)
        sum_out = halve(sum_out, other_chip, over(2), 1)
        sum_b = cut_core(sum_b)
        mixture = ahead(mixture)
        extra, grad_inputs = through_projections(after(dqkv, sum_b))
        sum_a, sum_out, sum_b, mixture, extra = fence(sum_a, sum_out, sum_b, mixture, extra)
        sum_a = halve(sum_a, other_chip, over(2))
        sum_b = halve(sum_b, d, swap)
        sum_out = halve(sum_out, low, over(4), 1)
        extra = both(extra, 1)
        sum_a, sum_out, sum_b, extra = fence(sum_a, sum_out, sum_b, extra)
        sum_b = halve(sum_b, other_chip, over(2))
        sum_out = halve(sum_out, high, over(8), 1)
        extra = both(add(*extra), 2)
        arrived_up.append(swap(after(away_up[:middle_row], sum_a)))
        sum_a, sum_out, sum_b, arrived_up, extra = fence(sum_a, sum_out, sum_b, arrived_up, extra)
        sums = halve([jnp.concatenate([add(*sum_a), add(*sum_b)], axis=1)], low, over(4))
        sum_out = halve(sum_out, d, swap)
        extra = both(add(*extra), 4)
        sums, sum_out, extra = fence(sums, sum_out, extra)
        sums = halve(sums, high, lambda value: value)
        sum_out = both(after(add(*sum_out).reshape(-1, width), sums[-1]), 8)
        sums[-1] = across(sums[-1], 8)
        sums, sum_out = fence(sums, sum_out)
        sums = both(add(*sums), 8)
        ys[0] = exchange(*after(ys[0], sum_out))
        sum_out = both(join(*sum_out, high, 0), 4)
        extra = both(after(add(*extra), sum_out[0]), 8)
        arrived_up.append(swap(after(away_up[middle_row:], sums[0])))
        sums, sum_out, ys[0], extra, arrived_up = fence(sums, sum_out, ys[0], extra, arrived_up)
        sums = both(join(*sums, high, 0), 4)
        sum_out = both(join(*sum_out, low, 0), 2)
        ys[0] = relay(ys[0])
        extra = add(*extra)
        extra = (extra, swap(extra))
        mixture = mix(3, mixture)
        sums, mixture, extra = fence(sums, mixture, extra)
        sums = both(join(*sums, low, 0), 2)
        arrived_down = swap(after(away_down, mixture))
        mixture = ahead(mixture)
        grad_gate = (keep_gate + arrived_gate.astype(f32))[None]
        grad_up = (keep_up + jnp.concatenate(arrived_up, axis=0).astype(f32))[None]
        sums, sum_out, grad_gate, grad_up, arrived_down, mixture = fence(
            sums, sum_out, grad_gate, grad_up, arrived_down, mixture
        )
        sums = both(join(*sums, other_chip, 0), 1)
        sum_out = both(join(*sum_out, other_chip, 0), 1)
        sum_out = join(*sum_out, core, 0).astype(f32)
        grad_down = (keep_down + arrived_down.astype(f32))[None]
        mixed = mix(0, mixture, middle)[None]
        extra = lax.dynamic_slice_in_dim(add(*extra), d * size, size, 1).astype(f32)
        sum_q, sum_key, sum_value = [
            join(sums[0][:, cols], sums[1][:, cols], core, 0).astype(f32)
            for cols in [
                slice(0, q_width),
                slice(q_width, q_width + kv_width),
                slice(q_width + kv_width, q_width + 2 * kv_width),
            ]
        ]
    else:
        dkv = lax.psum_scatter(dkv.astype(bf16), "dp", scatter_dimension=0, tiled=True).astype(f32)
        dqkv = unrotated(dkv)
        extra, grad_inputs = through_projections(dqkv)
        sum_qkv = sum_all(*weight_grad(half_index, hidden_one, dqkv))
        sum_q, sum_key = sum_qkv[:, :q_width], sum_qkv[:, q_width : q_width + kv_width]
        sum_value = sum_qkv[:, q_width + kv_width :]
        sum_out = sum_all(*grad_out)
        extra = lax.psum_scatter(extra, "dp", scatter_dimension=1, tiled=True)
        extra = lax.psum(extra, "expert").astype(f32)
        ys = {k: relay(exchange(*y)) for k, y in ys.items()}
        mixture = None
        for k in turns[:-1]:
            mixture = ahead(mix(k, mixture))
        mixed = mix(0, mixture, middle)[None]
    return (
        mixed,
        grad_inputs[None],
        extra[0],
        sum_q,
        sum_key,
        sum_value,
        sum_out,
        extra[1],
        extra[2 : 2 + experts].T,
        grad_gate,
        grad_up,
        grad_down,
    )


def solution(mesh):
    rows = P("expert", "dp", None)
    return jax.shard_map(
        functools.partial(on_device, mesh.shape["dp"], mesh.shape["expert"]),
        mesh=mesh,
        in_specs=(
            rows,
            rows,
            P("expert", "dp"),
            P("expert", "dp"),
            rows,
            rows,
            P("dp"),
            P("dp", None),
            P("dp", None),
            P("dp", None),
            P("dp", None),
            P("dp"),
            P("dp", None),
            rows,
            rows,
            P("expert", None, "dp"),
        ),
        out_specs=(
            rows,
            rows,
            P("dp"),
            P("dp", None),
            P("dp", None),
            P("dp", None),
            P("dp", None),
            P("dp"),
            P("dp", None),
            rows,
            rows,
            P("expert", None, "dp"),
        ),
        check_vma=False,
    )
```

```python
import functools
import math

import jax
import jax.numpy as jnp
from jax import lax
from jax.experimental import pallas as pl
from jax.experimental.pallas import tpu as pltpu
from jax.sharding import PartitionSpec as P

HEADS = 12
KV_HEADS = 2
HEAD_DIM = 128
TOP = 4
GROUP = HEADS // KV_HEADS
PLANE = 4
LANES = 128
PIECES = 3

EPSILON = 1e-06
ROPE_BASE = 1000000.0
MASKED = -1e30
MIB = 1024 * 1024

f32 = jnp.float32
bf16 = jnp.bfloat16


def dot(a, b):
    return jnp.dot(a, b, preferred_element_type=f32)


def dot_nt(a, b):
    return lax.dot_general(a, b, (((1,), (1,)), ((), ())), preferred_element_type=f32)


def dot_tn(a, b):
    return lax.dot_general(a, b, (((0,), (0,)), ((), ())), preferred_element_type=f32)


def whole(shape):
    return pl.BlockSpec(shape, lambda *_: (0,) * len(shape))


def call(kernel, grid, in_specs, out_specs, out_shape, scratch=(), prefetch=0, flops=0, moved=0, vmem=20, aliases=None):
    return pl.pallas_call(
        kernel,
        grid_spec=pltpu.PrefetchScalarGridSpec(
            num_scalar_prefetch=prefetch,
            grid=grid,
            in_specs=in_specs,
            out_specs=out_specs,
            scratch_shapes=list(scratch),
        ),
        out_shape=out_shape,
        input_output_aliases=aliases or {},
        cost_estimate=pl.CostEstimate(flops=flops // 64, bytes_accessed=moved // 64, transcendentals=0),
        compiler_params=pltpu.CompilerParams(
            dimension_semantics=("arbitrary",) * len(grid), vmem_limit_bytes=vmem * MIB
        ),
    )


def qkv_kernel(offsets, x_ref, gain_ref, cos_ref, sin_ref, *refs):
    pieces, (out_ref, h_ref) = refs[:-2], refs[-2:]
    step = pl.program_id(0)

    @pl.when(step == 0)
    def _():
        x = x_ref[...].astype(f32)
        r = lax.rsqrt(jnp.mean(x * x, axis=1, keepdims=True) + EPSILON)
        h_ref[...] = (x * r * gain_ref[...]).astype(bf16)

    acc = None
    for n, w_ref in enumerate(pieces):
        rows = w_ref.shape[0]
        start = pl.multiple_of(offsets[n], LANES)
        part = dot(h_ref[:, pl.ds(start, rows)], w_ref[...])
        acc = part if acc is None else acc + part

    rotary = step * out_ref.shape[1] < (HEADS + KV_HEADS) * HEAD_DIM

    @pl.when(rotary)
    def _():
        for n in range(out_ref.shape[1] // HEAD_DIM):
            a = acc[:, n * HEAD_DIM : (n + 1) * HEAD_DIM]
            turned = a * cos_ref[...] + pltpu.roll(a, HEAD_DIM // 2, 1) * sin_ref[...]
            out_ref[:, n * HEAD_DIM : (n + 1) * HEAD_DIM] = turned.astype(bf16)

    @pl.when(jnp.logical_not(rotary))
    def _():
        out_ref[...] = acc.astype(bf16)


def project_qkv(x, gain, cosine, sine, offsets, pieces):
    tokens, width = x.shape
    columns = pieces[0][0].shape[1]
    tile = 256
    return call(
        qkv_kernel,
        (columns // tile,),
        [whole(x.shape), whole(gain.shape), whole(cosine.shape), whole(sine.shape)]
        + [pl.BlockSpec((n, tile), lambda i, *_: (0, i)) for _, n in pieces],
        [pl.BlockSpec((tokens, tile), lambda i, *_: (0, i)), whole(x.shape)],
        [jax.ShapeDtypeStruct((tokens, columns), bf16), jax.ShapeDtypeStruct(x.shape, bf16)],
        prefetch=1,
        flops=2 * tokens * width * columns,
        moved=2 * width * columns + 4 * tokens * columns,
    )(offsets, x, gain, cosine, sine, *[p for p, _ in pieces])


def back_kernel(offsets, x_ref, *refs):
    pieces, (out_ref, acc_ref) = refs[:-2], refs[-2:]
    step = pl.program_id(0)
    for n, w_ref in enumerate(pieces):
        rows = w_ref.shape[0]
        span = pl.ds(pl.multiple_of(offsets[n], LANES), rows)
        part = dot_nt(x_ref[...], w_ref[...])
        acc_ref[:, span] = jnp.where(step == 0, part, acc_ref[:, span] + part)

    @pl.when(step == pl.num_programs(0) - 1)
    def _():
        out_ref[...] = acc_ref[...].astype(out_ref.dtype)


def project_back(x, offsets, pieces, dtype):
    tokens, columns = x.shape
    width = sum(n for _, n in pieces)
    tile = 512
    return call(
        back_kernel,
        (columns // tile,),
        [pl.BlockSpec((tokens, tile), lambda i, *_: (0, i))]
        + [pl.BlockSpec((n, tile), lambda i, *_: (0, i)) for _, n in pieces],
        whole((tokens, width)),
        jax.ShapeDtypeStruct((tokens, width), dtype),
        scratch=[pltpu.VMEM((tokens, width), f32)],
        prefetch=1,
        flops=2 * tokens * width * columns,
        moved=2 * width * columns + 6 * tokens * columns,
    )(offsets, x, *[p for p, _ in pieces])


def weight_grad_kernel(core, x_ref, y_ref, keep_ref, away_ref):
    rows = keep_ref.shape[1]
    for n, out_ref in enumerate((keep_ref, away_ref)):
        part = core[0] if n == 0 else 1 - core[0]
        start = pl.multiple_of(part * rows, LANES)
        out_ref[0] = dot_tn(x_ref[:, pl.ds(start, rows)], y_ref[...]).astype(bf16)


def weight_grad(core, x, y, block=0, blocks=1):
    tokens, width = x.shape
    columns = y.shape[1] // blocks
    half = width // 2
    shape = (2, half // 2, columns)
    return call(
        weight_grad_kernel,
        (2,),
        [
            pl.BlockSpec((tokens, half), lambda i, *_: (0, i)),
            pl.BlockSpec((tokens, columns), lambda i, *_: (0, block)),
        ],
        [pl.BlockSpec((1,) + shape[1:], lambda i, *_: (i, 0, 0))] * 2,
        [jax.ShapeDtypeStruct(shape, bf16)] * 2,
        prefetch=1,
        flops=2 * tokens * width * columns,
        moved=4 * width * columns,
    )(core, x, y)


def heads_together(keys):
    return 2 if keys <= 1024 else 1


def attend_kernel(q_ref, k_ref, v_ref, bias_ref, o_ref, p_ref):
    for n in range(p_ref.shape[0]):
        span = slice(n * HEAD_DIM, (n + 1) * HEAD_DIM)
        scores = dot_nt(q_ref[:, span], k_ref[...]) * (math.log2(math.e) / math.sqrt(HEAD_DIM)) + bias_ref[...]
        peak = jnp.max(scores, axis=1, keepdims=True)
        exps = jnp.exp2(scores - peak)
        probs = (exps * (1.0 / jnp.sum(exps, axis=1, keepdims=True))).astype(bf16)
        p_ref[n] = probs
        o_ref[:, span] = dot(probs, v_ref[...]).astype(bf16)


def attend(qkv, keys_values, bias):
    tokens = qkv.shape[0]
    keys = keys_values.shape[0]
    heads = heads_together(keys)
    wide = (tokens, heads * HEAD_DIM)
    return call(
        attend_kernel,
        (HEADS // heads,),
        [
            pl.BlockSpec(wide, lambda h: (0, h)),
            pl.BlockSpec((keys, HEAD_DIM), lambda h: (0, h * heads // GROUP)),
            pl.BlockSpec((keys, HEAD_DIM), lambda h: (0, KV_HEADS + h * heads // GROUP)),
            whole(bias.shape),
        ],
        [
            pl.BlockSpec(wide, lambda h: (0, h)),
            pl.BlockSpec((heads, tokens, keys), lambda h: (h, 0, 0)),
        ],
        [
            jax.ShapeDtypeStruct((tokens, HEADS * HEAD_DIM), bf16),
            jax.ShapeDtypeStruct((HEADS, tokens, keys), bf16),
        ],
        flops=4 * HEADS * tokens * keys * HEAD_DIM,
        moved=2 * HEADS * tokens * keys,
        vmem=24 * max(1, keys // 1536),
    )(qkv, keys_values, keys_values, bias)


def attend_back_kernel(p_ref, do_ref, q_ref, k_ref, v_ref, cos_ref, sin_ref, dq_ref, dk_ref, dv_ref):
    scale = 1.0 / math.sqrt(HEAD_DIM)
    heads = p_ref.shape[0]
    member = lax.rem(pl.program_id(0), GROUP // heads)
    dk, dv = None, None
    for n in range(heads):
        span = slice(n * HEAD_DIM, (n + 1) * HEAD_DIM)
        probs = p_ref[n]
        wide = probs.astype(f32)
        do = do_ref[:, span]
        grad_probs = dot_nt(do, v_ref[...])
        delta = jnp.sum(wide * grad_probs, axis=1, keepdims=True)
        grad_scores = (wide * (grad_probs - delta)).astype(bf16)
        dq = dot(grad_scores, k_ref[...]) * scale
        dq_ref[:, span] = (dq * cos_ref[...] - pltpu.roll(dq, HEAD_DIM // 2, 1) * sin_ref[...]).astype(bf16)
        dk_part, dv_part = dot_tn(grad_scores, q_ref[:, span]), dot_tn(probs, do)
        dk, dv = (dk_part, dv_part) if n == 0 else (dk + dk_part, dv + dv_part)
    dk = dk * scale

    @pl.when(member == 0)
    def _():
        dk_ref[...] = dk
        dv_ref[...] = dv

    @pl.when(member > 0)
    def _():
        dk_ref[...] += dk
        dv_ref[...] += dv


def attend_back(probs, do, qkv, keys_values, cosine, sine):
    tokens = qkv.shape[0]
    keys = keys_values.shape[0]
    kv_width = KV_HEADS * HEAD_DIM
    heads = heads_together(keys)
    wide = (tokens, heads * HEAD_DIM)
    return call(
        attend_back_kernel,
        (HEADS // heads,),
        [
            pl.BlockSpec((heads, tokens, keys), lambda h: (h, 0, 0)),
            pl.BlockSpec(wide, lambda h: (0, h)),
            pl.BlockSpec(wide, lambda h: (0, h)),
            pl.BlockSpec((keys, HEAD_DIM), lambda h: (0, h * heads // GROUP)),
            pl.BlockSpec((keys, HEAD_DIM), lambda h: (0, KV_HEADS + h * heads // GROUP)),
            whole(cosine.shape),
            whole(sine.shape),
        ],
        [
            pl.BlockSpec(wide, lambda h: (0, h)),
            pl.BlockSpec((keys, HEAD_DIM), lambda h: (0, h * heads // GROUP)),
            pl.BlockSpec((keys, HEAD_DIM), lambda h: (0, h * heads // GROUP)),
        ],
        [
            jax.ShapeDtypeStruct((tokens, HEADS * HEAD_DIM), bf16),
            jax.ShapeDtypeStruct((keys, kv_width), f32),
            jax.ShapeDtypeStruct((keys, kv_width), f32),
        ],
        flops=8 * HEADS * tokens * keys * HEAD_DIM,
        moved=2 * HEADS * tokens * keys,
        vmem=24 * max(1, keys // 1536),
    )(probs, do, qkv, keys_values, keys_values, cosine, sine)


def middle_kernel(experts, offsets, o_ref, x_ref, gain_ref, router_ref, routes_ref, *refs):
    pieces, (middle_ref, payload_ref, gates_ref) = refs[:-3], refs[-3:]
    step = pl.program_id(0)
    tile = x_ref.shape[1]
    acc = x_ref[...].astype(f32)
    for n, w_ref in enumerate(pieces):
        start = pl.multiple_of(offsets[n], LANES)
        acc = acc + dot(o_ref[:, pl.ds(start, w_ref.shape[0])], w_ref[...])
    middle_ref[:, pl.ds(pl.multiple_of(step * tile, tile), tile)] = acc

    @pl.when(step == pl.num_programs(0) - 1)
    def _():
        middle = middle_ref[...]
        width = middle.shape[1]
        r = lax.rsqrt(jnp.mean(middle * middle, axis=1, keepdims=True) + EPSILON)
        h = (middle * r * gain_ref[...]).astype(bf16)
        payload_ref[:, :width] = h
        logits = dot_nt(h, router_ref[...])
        lane = lax.broadcasted_iota(jnp.int32, logits.shape, 1)
        chosen = lane == routes_ref[:, 0:1]
        for k in range(1, TOP):
            chosen = chosen | (lane == routes_ref[:, k : k + 1])
        logits = jnp.where(chosen, logits, MASKED)
        exps = jnp.where(chosen, jnp.exp(logits - jnp.max(logits, axis=1, keepdims=True)), 0.0)
        gates = exps / jnp.sum(exps, axis=1, keepdims=True)
        gates_ref[...] = gates
        high = gates.astype(bf16).astype(f32)
        payload_ref[:, width:] = (high + pltpu.roll(gates - high, experts, 1)).astype(bf16)


def project_out(o, x, gain, router, routes, offsets, pieces, experts):
    tokens, width = x.shape
    tile = 256
    return call(
        functools.partial(middle_kernel, experts),
        (width // tile,),
        [
            whole(o.shape),
            pl.BlockSpec((tokens, tile), lambda i, *_: (0, i)),
            whole(gain.shape),
            whole(router.shape),
            whole(routes.shape),
        ]
        + [pl.BlockSpec((n, tile), lambda i, *_: (0, i)) for _, n in pieces],
        [whole((tokens, width)), whole((tokens, width + LANES)), whole((tokens, LANES))],
        [
            jax.ShapeDtypeStruct((tokens, width), f32),
            jax.ShapeDtypeStruct((tokens, width + LANES), bf16),
            jax.ShapeDtypeStruct((tokens, LANES), f32),
        ],
        prefetch=1,
        flops=2 * tokens * width * o.shape[1],
        moved=2 * width * o.shape[1] + 10 * tokens * width,
    )(offsets, o, x, gain, router, routes, *[p for p, _ in pieces])


def one_hot(slots_ref, j, rows):
    tokens = slots_ref.shape[1]
    slot = lax.broadcasted_iota(jnp.int32, (rows, tokens), 0)
    return jnp.where(slot == slots_ref[j : j + 1, :], 1.0, 0.0).astype(bf16)


def select_kernel(slots_ref, block_ref, *outs):
    rows = outs[0].shape[0]
    picks = jnp.concatenate([one_hot(slots_ref, j, rows) for j in range(PLANE)], axis=0)
    chosen = dot(picks, block_ref[...]).astype(bf16)
    outs = outs if len(outs) == PLANE else [outs[0], outs[1], outs[2].at[0], outs[2].at[1]]
    for j, out in enumerate(outs):
        out[...] = chosen[j * rows : (j + 1) * rows]


def piece_shapes(rows, width, stacked):
    return [(rows, width)] * 2 + [(2, rows, width)] if stacked else [(rows, width)] * PLANE


def select(slots, block, rows, stacked):
    tokens, width = block.shape
    shapes = piece_shapes(rows, width, stacked)
    return call(
        select_kernel,
        (1,),
        [whole(slots.shape), whole(block.shape)],
        [whole(shape) for shape in shapes],
        [jax.ShapeDtypeStruct(shape, bf16) for shape in shapes],
        flops=2 * PLANE * rows * tokens * width,
        moved=2 * (PLANE * rows + tokens) * width,
    )(slots, block)


def piece_specs(parts):
    rows, width = parts[0].shape
    flat = whole((rows, width))
    if parts[1].ndim == 2:
        return [flat] * PLANE
    first = pl.BlockSpec((1, rows, width), lambda *_: (0, 0, 0))
    second = pl.BlockSpec((1, rows, width), lambda *_: (1, 0, 0))
    return [flat, first, first, second]


def piece_rows(refs):
    return [ref[0] if len(ref.shape) == 3 else ref[...] for ref in refs]


def combine_kernel(slots_ref, *refs):
    parts, rest = refs[:PLANE], refs[PLANE:]
    out = rest[-1]
    rows = parts[0].shape[0]
    picks = jnp.concatenate([one_hot(slots_ref, j, rows) for j in range(PLANE)], axis=0)
    total = dot_tn(picks, jnp.concatenate(piece_rows(parts), axis=0))
    for before in rest[:-1]:
        total = total + before[...].astype(f32)
    out[...] = total.astype(out.dtype)


def combine(slots, parts, rows, extra, dtype):
    tokens = slots.shape[1]
    width = parts[0].shape[1]
    extra = [value for value in extra if value is not None]
    return call(
        combine_kernel,
        (1,),
        [whole(slots.shape)] + piece_specs(parts) + [whole((tokens, width))] * len(extra),
        whole((tokens, width)),
        jax.ShapeDtypeStruct((tokens, width), dtype),
        flops=2 * PLANE * rows * tokens * width,
        moved=2 * (PLANE * rows + 3 * tokens) * width,
    )(slots, *parts, *extra)


def expert_kernel(experts, part, counts, at, *refs):
    xs, cs = refs[:PLANE], refs[PLANE : 2 * PLANE]
    groups, used = [], 2 * PLANE
    for axis, count in zip((0, 0, 1), counts):
        group = refs[used : used + count]
        starts = [pl.multiple_of(at[1 + used - 2 * PLANE + n], LANES) for n in range(count)]
        groups.append([(pl.ds(start, w.shape[axis]), w) for start, w in zip(starts, group)])
        used += count
    wgs, wus, wds = groups
    x_ref, dy_ref, y_acc, d_acc, gate_ref, sems = refs[-6:]
    outs = refs[-6 - PLANE - PIECES - 5 : -6]
    drows, ys = outs[:PLANE], outs[PLANE : PLANE + PIECES]
    rows_out, dy_out, a_ref, dg_ref, du_ref = outs[PLANE + PIECES :]
    xs = [ref.at[0] if len(ref.shape) == 3 else ref for ref in xs]
    cs = [ref.at[0] if len(ref.shape) == 3 else ref for ref in cs]
    ys = [ys[0], ys[1], ys[2].at[0], ys[2].at[1]]
    step = pl.program_id(0)
    expert = at[0]
    rows = xs[0].shape[0]
    width = x_ref.shape[1]
    lane = lax.broadcasted_iota(jnp.int32, (rows, LANES), 1)
    keep = [
        pltpu.make_async_copy(src, dst.at[pl.ds(part * PLANE * rows, PLANE * rows)], sems.at[n])
        for n, (src, dst) in enumerate(((x_ref, rows_out), (dy_ref, dy_out)))
    ]

    @pl.when(step == 0)
    def _():
        for j in range(PLANE):
            span = slice(j * rows, (j + 1) * rows)
            x_ref[span, :] = xs[j][:, :width]
            tail = xs[j][:, width:].astype(f32)
            mine = (lane == expert) | (lane == expert + experts)
            gate = jnp.sum(jnp.where(mine, tail, 0.0), axis=1, keepdims=True)
            gate_ref[span, :] = jnp.broadcast_to(gate, (rows, LANES))
            dy_ref[span, :] = (gate * cs[j][...].astype(f32)).astype(bf16)
        for copy in keep:
            copy.start()

    def total(values):
        return functools.reduce(lambda a, b: a + b, values)

    g = total([dot(x_ref[:, span], w[...]) for span, w in wgs])
    u = total([dot(x_ref[:, span], w[...]) for span, w in wus])
    sigma = 1.0 / (1.0 + jnp.exp(-g))
    swish = g * sigma
    a = (swish * u).astype(bf16)
    da = total([dot_nt(dy_ref[:, span], w[...]) for span, w in wds])
    dg = (da * u * sigma * (1.0 + g * (1.0 - sigma))).astype(bf16)
    du = (da * swish).astype(bf16)
    a_ref[...] = a
    dg_ref[...] = dg
    du_ref[...] = du
    first = step == 0
    for span, w in wds:
        y = dot(a, w[...])
        y_acc[:, span] = jnp.where(first, y, y_acc[:, span] + y)
    for span, w in wgs:
        d = dot_nt(dg, w[...])
        d_acc[:, span] = jnp.where(first, d, d_acc[:, span] + d)
    for span, w in wus:
        d_acc[:, span] += dot_nt(du, w[...])

    @pl.when(step == pl.num_programs(0) - 1)
    def _():
        for j in range(PLANE):
            span = slice(j * rows, (j + 1) * rows)
            yj = y_acc[span, :].astype(bf16).astype(f32)
            ys[j][...] = (gate_ref[span, 0:1] * yj).astype(bf16)
            dgate = jnp.sum(cs[j][...].astype(f32) * yj, axis=1, keepdims=True)
            high = dgate.astype(bf16).astype(f32)
            tail = jnp.where(lane == expert, high, 0.0) + jnp.where(lane == expert + experts, dgate - high, 0.0)
            drows[j][:, :width] = d_acc[span, :].astype(bf16)
            drows[j][:, width:] = tail.astype(bf16)
        for copy in keep:
            copy.wait()


def run_expert(index, part, parts, rows, experts, xs, cs, gates, ups, downs, kept):
    width = cs[0].shape[1]
    weights = gates + ups + downs
    hidden = gates[0][0].shape[1]
    tile = 256
    total = PLANE * rows
    at = jnp.stack([index] + [jnp.asarray(w[3]) for w in weights]).astype(jnp.int32)
    kept = [] if kept is None else list(kept)
    big = [width, width, hidden, hidden, hidden]
    shapes = piece_shapes(rows, width + LANES, False) + piece_shapes(rows, width, True)

    return call(
        functools.partial(expert_kernel, experts, part, (len(gates), len(ups), len(downs))),
        (hidden // tile,),
        piece_specs(xs)
        + piece_specs(cs)
        + [pl.BlockSpec((w[1], tile), lambda i, *_, block=w[2]: (block, i)) for w in gates + ups]
        + [pl.BlockSpec((tile, w[1]), lambda i, *_, block=w[2]: (i, block)) for w in downs]
        + [pl.BlockSpec(memory_space=pl.ANY)] * len(kept),
        [whole(shape) for shape in shapes]
        + [pl.BlockSpec(memory_space=pl.ANY)] * 2
        + [pl.BlockSpec((total, tile), lambda i, *_: (part, i))] * 3,
        [jax.ShapeDtypeStruct(shape, bf16) for shape in shapes]
        + [jax.ShapeDtypeStruct((parts * total, n), bf16) for n in big],
        scratch=[
            pltpu.VMEM((total, width), bf16),
            pltpu.VMEM((total, width), bf16),
            pltpu.VMEM((total, width), f32),
            pltpu.VMEM((total, width), f32),
            pltpu.VMEM((total, LANES), f32),
            pltpu.SemaphoreType.DMA((2,)),
        ],
        prefetch=1,
        flops=12 * total * width * hidden,
        moved=6 * width * hidden + 16 * total * width,
        vmem=60,
        aliases={1 + 2 * PLANE + len(weights) + n: PLANE + PIECES + n for n in range(len(kept))},
    )(at, *xs, *cs, *[w[0] for w in weights], *kept)


def halves_kernel(order, x_ref, y_ref, own_ref, away_ref):
    part = dot_tn(x_ref[...], y_ref[...])

    @pl.when(pl.program_id(0) == 0)
    def _():
        own_ref[...] = part

    @pl.when(pl.program_id(0) == 1)
    def _():
        away_ref[...] = part.astype(bf16)


def grad_halves(order, x, y, cut_y):
    rows = x.shape[0]
    wide = (rows, (y if cut_y else x).shape[1] // 2)
    cut = pl.BlockSpec(wide, lambda i, order: (0, order[i]))
    shape = (x.shape[1], wide[1]) if cut_y else (wide[1], y.shape[1])
    return call(
        halves_kernel,
        (2,),
        [whole(x.shape), cut] if cut_y else [cut, whole(y.shape)],
        [whole(shape), whole(shape)],
        [jax.ShapeDtypeStruct(shape, f32), jax.ShapeDtypeStruct(shape, bf16)],
        prefetch=1,
        flops=2 * rows * x.shape[1] * y.shape[1],
        moved=2 * rows * (x.shape[1] + y.shape[1]) + 6 * shape[0] * shape[1],
        vmem=28,
    )(order, x, y)


def fence(*values):
    leaves, tree = jax.tree.flatten(values)
    arrays = [n for n, leaf in enumerate(leaves) if isinstance(leaf, jax.Array)]
    for n, leaf in zip(arrays, lax.optimization_barrier([leaves[n] for n in arrays])):
        leaves[n] = leaf
    return jax.tree.unflatten(tree, leaves)


def after(value, *others):
    return fence(value, *others)[0]


def rope_tables(position):
    half_width = HEAD_DIM // 2
    frequency = ROPE_BASE ** (-jnp.arange(half_width, dtype=f32) / half_width)
    angle = position.astype(f32)[:, None] * frequency[None, :]
    cosine, sine = jnp.cos(angle), jnp.sin(angle)
    return jnp.concatenate([cosine, cosine], axis=1), jnp.concatenate([-sine, sine], axis=1)


def on_device(
    copies,
    experts,
    tokens,
    cotangent,
    segment_ids,
    padding,
    routes,
    placement_order,
    norm_attn,
    w_query,
    w_key,
    w_value,
    w_out,
    norm_ffn,
    w_router,
    w_gate,
    w_up,
    w_down,
):
    planes = experts // PLANE
    paired = copies == 2
    d = lax.axis_index("dp")
    e = lax.axis_index("expert")
    z, q = e // PLANE, lax.rem(e, PLANE)
    core = lax.rem(e, 2)

    def swap(value):
        return lax.ppermute(value, "dp", [(0, 1), (1, 0)])

    def across(value, j):
        return lax.ppermute(value, "expert", [(i, i ^ j) for i in range(experts)])

    def ahead(value):
        return lax.ppermute(value, "expert", [(i, (i + PLANE) % experts) for i in range(experts)])

    def join(own, other, index, axis):
        first = jnp.where(index == 0, own, other)
        second = jnp.where(index == 0, other, own)
        return jnp.concatenate([first, second], axis=axis)

    def gather(own, axis):
        if paired:
            return join(own, swap(own), d, axis)
        return lax.all_gather(own, "dp", axis=axis, tiled=True)

    def half_rows(own):
        half = own.shape[0] // 2
        return lax.dynamic_slice_in_dim(own, core * half, half, 0)

    def assemble(pieces):
        if len(pieces) == 1:
            return pieces[0]
        own, got, twin = pieces
        return join(own, join(got, twin, core, 0), d, 0)

    def z_send(value, s):
        return lax.ppermute(value, "expert", [(i, (i + s * PLANE) % experts) for i in range(experts)])

    x = tokens[0]
    cot = cotangent[0]
    tok_count, width = x.shape
    position = d * tok_count + jnp.arange(tok_count, dtype=jnp.int32)
    kv_width = KV_HEADS * HEAD_DIM
    q_width = HEADS * HEAD_DIM

    capacity = tok_count * TOP * 9 // (8 * experts)
    rows = (capacity + 15) // 16 * 16
    far = tok_count * TOP
    wishes = jnp.concatenate([routes[0].T, placement_order[0].T], axis=0)
    if paired:
        size = w_query.shape[0]
        got_half = jnp.concatenate([half_rows(w_query), half_rows(w_key), half_rows(w_value)], axis=1)
        small_own = jnp.concatenate([norm_attn[None], norm_ffn[None], w_router.T], axis=0)
        own_info = jnp.where(padding[0] == 1, segment_ids[0], -1)[None]
        first_own = jnp.concatenate(
            [small_own, jnp.pad(own_info.astype(bf16), ((0, 0), (0, size - tok_count)))], axis=0
        )
        first_rows = first_own.shape[0]
        first_own = jnp.pad(first_own, ((0, -first_rows % 16), (0, got_half.shape[1] - size)))
        wishes, got_half = fence(wishes, jnp.concatenate([got_half, first_own], axis=0))
    ring_wishes = jnp.stack([wishes] + [z_send(wishes, k) for k in range(1, planes)])
    near = jnp.stack([z * PLANE + (q ^ j) for j in range(PLANE)]).astype(jnp.int32)
    hits = ring_wishes[:, None, :TOP] == near[None, :, None, None]
    order = jnp.min(jnp.where(hits, ring_wishes[:, None, TOP:], far), axis=2)
    rank = jnp.sum((order[:, :, None, :] < order[:, :, :, None]).astype(jnp.int32), axis=3)
    slots = jnp.where((order < far) & (rank < capacity), rank, -1)

    qkv_own = jnp.concatenate([w_query, w_key, w_value], axis=1)
    cosine, sine = rope_tables(position)
    if paired:
        start = (1 - d) * size
        offsets = jnp.stack([d * size, start + core * size // 2, start + (1 - core) * size // 2]).astype(jnp.int32)
        cut = size // 6 // LANES * LANES
        cut_offsets = [d * size]
        for begin in (0, cut):
            cut_offsets += [start + core * size // 2 + begin, start + (1 - core) * size // 2 + begin]
        cut_offsets = jnp.stack(cut_offsets).astype(jnp.int32)
        got = swap(got_half)
        cot_one = ahead(cot)
        out_half = half_rows(w_out)
        out_late, out_got = out_half[:cut], out_half[cut:]
        first_other = got[size // 2 : size // 2 + first_rows, :size]
        small = join(small_own, first_other[:-1], d, 1)
        info = jnp.concatenate([own_info, first_other[-1:, :tok_count].astype(jnp.int32)], axis=1)
        other_position = (1 - d) * tok_count + jnp.arange(tok_count, dtype=jnp.int32)
        key_place = jnp.concatenate([position, other_position])[None]
    else:
        small = gather(jnp.concatenate([norm_attn[None], norm_ffn[None], w_router.T], axis=0), 1)
        cot_one = ahead(cot)
        offsets = cut_offsets = jnp.zeros((1,), jnp.int32)
        out_late = out_got = ()
        got = lax.all_gather(qkv_own, "dp", axis=0, tiled=True)
        own_info = jnp.where(padding[0] == 1, segment_ids[0], -1)[None]
        info = lax.all_gather(own_info, "dp", axis=1, tiled=True)
        key_place = jnp.arange(copies * tok_count, dtype=jnp.int32)[None]
    gain_one = small[0:1].astype(f32)
    gain_two = small[1:2].astype(f32)
    router_rows = jnp.pad(small[2:], ((0, LANES - experts), (0, 0)))
    small = small[2:]
    segment, place = segment_ids[0][:, None], position[:, None]
    allowed = (key_place <= place) & (info == segment) | (key_place == place)
    bias = jnp.where(allowed, 0.0, MASKED)

    def exchange(own, near_by, chips):
        return own, near_by, across(chips, 2)

    def direct(parts):
        return [parts[0]] + [across(parts[j], j) for j in range(1, PLANE)]

    def relay(parts):
        own, near_by, landed = parts
        near_by = across(jnp.concatenate([near_by[None], landed[1:]], axis=0), 1)
        return [own, near_by, landed, near_by]

    def hand_out(k, block):
        return exchange(*select(slots[k], block, rows, True))

    cots = {0: hand_out(0, cot)}
    expert_own = [w_gate[0], w_up[0], w_down[0]]
    got, slots, qkv_own, out_late, out_got, cosine, sine, cots[0], cut_offsets = fence(
        got, slots, qkv_own, out_late, out_got, cosine, sine, cots[0], cut_offsets
    )
    cot_two = ahead(cot_one)
    if paired:
        qkv_pieces = [(qkv_own, size), (got, size // 2), (across(got, 1), size // 2)]
        out_got = swap(out_got)
    else:
        qkv_pieces = [(got, width)]
        out_got = lax.all_gather(w_out, "dp", axis=0, tiled=True)
    qkv, hidden_one = project_qkv(x, gain_one, cosine, sine, offsets, qkv_pieces)

    own_kv = qkv[:, q_width:]
    bias, gain_two, router_rows, small = after((bias, gain_two, router_rows, small), own_kv)
    cots[0] = relay(after(cots[0], own_kv))
    cots[1] = select(slots[1], after(cot_one, own_kv), rows, True)
    if paired:
        keys_values = jnp.concatenate([own_kv, swap(own_kv)], axis=0)
    else:
        keys_values = lax.all_gather(own_kv, "dp", axis=0, tiled=True)
    keys_values, out_got, cots[0], cots[1], bias, gain_two, router_rows, small, cot_two = fence(
        keys_values, out_got, cots[0], cots[1], bias, gain_two, router_rows, small, cot_two
    )
    ring_cot = [cot, cot_one, cot_two]
    for _ in range(3, planes):
        ring_cot.append(ahead(ring_cot[-1]))
    if paired:
        out_late = swap(after(out_late, keys_values))
        out_pieces = [(out_got, size // 2 - cut), (across(out_got, 1), size // 2 - cut)]
    else:
        out_pieces = [(out_got, q_width)]
    cots[1] = exchange(*cots[1])
    attended, probs = attend(qkv, keys_values, bias)
    if paired:
        out_late, _ = fence(out_late, attended)
        gate_up = swap(after(jnp.concatenate(expert_own[:2], axis=0), out_late))
        out_pieces = [(w_out, size), (out_late, cut), (across(out_late, 1), cut)] + out_pieces

    middle, payload, gates = project_out(
        attended, x, gain_two, router_rows, routes[0], cut_offsets, out_pieces, experts
    )
    if paired:
        payload, ring_cot = fence(payload, ring_cot)

    ring = [payload, ahead(payload)]
    xs, drows, ys, kept = {}, {}, {}, None
    turns = list(range(1, planes)) + [0]

    def work(k, kept):
        outs = run_expert(e, k, planes, rows, experts, xs[k], cots[k], *expert_weights, kept)
        drows[k] = outs[:PLANE]
        ys[k] = outs[PLANE : PLANE + PIECES]
        return outs[PLANE + PIECES :]

    def give_back(k, before, dtype):
        return combine(slots[k], drows[k], rows, [before], dtype)

    def mix(k, *before):
        return combine(slots[k], ys[k], rows, before, bf16)

    cots[1] = relay(after(cots[1], payload))
    for k in range(2, planes):
        cots[k] = hand_out(k, after(ring_cot[k], payload))
    if paired:
        ring[1], gate_up, cots = fence(ring[1], gate_up, cots)
        down = swap(after(expert_own[2], ring[1]))
        other = (1 - d) * size
        expert_weights = [
            [(expert_own[0], size, 0, d * size), (gate_up, size, 0, other)],
            [(expert_own[1], size, 0, d * size), (gate_up, size, 1, other)],
            [(expert_own[2], size, 0, d * size), (down, size, 0, other)],
        ]
        ring.append(ahead(ring[1]))
        xs[1] = direct(select(slots[1], ring[1], rows, False))
        ring[2], xs[1], cots, expert_weights = fence(ring[2], xs[1], cots, expert_weights)
        ring.append(ahead(ring[2]))
        xs[2] = select(slots[2], ring[2], rows, False)
        xs[1], xs[2] = fence(xs[1], xs[2])
        xs[2] = direct(xs[2])
        kept = work(1, kept)
        drows[1], kept, xs[2] = fence(drows[1], kept, xs[2])
        drows[1] = direct(drows[1])
        cots[2], cots[3] = [relay(after(cots[k], kept)) for k in (2, 3)]
        kept = work(2, kept)
        drows[1], drows[2], kept, ring[3] = fence(drows[1], drows[2], kept, ring[3])
        back = give_back(1, None, bf16)
        back, drows[2] = fence(back, drows[2])
        back = ahead(back)
        drows[2] = direct(drows[2])
        xs[3] = exchange(*select(slots[3], ring[3], rows, True))
        xs[0] = select(slots[0], after(payload, ring[3]), rows, True)
        xs[0], xs[3], drows[2], back, kept = fence(xs[0], xs[3], drows[2], back, kept)
        back = give_back(2, back, bf16)
        xs[3] = relay(xs[3])
        back, kept, xs[3] = fence(back, kept, xs[3])
        back = ahead(back)
        xs[0] = exchange(*xs[0])
        kept = work(3, kept)
        drows[3], xs[0], kept = fence(drows[3], xs[0], kept)
        drows[3] = direct(drows[3])
        xs[0] = relay(xs[0])
        kept = work(0, kept)
        drows[0], drows[3], kept, back = fence(drows[0], drows[3], kept, back)
        back = give_back(3, back, bf16)

        back, drows[0], kept, ys = fence(back, drows[0], kept, ys)
        back = ahead(back)
        drows[0] = direct(drows[0])
        ys[1] = exchange(*ys[1])
    else:
        expert_weights = [
            [(lax.all_gather(w, "dp", axis=axis, tiled=True), width, 0, 0)]
            for w, axis in zip(expert_own, (0, 0, 1))
        ]
        for k in range(2, planes):
            cots[k] = relay(cots[k])
            ring.append(ahead(ring[-1]))
        back = None
        for k in turns:
            xs[k] = direct(select(slots[k], ring[k], rows, False))
            kept = work(k, kept)
            drows[k] = direct(drows[k])
            if k > 0:
                back = ahead(give_back(k, back, bf16))

    row_all, dy_all, a_all, dg_all, du_all = kept
    if paired:
        halves = jnp.stack([d, 1 - d]).astype(jnp.int32)
        keep_gate, away_gate = grad_halves(halves, row_all, dg_all, False)
        keep_up, away_up = grad_halves(halves, row_all, du_all, False)
        keep_down, away_down = grad_halves(halves, a_all, dy_all, True)
        drows[0], ys, away_gate, away_up, away_down, back = fence(
            drows[0], ys, away_gate, away_up, away_down, back
        )
        arrived_gate = swap(away_gate)
        ys[2], ys[3] = exchange(*ys[2]), exchange(*ys[3])
        ys[1] = relay(ys[1])
        mixture = mix(1)
        back, mixture = fence(back, mixture)
        mixture = ahead(mixture)
        back = give_back(0, back, f32)
        middle_row = away_up.shape[0] // 2
        arrived_up = []
    else:
        grad_gate, grad_up, grad_down = [
            lax.psum_scatter(full.astype(bf16), "dp", scatter_dimension=axis, tiled=True).astype(f32)[None]
            for full, axis in (
                (dot_tn(row_all, dg_all), 0),
                (dot_tn(row_all, du_all), 0),
                (dot_tn(a_all, dy_all), 1),
            )
        ]
        back = give_back(0, back, f32)

    upstream = cot.astype(f32)
    gates = gates[:, :experts]
    dgates = back[:, width : width + experts] + back[:, width + experts : width + 2 * experts]
    dlogits = (gates * (dgates - jnp.sum(gates * dgates, axis=1, keepdims=True))).astype(bf16)
    hidden_two = payload[:, :width]
    dh2 = back[:, :width] + dot(dlogits, small)
    scale_two = lax.rsqrt(jnp.mean(middle * middle, axis=1, keepdims=True) + EPSILON)
    normed_two = middle * scale_two
    e2 = dh2 * gain_two
    dmiddle = upstream + scale_two * (e2 - normed_two * jnp.mean(e2 * normed_two, axis=1, keepdims=True))
    dmb = dmiddle.astype(bf16)
    half_index = jnp.stack([core if paired else 0]).astype(jnp.int32)
    do = project_back(dmb, cut_offsets, out_pieces, bf16)
    grad_out = weight_grad(half_index, attended, dmb)

    other_chip = lax.rem(q // 2, 2)

    def add(*values):
        return functools.reduce(lambda a, b: a + b, [v.astype(f32) for v in values]).astype(bf16)

    def pick(value, index, axis=0):
        return lax.dynamic_index_in_dim(value, index, axis, keepdims=False)

    def halve(parts, index, send, axis=0):
        parts = [p.reshape(p.shape[:axis] + (2, -1, p.shape[-1])) for p in parts]
        away = add(*[pick(p, 1 - index, axis) for p in parts])
        return [pick(p, index, axis) for p in parts] + [send(away)]

    def over(j):
        return lambda value: across(value, j)

    def cut_core(parts):
        return [parts[0], across(parts[1], 1)]

    def both(part, j):
        return part, across(part, j)

    def sum_all(keep, away):
        both = jnp.concatenate([keep, away], axis=1).reshape(-1, keep.shape[2])
        part = lax.psum_scatter(both, "dp", scatter_dimension=0, tiled=True)
        return lax.psum(part, "expert").astype(f32)

    def unrotate(value):
        turned = jnp.concatenate([value[:, HEAD_DIM // 2 :], value[:, : HEAD_DIM // 2]], axis=1)
        return value * cosine - turned * sine

    dqp, dk, dv = attend_back(probs, do, qkv, keys_values, cosine, sine)
    dkv = jnp.concatenate([dk, dv], axis=1)
    input_tokens = x.astype(f32)
    scale_one = lax.rsqrt(jnp.mean(input_tokens * input_tokens, axis=1, keepdims=True) + EPSILON)
    normed_one = input_tokens * scale_one
    grad_norm_ffn_local = jnp.sum(dh2 * normed_two, axis=0)
    grad_router_local = lax.dot_general(dlogits, hidden_two, (((0,), (0,)), ((), ())), preferred_element_type=f32)

    def unrotated(dkv):
        dkp = [unrotate(dkv[:, n * HEAD_DIM : (n + 1) * HEAD_DIM]) for n in range(KV_HEADS)]
        dkvp = jnp.concatenate([v.astype(bf16) for v in dkp] + [dkv[:, kv_width:].astype(bf16)], axis=1)
        return jnp.concatenate([dqp, dkvp], axis=1)

    def through_projections(dqkv):
        dh1 = project_back(dqkv, offsets, qkv_pieces, f32)
        grad_norm_attn_local = jnp.sum(dh1 * normed_one, axis=0)
        extra = jnp.concatenate(
            [grad_norm_attn_local[None], grad_norm_ffn_local[None], grad_router_local], axis=0
        )
        extra = extra.astype(bf16)
        e1 = dh1 * gain_one
        grad_inputs = dmiddle + scale_one * (
            e1 - normed_one * jnp.mean(e1 * normed_one, axis=1, keepdims=True)
        )
        return extra, grad_inputs

    if paired:
        low, high = lax.rem(z, 2), z // 2
        away_dkv = dkv[tok_count:].astype(bf16)
        away_dkv, dqp, ys, arrived_gate, mixture = fence(away_dkv, dqp, ys, arrived_gate, mixture)
        other_dkv = swap(away_dkv)
        ys[2] = relay(ys[2])
        sum_a = weight_grad(half_index, hidden_one, dqp)
        grad_out = weight_grad(half_index, after(attended, sum_a), dmb)
        sum_a, other_dkv, grad_out = fence(sum_a, other_dkv, grad_out)
        sum_a, sum_out = cut_core(sum_a), cut_core(grad_out)
        ys[3] = relay(ys[3])
        dqkv = unrotated(dkv[:tok_count] + other_dkv.astype(f32))
        sum_b = weight_grad(half_index, hidden_one, dqkv[:, q_width:])
        mixture = mix(2, mixture)
        sum_a, sum_out, sum_b, dqkv, ys, mixture = fence(sum_a, sum_out, sum_b, dqkv, ys, mixture)
        sum_a = halve(sum_a, d, swap)
        sum_out = halve(sum_out, other_chip, over(2), 1)
        sum_b = cut_core(sum_b)
        mixture = ahead(mixture)
        extra, grad_inputs = through_projections(after(dqkv, sum_b))
        sum_a, sum_out, sum_b, mixture, extra = fence(sum_a, sum_out, sum_b, mixture, extra)
        sum_a = halve(sum_a, other_chip, over(2))
        sum_b = halve(sum_b, d, swap)
        sum_out = halve(sum_out, low, over(4), 1)
        extra = both(extra, 1)
        sum_a, sum_out, sum_b, extra = fence(sum_a, sum_out, sum_b, extra)
        sum_b = halve(sum_b, other_chip, over(2))
        sum_out = halve(sum_out, high, over(8), 1)
        extra = both(add(*extra), 2)
        arrived_up.append(swap(after(away_up[:middle_row], sum_a)))
        sum_a, sum_out, sum_b, arrived_up, extra = fence(sum_a, sum_out, sum_b, arrived_up, extra)
        sums = halve([jnp.concatenate([add(*sum_a), add(*sum_b)], axis=1)], low, over(4))
        sum_out = halve(sum_out, d, swap)
        extra = both(add(*extra), 4)
        sums, sum_out, extra = fence(sums, sum_out, extra)
        sums = halve(sums, high, lambda value: value)
        sum_out = both(after(add(*sum_out).reshape(-1, width), sums[-1]), 8)
        sums[-1] = across(sums[-1], 8)
        sums, sum_out = fence(sums, sum_out)
        sums = both(add(*sums), 8)
        ys[0] = exchange(*after(ys[0], sum_out))
        sum_out = both(join(*sum_out, high, 0), 4)
        extra = both(after(add(*extra), sum_out[0]), 8)
        arrived_up.append(swap(after(away_up[middle_row:], sums[0])))
        sums, sum_out, ys[0], extra, arrived_up = fence(sums, sum_out, ys[0], extra, arrived_up)
        sums = both(join(*sums, high, 0), 4)
        sum_out = both(join(*sum_out, low, 0), 2)
        ys[0] = relay(ys[0])
        extra = add(*extra)
        extra = (extra, swap(extra))
        mixture = mix(3, mixture)
        sums, mixture, extra = fence(sums, mixture, extra)
        sums = both(join(*sums, low, 0), 2)
        arrived_down = swap(after(away_down, mixture))
        mixture = ahead(mixture)
        grad_gate = (keep_gate + arrived_gate.astype(f32))[None]
        grad_up = (keep_up + jnp.concatenate(arrived_up, axis=0).astype(f32))[None]
        sums, sum_out, grad_gate, grad_up, arrived_down, mixture = fence(
            sums, sum_out, grad_gate, grad_up, arrived_down, mixture
        )
        sums = both(join(*sums, other_chip, 0), 1)
        sum_out = both(join(*sum_out, other_chip, 0), 1)
        sum_out = join(*sum_out, core, 0).astype(f32)
        grad_down = (keep_down + arrived_down.astype(f32))[None]
        mixed = mix(0, mixture, middle)[None]
        extra = lax.dynamic_slice_in_dim(add(*extra), d * size, size, 1).astype(f32)
        sum_q, sum_key, sum_value = [
            join(sums[0][:, cols], sums[1][:, cols], core, 0).astype(f32)
            for cols in [
                slice(0, q_width),
                slice(q_width, q_width + kv_width),
                slice(q_width + kv_width, q_width + 2 * kv_width),
            ]
        ]
    else:
        dkv = lax.psum_scatter(dkv.astype(bf16), "dp", scatter_dimension=0, tiled=True).astype(f32)
        dqkv = unrotated(dkv)
        extra, grad_inputs = through_projections(dqkv)
        sum_qkv = sum_all(*weight_grad(half_index, hidden_one, dqkv))
        sum_q, sum_key = sum_qkv[:, :q_width], sum_qkv[:, q_width : q_width + kv_width]
        sum_value = sum_qkv[:, q_width + kv_width :]
        sum_out = sum_all(*grad_out)
        extra = lax.psum_scatter(extra, "dp", scatter_dimension=1, tiled=True)
        extra = lax.psum(extra, "expert").astype(f32)
        ys = {k: relay(exchange(*y)) for k, y in ys.items()}
        mixture = None
        for k in turns[:-1]:
            mixture = ahead(mix(k, mixture))
        mixed = mix(0, mixture, middle)[None]
    return (
        mixed,
        grad_inputs[None],
        extra[0],
        sum_q,
        sum_key,
        sum_value,
        sum_out,
        extra[1],
        extra[2 : 2 + experts].T,
        grad_gate,
        grad_up,
        grad_down,
    )


def solution(mesh):
    rows = P("expert", "dp", None)
    return jax.shard_map(
        functools.partial(on_device, mesh.shape["dp"], mesh.shape["expert"]),
        mesh=mesh,
        in_specs=(
            rows,
            rows,
            P("expert", "dp"),
            P("expert", "dp"),
            rows,
            rows,
            P("dp"),
            P("dp", None),
            P("dp", None),
            P("dp", None),
            P("dp", None),
            P("dp"),
            P("dp", None),
            rows,
            rows,
            P("expert", None, "dp"),
        ),
        out_specs=(
            rows,
            rows,
            P("dp"),
            P("dp", None),
            P("dp", None),
            P("dp", None),
            P("dp", None),
            P("dp"),
            P("dp", None),
            rows,
            rows,
            P("expert", None, "dp"),
        ),
        check_vma=False,
    )
```
